32 devices in a mesh: dp: 4 (over z), ep: 8 (over y, x, core).
Axes of the slice: x: 2, y: 2, z: 4, core: 2. Of those that a mesh axis runs over, the one named last changes fastest.
Arguments:
- tokens: bfloat16 [8192, 1024], P(('dp', 'ep')), may hold values from -6 to 6
- gain_attn: float32 [1024], replicated, may hold values from 0.5 to 1.5
- shift_attn: float32 [1024], replicated, may hold values from -1.5 to 1.5
- w_qkv: bfloat16 [1024, 3072], replicated, may hold values from -0.1875 to 0.1875
- w_o: bfloat16 [1024, 1024], replicated, may hold values from -3 to 3
- gain_ffn: float32 [1024], replicated, may hold values from 0.5 to 1.5
- shift_ffn: float32 [1024], replicated, may hold values from -1.5 to 1.5
- w_in: bfloat16 [8, 4096, 1024], P('ep'), may hold values from -0.1875 to 0.1875
- w_out: bfloat16 [8, 4096, 1024], P('ep'), may hold values from -0.1875 to 0.1875
- seq_lengths: int32 [4, 4], P('dp'), may hold values from 1 to 1920, as said below
- expert_ids: int32 [8192, 1], P(('dp', 'ep')), may hold values from 0 to 7; in each aligned block of 256 rows (0 to 255, 256 to 511, ...) at most 64 rows name the same one
- cotangent: bfloat16 [8192, 1024], P(('dp', 'ep')), may hold values from -6 to 6
Outputs:
- block_out: bfloat16 [8192, 1024], P(('dp', 'ep'))
- grad_tokens: float32 [8192, 1024], P(('dp', 'ep'))
- grad_w_qkv: float32 [1024, 3072], replicated
- grad_w_o: float32 [1024, 1024], replicated
- grad_gain_attn: float32 [1024], replicated
- grad_shift_attn: float32 [1024], replicated
- grad_gain_ffn: float32 [1024], replicated
- grad_shift_ffn: float32 [1024], replicated
- grad_w_in: float32 [8, 4096, 1024], P('ep', 'dp')
- grad_w_out: float32 [8, 4096, 1024], P('ep', 'dp')
The draws below stay inside these ranges and needn't reach their ends.
Inputs may be any that keep to these rules, and one draw needn't show every extreme that they name: `seq_lengths`: each group holds 4 sequences that fill its 2048 tokens; the second is 1920 tokens long and the others are shorter, each 1 or more. `expert_ids`: of the 256 rows of one device at most 64 name the same expert; in some such blocks one expert is named by exactly 64.
All inputs are finite; a program needn't handle non-finite values.
Results may differ from the reference program's by a relative error of at most 0.03.
Values may be sent and summed in bfloat16 or wider, within the bound.
A program may use at most 320 MiB of HBM per device.

```python
import math
import jax
import jax.numpy as jnp
import numpy as np
from jax import lax

D = 1024
HEADS = 16
HEAD_DIM = 64
FF = 4096
TOK_DEV = 256
EXPERTS = 8
CAP = 64
GROUP = 2048
LONGEST = 1920
NGROUPS = 4
TOKENS = 8192


def draw_seq_lengths(key, part):
    key = jax.random.fold_in(key, 11)
    first_key, second_key = jax.random.split(key)
    half_dev = TOK_DEV // 2
    leading = jax.random.randint(first_key, (NGROUPS,), 1, half_dev - 1)
    remaining = half_dev - leading
    middle = jax.random.randint(second_key, (NGROUPS,), 1, remaining)
    trailing = remaining - middle
    longest = jnp.full((NGROUPS,), LONGEST, jnp.int32)
    return jnp.stack([leading, longest, middle, trailing], axis=1).astype(jnp.int32)


def level_of(key, extent, cuts, smallest, top_value):
    gain = 1.0
    for axis_at, parts in cuts:
        steps = jax.random.uniform(jax.random.fold_in(jax.random.fold_in(key, 6), axis_at), (parts,), jnp.float32, smallest / len(cuts), top_value / len(cuts))
        gain = gain * jnp.repeat(jnp.exp(steps), extent[axis_at] // parts).reshape((-1,) + (1,) * (len(extent) - 1 - axis_at))
    return gain


def deal_out(rng, own, number, rows, count, top, reach, slope):
    ranking = jax.random.permutation(rng, count)
    crowded, ordinary = portions_of(count, rows * top, reach, slope, True), portions_of(count, rows * top, reach, slope, False)
    places = jnp.arange(count)

    def named(sizes, rotation):
        used = int((sizes > 0).sum())
        fixed = max(1, used // 4)
        moved = fixed + (places - fixed + rotation * (used - fixed)) % max(1, count - fixed)
        return jnp.zeros((count,), jnp.int32).at[ranking[jnp.where(places < fixed, places, moved)]].set(jnp.asarray(sizes, jnp.int32))

    sizes = jnp.where(number % 4 == 0, named(crowded, number // 4), named(ordinary, number - number // 4 - 1))
    mixed = jax.random.permutation(jax.random.fold_in(own, 3), count)
    source_of, sink = mixed[0:count // 2 * 2:2], mixed[1:count // 2 * 2:2]
    slack = jnp.minimum(sizes[source_of] - 1, reach - sizes[sink]) // 2
    slack = jnp.where((source_of == ranking[0]) | (sink == ranking[0]) | (sizes[sink] == 0), 0, jnp.maximum(slack, 0))
    moved = jax.random.randint(jax.random.fold_in(own, 4), (count // 2,), 0, 1 << 20) % (slack + 1)
    sizes = sizes.at[source_of].add(-moved).at[sink].add(moved)
    items = jnp.searchsorted(jnp.cumsum(sizes), jnp.arange(rows * top), side="right").astype(jnp.int32)
    grid = items.reshape(top, rows).T
    grid = grid[jax.random.permutation(jax.random.fold_in(own, 1), rows)]
    rotation = jax.random.randint(jax.random.fold_in(own, 2), (rows, 1), 0, top)
    return jnp.take_along_axis(grid, (jnp.arange(top)[None, :] + rotation) % top, axis=1)


def portions_of(count, total, reach, lean, full):
    portions = [(1 << 20) // math.isqrt(standing ** lean) + 1 for standing in range(1, count + 1)]
    largest = reach if full else min(reach, max(-(-total // count), total * portions[0] // sum(portions)))
    least = 1 if total - largest >= count - 1 else 0
    given, rest = [largest] + [least] * (count - 1), total - largest - least * (count - 1)
    while rest > 0:
        free = [i for i in range(1, count) if given[i] < largest] or [i for i in range(1, count) if given[i] < reach]
        whole, left = sum([portions[i] for i in free]), rest
        for i in free:
            more = min(reach - given[i], max(1, left * portions[i] // whole), rest)
            given[i] = given[i] + more
            rest = rest - more
    return np.array(given)


def normal_values(rng, shape, scale, reach, cuts=(), kind=jnp.bfloat16):
    level = level_of(rng, shape, cuts, -0.22, 0.18) if cuts else 1.0
    values = jax.random.normal(rng, shape, jnp.float32) * scale * level
    return jnp.minimum(jnp.maximum(values, -reach), reach).astype(kind)


def setup_inputs(seed: int = 0) -> dict:
    key_of = jax.random.split(jax.random.key(seed), 13)
    tokens = normal_values(key_of[0], (TOKENS, D), 1.0, 6.0, ((0, 32),))
    gain_attn = jnp.clip(1.0 + 0.1 * jax.random.normal(key_of[1], (D,), jnp.float32), 0.5, 1.5)
    shift_attn = normal_values(key_of[2], (D,), 0.3, 1.5, (), jnp.float32)
    w_qkv = normal_values(key_of[3], (D, 3 * D), D ** -0.5, 0.1875)
    w_o = normal_values(key_of[4], (D, D), (max(D // 256, 1)) ** -0.5, 3.0)
    gain_ffn = jnp.clip(1.0 + 0.1 * jax.random.normal(key_of[5], (D,), jnp.float32), 0.5, 1.5)
    shift_ffn = normal_values(key_of[6], (D,), 0.3, 1.5, (), jnp.float32)
    w_in = normal_values(key_of[7], (EXPERTS, FF, D), D ** -0.5, 0.1875, ((0, 8),))
    w_out = normal_values(key_of[8], (EXPERTS, FF, D), (FF // 4) ** -0.5, 0.1875, ((0, 8),))
    seq_lengths = draw_seq_lengths(jax.random.fold_in(key_of[12], 71), 0)
    expert_ids_keys = jax.random.split(jax.random.fold_in(key_of[10], 1), TOKENS // TOK_DEV)
    expert_ids_turns = jax.random.permutation(jax.random.fold_in(key_of[10], 3), TOKENS // TOK_DEV)
    expert_ids = jax.vmap(lambda own, number: deal_out(jax.random.fold_in(key_of[10], 2), own, number, TOK_DEV, EXPERTS, 1, CAP, 2))(expert_ids_keys, expert_ids_turns).reshape((TOKENS, 1))
    cotangent = normal_values(key_of[11], (TOKENS, D), 1.0, 6.0, ((0, 32),))
    return dict(tokens=tokens, gain_attn=gain_attn, shift_attn=shift_attn, w_qkv=w_qkv, w_o=w_o, gain_ffn=gain_ffn, shift_ffn=shift_ffn, w_in=w_in, w_out=w_out, seq_lengths=seq_lengths, expert_ids=expert_ids, cotangent=cotangent)


HIGH = lax.Precision.HIGHEST

@jax.custom_vjp
def low(v):
    return lax.optimization_barrier(v.astype(jnp.bfloat16)).astype(jnp.float32)

@jax.custom_vjp
def low_back(v):
    return v

def low_keep(v):
    return (low(v), None)

def low_pass(kept, grad):
    return (grad,)

def back_keep(v):
    return (v, None)

def back_low(kept, grad):
    return (low(grad),)
low.defvjp(low_keep, low_pass)
low_back.defvjp(back_keep, back_low)

def layer_norm(rows_in, gain_vec, shift_vec):
    average = lax.optimization_barrier(jnp.mean(rows_in, axis=-1, keepdims=True))
    centered = rows_in - average
    variance = lax.optimization_barrier(jnp.mean(centered * centered, axis=-1, keepdims=True))
    return centered * lax.rsqrt(variance + 1e-05) * gain_vec + shift_vec

def sequence_starts(lengths, positions):
    ends_at = jnp.cumsum(lengths)
    starts_at = ends_at - lengths
    return lax.optimization_barrier(jnp.max(jnp.where(starts_at[None, :] <= positions[:, None], starts_at[None, :], 0), axis=1))

def attend_group(query_rows, key_rows, value_rows, lengths):
    positions = jnp.arange(GROUP, dtype=jnp.int32)
    starts_of = sequence_starts(lengths, positions).astype(jnp.int32)
    block_rows = min(512, GROUP)
    key_heads = key_rows.reshape(GROUP, HEADS, HEAD_DIM)
    value_heads = value_rows.reshape(GROUP, HEADS, HEAD_DIM)

    def one_block(block_index):
        first_row = (block_index * block_rows).astype(jnp.int32)
        query_block = lax.dynamic_slice_in_dim(query_rows, first_row, block_rows, 0).reshape(block_rows, HEADS, HEAD_DIM)
        query_pos = first_row + jnp.arange(block_rows, dtype=jnp.int32)
        query_start = lax.dynamic_slice_in_dim(starts_of, first_row, block_rows, 0)
        scores = jnp.einsum('qhd,khd->hqk', query_block, key_heads, precision=HIGH) * HEAD_DIM ** (-0.5)
        scores = low_back(scores)
        allowed = ((positions[None, :] <= query_pos[:, None]) & (positions[None, :] >= query_start[:, None]))[None]
        scores = jnp.where(allowed, scores, -1e+30)
        weights = jnp.where(allowed, jnp.exp(scores - lax.optimization_barrier(jnp.max(scores, axis=-1, keepdims=True))), 0.0)
        softmax_w = low(weights / lax.optimization_barrier(jnp.sum(weights, axis=-1, keepdims=True)))
        return jnp.einsum('hqk,khd->qhd', softmax_w, value_heads, precision=HIGH).reshape(block_rows, D)
    blocks = lax.map(jax.checkpoint(one_block), jnp.arange(GROUP // block_rows, dtype=jnp.int32))
    return blocks.reshape(GROUP, D)

def forward(inputs, gain_attn, shift_attn, w_qkv, w_o, gain_ffn, shift_ffn, w_in, w_out, seq_lengths, expert_of):
    normed = low(layer_norm(inputs, gain_attn, shift_attn))
    qkv = jnp.dot(normed, w_qkv, precision=HIGH)
    queries = low_back(low(qkv[:, :D]))
    key_rows = low_back(low(qkv[:, D:2 * D]))
    value_rows = low_back(low(qkv[:, 2 * D:]))

    def group_step(running, pieces):
        query_part, key_part, value_part, lengths = pieces
        return (running, attend_group(query_part, key_part, value_part, lengths))
    _, attended = lax.scan(group_step, jnp.zeros((), jnp.float32), (queries.reshape(NGROUPS, GROUP, D), key_rows.reshape(NGROUPS, GROUP, D), value_rows.reshape(NGROUPS, GROUP, D), seq_lengths))
    attended = low_back(low(attended.reshape(TOKENS, D)))
    hidden_res = inputs + low_back(jnp.dot(attended, w_o, precision=HIGH))
    routed = low_back(low(layer_norm(hidden_res, gain_ffn, shift_ffn)))

    def expert_step(running_total, pieces):
        weight_in, weight_out, expert_index = pieces
        pre_act = low_back(jnp.dot(routed, weight_in.T, precision=HIGH))
        activated = low(jax.nn.gelu(pre_act, approximate=True))
        chosen = (expert_of == expert_index).astype(running_total.dtype)[:, None]
        return (running_total + chosen * jnp.dot(activated, weight_out, precision=HIGH), None)
    expert_sum, _ = lax.scan(jax.checkpoint(expert_step), jnp.zeros_like(hidden_res), (w_in, w_out, jnp.arange(EXPERTS, dtype=jnp.int32)))
    return hidden_res + low_back(low(expert_sum))

def reference(tokens, gain_attn, shift_attn, w_qkv, w_o, gain_ffn, shift_ffn, w_in, w_out, seq_lengths, expert_ids, cotangent):
    floats = (tokens.astype(jnp.float32), gain_attn.astype(jnp.float32), shift_attn.astype(jnp.float32), w_qkv.astype(jnp.float32), w_o.astype(jnp.float32), gain_ffn.astype(jnp.float32), shift_ffn.astype(jnp.float32), w_in.astype(jnp.float32), w_out.astype(jnp.float32))
    expert_of = expert_ids[:, 0]

    def wrapped(*params):
        return forward(*params, seq_lengths, expert_of)
    output, pullback = jax.vjp(wrapped, *floats)
    grads = pullback(cotangent.astype(jnp.float32))
    return (output.astype(jnp.bfloat16), grads[0], grads[3], grads[4], grads[1], grads[2], grads[5], grads[6], grads[7], grads[8])
```

```python
import functools
import jax
import jax.numpy as jnp
from jax import lax
from jax.experimental import pallas as pl
from jax.experimental.pallas import tpu as pltpu
from jax.sharding import PartitionSpec as P

HEADS = 16
EPSILON = 1e-05
HEAD=64
BQ=256
MASKED=-1e30
F32=jnp.float32; BF=jnp.bfloat16
NT=(((1,),(1,)),((),()))
NN=(((1,),(0,)),((),()))
def dot(a,b,dims): return lax.dot_general(a,b,dims,preferred_element_type=F32)

def start_row(len_ref, first, width):
    pos = first + lax.broadcasted_iota(jnp.int32,(1,width),1)
    start = jnp.zeros((1,width),jnp.int32)
    edge = jnp.int32(0)
    for s in range(len_ref.shape[1]-1):
        edge = edge + len_ref[0,s]
        start = jnp.where(pos>=edge, edge, start)
    return pos, start

def split_heads(block, heads):
    if heads==1: return [block]
    lane = lax.broadcasted_iota(jnp.int32, block.shape, 1)
    return [jnp.where((lane>=h*HEAD)&(lane<(h+1)*HEAD), block, jnp.zeros_like(block)) for h in range(heads)]

def fwd_kernel(len_ref, q_ref, k_ref, v_ref, o_ref, lse_ref, vt_ref):
    rows, width = q_ref.shape
    heads = width//HEAD
    bk = BQ
    for b in range(rows//BQ):
        vt_ref[:, b*BQ:(b+1)*BQ] = v_ref[b*BQ:(b+1)*BQ,:].astype(F32).T.astype(BF)
    def qstep(i,_):
        base = pl.multiple_of(i*BQ,BQ)
        qb = q_ref[pl.ds(base,BQ),:]*BF(HEAD**-0.5)
        qh = split_heads(qb, heads)
        pos,start = start_row(len_ref, base, BQ)
        def kstep(j, carry, diag):
            kb = pl.multiple_of(j*bk,bk)
            kk = k_ref[pl.ds(kb,bk),:]
            key = kb + lax.broadcasted_iota(jnp.int32,(bk,BQ),0)
            ok = key>=start
            if diag: ok = ok & (key<=pos)
            out=[]
            for h in range(heads):
                m,l,acc = carry[h]
                s = jnp.where(ok, dot(kk,qh[h],NT), MASKED)
                nm = jnp.maximum(m, jnp.max(s,axis=0,keepdims=True))
                p = jnp.exp(s-nm)
                if diag: p = jnp.where(ok,p,0.0)
                al = jnp.exp(m-nm)
                l = l*al + jnp.sum(p,axis=0,keepdims=True)
                acc = acc*al + dot(vt_ref[h*HEAD:(h+1)*HEAD, pl.ds(kb,bk)], p.astype(BF), NN)
                out.append((nm,l,acc))
            return tuple(out)
        init = tuple((jnp.full((1,BQ),MASKED,F32),jnp.zeros((1,BQ),F32),jnp.zeros((HEAD,BQ),F32)) for _ in range(heads))
        c = kstep(i, init, True)
        c = lax.fori_loop(0,i,lambda j,c: kstep(j,c,False), c)
        o = jnp.concatenate([acc/l for m,l,acc in c],axis=0)
        o_ref[pl.ds(base,BQ),:] = o.T.astype(BF)
        lse_ref[:, pl.ds(base,BQ)] = jnp.concatenate([m+jnp.log(l) for m,l,acc in c]+[jnp.zeros((8-heads,BQ),F32)],axis=0)
        return 0
    lax.fori_loop(0, rows//BQ, qstep, 0)

def bwd_kernel(len_ref, q_ref, k_ref, v_ref, o_ref, g_ref, lse_ref, dq_ref, dk_ref, dv_ref, kt_ref, dka, dva):
    rows, width = q_ref.shape
    heads = width//HEAD
    bk = BQ
    dka[...] = jnp.zeros_like(dka); dva[...]=jnp.zeros_like(dva)
    for b in range(rows//BQ):
        kt_ref[:, b*BQ:(b+1)*BQ] = k_ref[b*BQ:(b+1)*BQ,:].astype(F32).T.astype(BF)
    def qstep(i,_):
        base = pl.multiple_of(i*BQ,BQ)
        qb = q_ref[pl.ds(base,BQ),:]*BF(HEAD**-0.5)
        gb = g_ref[pl.ds(base,BQ),:]
        qh = split_heads(qb, heads); gh = split_heads(gb, heads)
        go = (gb.astype(F32)*o_ref[pl.ds(base,BQ),:].astype(F32)).T
        deltas = [jnp.sum(go[h*HEAD:(h+1)*HEAD],axis=0,keepdims=True) for h in range(heads)]
        lses = [lse_ref[h:h+1, pl.ds(base,BQ)] for h in range(heads)]
        pos,start = start_row(len_ref, base, BQ)
        def kstep(j, dq, diag):
            kb = pl.multiple_of(j*bk,bk)
            kk = k_ref[pl.ds(kb,bk),:]; vv=v_ref[pl.ds(kb,bk),:]
            key = kb + lax.broadcasted_iota(jnp.int32,(bk,BQ),0)
            ok = key>=start
            if diag: ok = ok & (key<=pos)
            out=[]
            dk=dka[pl.ds(kb,bk),:]; dv=dva[pl.ds(kb,bk),:]
            for h in range(heads):
                s = dot(kk,qh[h],NT)
                p = jnp.where(ok, jnp.exp(s-lses[h]), 0.0)
                dp = dot(vv,gh[h],NT)
                ds = (p*(dp-deltas[h])).astype(BF)
                dv = dv + dot(p.astype(BF), gh[h], NN)
                dk = dk + dot(ds, qh[h], NN)
                out.append(dq[h] + dot(kt_ref[h*HEAD:(h+1)*HEAD, pl.ds(kb,bk)], ds, NN))
            dka[pl.ds(kb,bk),:]=dk; dva[pl.ds(kb,bk),:]=dv
            return tuple(out)
        dq = tuple(jnp.zeros((HEAD,BQ),F32) for _ in range(heads))
        dq = kstep(i,dq,True)
        dq = lax.fori_loop(0,i,lambda j,c:kstep(j,c,False),dq)
        dq_ref[pl.ds(base,BQ),:] = (jnp.concatenate(dq,axis=0).T*(HEAD**-0.5)).astype(BF)
        return 0
    lax.fori_loop(0, rows//BQ, qstep, 0)
    dk_ref[...] = dka[...].astype(BF); dv_ref[...]=dva[...].astype(BF)

VM=pl.BlockSpec(memory_space=pltpu.VMEM); SM=pl.BlockSpec(memory_space=pltpu.SMEM)
def attn_fwd(lengths,q,k,v):
    S,W=q.shape
    return pl.pallas_call(fwd_kernel,out_shape=(jax.ShapeDtypeStruct((S,W),BF),jax.ShapeDtypeStruct((8,S),F32)),
      in_specs=[SM,VM,VM,VM],out_specs=(VM,VM),scratch_shapes=[pltpu.VMEM((W,S),BF)],compiler_params=pltpu.CompilerParams(vmem_limit_bytes=40<<20))(lengths,q,k,v)
def attn_bwd(lengths,q,k,v,o,g,lse):
    S,W=q.shape
    sh=jax.ShapeDtypeStruct((S,W),BF)
    return pl.pallas_call(bwd_kernel,out_shape=(sh,sh,sh),
      in_specs=[SM]+[VM]*6,out_specs=(VM,VM,VM),scratch_shapes=[pltpu.VMEM((W,S),BF),pltpu.VMEM((S,W),F32),pltpu.VMEM((S,W),F32)],compiler_params=pltpu.CompilerParams(vmem_limit_bytes=40<<20))(lengths,q,k,v,o,g,lse)


def norm_forward(rows_in, gain_vec, shift_vec):
    average = jnp.mean(rows_in, axis=-1, keepdims=True)
    centered = rows_in - average
    inv_std = lax.rsqrt(jnp.mean(centered * centered, axis=-1, keepdims=True) + EPSILON)
    unit_rows = centered * inv_std
    return (unit_rows * gain_vec + shift_vec, unit_rows, inv_std)


def norm_backward(grad_rows, unit_rows, inv_std, gain_vec):
    grad_unit = grad_rows * gain_vec
    grad_in = inv_std * (
        grad_unit
        - jnp.mean(grad_unit, axis=-1, keepdims=True)
        - unit_rows * jnp.mean(grad_unit * unit_rows, axis=-1, keepdims=True)
    )
    return (grad_in, jnp.sum(grad_rows * unit_rows, axis=0), jnp.sum(grad_rows, axis=0))


def contract_rows(left, right):
    return lax.dot_general(
        left, right, (((0,), (0,)), ((), ())), preferred_element_type=jnp.float32
    )


def contract_cols(left, right):
    return lax.dot_general(
        left, right, (((1,), (1,)), ((), ())), preferred_element_type=jnp.float32
    )


def exchange(blocks):
    return lax.all_to_all(blocks, "ep", split_axis=0, concat_axis=0, tiled=True)


def on_device(
    tokens,
    gain_attn,
    shift_attn,
    w_qkv,
    w_o,
    gain_ffn,
    shift_ffn,
    w_in,
    w_out,
    seq_lengths,
    expert_ids,
    cotangent,
):
    rows, width = tokens.shape
    ranks = lax.axis_size("ep")
    copies = lax.axis_size("dp")
    own = width // ranks
    capacity = 2 * rows // ranks
    inputs = tokens.astype(jnp.float32)
    weight_in = w_in[0]
    weight_out = w_out[0]
    hidden = weight_in.shape[0]
    part = hidden // copies
    my_copy = lax.axis_index("dp")
    part_in = lax.dynamic_slice_in_dim(weight_in, my_copy * part, part, 0)
    part_out = lax.dynamic_slice_in_dim(weight_out, my_copy * part, part, 0)

    chosen_ids = expert_ids[:, 0]
    one_hot = (chosen_ids[:, None] == jnp.arange(ranks, dtype=jnp.int32)[None, :]).astype(jnp.int32)
    slot_of = jnp.sum((jnp.cumsum(one_hot, axis=0) - 1) * one_hot, axis=1)
    target = chosen_ids * capacity + slot_of
    placing = (
        jnp.arange(ranks * capacity, dtype=jnp.int32)[:, None] == target[None, :]
    ).astype(jnp.bfloat16)

    def dispatch(values):
        out = jnp.dot(placing, values, preferred_element_type=jnp.float32).astype(jnp.bfloat16)
        return exchange(out.reshape(ranks, capacity, width)).reshape(-1, width)

    g_own = dispatch(cotangent)
    g_all = lax.all_gather(g_own, "dp", axis=0, tiled=True)

    normed, unit_attn, inv_attn = norm_forward(inputs, gain_attn, shift_attn)
    normed_low = normed.astype(jnp.bfloat16)
    normed_all = lax.all_gather(normed_low, "ep", axis=0, tiled=True)
    qkv = jnp.dot(normed_low, w_qkv, preferred_element_type=jnp.float32).astype(jnp.bfloat16)
    to_heads = qkv.reshape(rows, 3, ranks, own).transpose(2, 0, 1, 3).reshape(ranks, rows, 3 * own)
    mine = exchange(to_heads).reshape(ranks * rows, 3 * own)
    queries, keys, values = mine[:, :own], mine[:, own : 2 * own], mine[:, 2 * own :]
    att_heads, lse = attn_fwd(seq_lengths, queries, keys, values)
    attended_low = (
        exchange(att_heads.reshape(ranks, rows, own)).transpose(1, 0, 2).reshape(rows, width)
    )
    hidden_res = inputs + jnp.dot(attended_low, w_o, preferred_element_type=jnp.float32)
    routed, unit_ffn, inv_ffn = norm_forward(hidden_res, gain_ffn, shift_ffn)
    routed_low = routed.astype(jnp.bfloat16)

    x_own = dispatch(routed_low)
    x_all = lax.all_gather(x_own, "dp", axis=0, tiled=True)
    pre = contract_cols(x_own, weight_in)
    grad_act = contract_cols(g_own, weight_out)
    act, gelu_pull = jax.vjp(lambda inner: jax.nn.gelu(inner, approximate=True), pre)
    grad_pre = gelu_pull(grad_act)[0].astype(jnp.bfloat16)
    grad_rows = jnp.dot(grad_pre, weight_in, preferred_element_type=jnp.float32).astype(
        jnp.bfloat16
    )
    grad_back = exchange(grad_rows.reshape(ranks, capacity, width))
    grad_routed = contract_rows(placing, grad_back.reshape(-1, width))
    produced = jnp.dot(
        act.astype(jnp.bfloat16), weight_out, preferred_element_type=jnp.float32
    ).astype(jnp.bfloat16)
    returned = exchange(produced.reshape(ranks, capacity, width))
    expert_rows = contract_rows(placing, returned.reshape(-1, width))
    block_out = (hidden_res + expert_rows).astype(jnp.bfloat16)

    grad_normed2, grad_gain_ffn, grad_shift_ffn = norm_backward(
        grad_routed, unit_ffn, inv_ffn, gain_ffn
    )
    grad_hidden = cotangent.astype(jnp.float32) + grad_normed2
    grad_hidden_low = grad_hidden.astype(jnp.bfloat16)
    grad_att = contract_cols(grad_hidden_low, w_o).astype(jnp.bfloat16)
    grad_att_heads = exchange(grad_att.reshape(rows, ranks, own).transpose(1, 0, 2)).reshape(
        ranks * rows, own
    )
    gh_all = lax.all_gather(grad_hidden_low, "ep", axis=0, tiled=True)
    dq, dk, dv = attn_bwd(seq_lengths, queries, keys, values, att_heads, grad_att_heads, lse)
    dqkv = jnp.concatenate([dq, dk, dv], axis=1)
    dqkv_back = exchange(dqkv.reshape(ranks, rows, 3 * own))
    grad_qkv = dqkv_back.reshape(ranks, rows, 3, own).transpose(1, 2, 0, 3).reshape(rows, 3 * width)
    grad_normed1 = contract_cols(grad_qkv, w_qkv)
    grad_in1, grad_gain_attn, grad_shift_attn = norm_backward(
        grad_normed1, unit_attn, inv_attn, gain_attn
    )
    grad_tokens = grad_hidden + grad_in1

    pre_part = contract_cols(x_all, part_in)
    act_part, part_pull = jax.vjp(lambda inner: jax.nn.gelu(inner, approximate=True), pre_part)
    grad_pre_part = part_pull(contract_cols(g_all, part_out))[0].astype(jnp.bfloat16)
    grad_w_in = contract_rows(grad_pre_part, x_all)[None]
    grad_w_out = contract_rows(act_part.astype(jnp.bfloat16), g_all)[None]

    g_w_qkv = contract_rows(normed_all, dqkv)
    g_w_o = contract_rows(gh_all, att_heads)
    both = jnp.concatenate([g_w_qkv, g_w_o], axis=1).astype(jnp.bfloat16)
    both = lax.psum_scatter(both, "dp", scatter_dimension=0, tiled=True)
    both = lax.all_gather(both, ("dp", "ep"), axis=0, tiled=True)
    both = both.reshape(copies, ranks, width // copies, 4, own).astype(jnp.float32)
    g_qkv_out = both[:, :, :, :3].transpose(0, 2, 3, 1, 4).reshape(width, 3 * width)
    g_o_out = both[:, :, :, 3].transpose(1, 3, 0, 2).reshape(width, width)
    summed = lax.psum(
        (grad_gain_attn, grad_shift_attn, grad_gain_ffn, grad_shift_ffn), ("dp", "ep")
    )
    return (
        block_out,
        grad_tokens,
        g_qkv_out,
        g_o_out,
        summed[0],
        summed[1],
        summed[2],
        summed[3],
        grad_w_in,
        grad_w_out,
    )


def solution(mesh):
    return jax.shard_map(
        on_device,
        mesh=mesh,
        in_specs=(
            P(("dp", "ep"), None),
            P(),
            P(),
            P(),
            P(),
            P(),
            P(),
            P("ep", None, None),
            P("ep", None, None),
            P("dp", None),
            P(("dp", "ep"), None),
            P(("dp", "ep"), None),
        ),
        out_specs=(
            P(("dp", "ep"), None),
            P(("dp", "ep"), None),
            P(),
            P(),
            P(),
            P(),
            P(),
            P(),
            P("ep", "dp", None),
            P("ep", "dp", None),
        ),
        check_vma=False,
    )
```

```python
import functools
import types

import jax
import jax.numpy as jnp
from jax import lax
from jax.experimental import pallas as pl
from jax.experimental.pallas import tpu as pltpu
from jax.sharding import PartitionSpec as P

HEADS = 16
EPSILON = 1e-05
MASKED = -1e30
TILE = 512
SMALL = 8
MESH = pl.DeviceIdType.MESH
F32 = jnp.float32
BF = jnp.bfloat16
NN = (((1,), (0,)), ((), ()))
NT = (((1,), (1,)), ((), ()))
TN = (((0,), (0,)), ((), ()))


def dot(left, right, dims):
    return lax.dot_general(left, right, dims, preferred_element_type=F32)


def partner(me, k, n):
    out, weight = 0, 1
    while weight < n:
        bit = lax.rem(lax.div(me, weight), 2)
        out = out + (lax.rem(bit + 1, 2) if k & weight else bit) * weight
        weight *= 2
    return out


def send(src, dst, send_sem, recv_sem, target):
    return pltpu.make_async_remote_copy(
        src_ref=src,
        dst_ref=dst,
        send_sem=send_sem,
        recv_sem=recv_sem,
        device_id=target,
        device_id_type=MESH,
    )


def order_of(n):
    return sorted(range(1, n), key=lambda k: (-bin(k // 2).count("1"), k))


def flat(value):
    return value.reshape(value.shape[0] * value.shape[1], value.shape[2])


def tiles(count, body):
    def step(t, _):
        body(pl.ds(pl.multiple_of(t * TILE, TILE), TILE))
        return 0

    lax.fori_loop(0, count // TILE, step, 0)


def norm_rows(rows_in):
    average = jnp.mean(rows_in, axis=-1, keepdims=True)
    centered = rows_in - average
    inv_std = lax.rsqrt(jnp.mean(centered * centered, axis=-1, keepdims=True) + EPSILON)
    return centered * inv_std, inv_std


CHUNK = 32


def by_rows(count, body, carry=0):
    def step(i, state):
        return body(pl.ds(pl.multiple_of(i * CHUNK, CHUNK), CHUNK), state)

    return lax.fori_loop(0, count // CHUNK, step, carry)


def norm_apply(src, gain, shift, dst):
    def body(at, _):
        unit, _ = norm_rows(src[at, :].astype(F32))
        dst[at, :] = (unit * gain[...] + shift[...]).astype(BF)
        return 0

    by_rows(src.shape[0], body)


def norm_back(src, grad, gain, store):
    def body(at, sums):
        unit, inv = norm_rows(src[at, :].astype(F32))
        incoming = grad[at, :]
        grad_unit = incoming * gain[...]
        grad_in = inv * (
            grad_unit
            - jnp.mean(grad_unit, axis=-1, keepdims=True)
            - unit * jnp.mean(grad_unit * unit, axis=-1, keepdims=True)
        )
        store(at, grad_in)
        return (
            sums[0] + jnp.sum(incoming * unit, axis=0, keepdims=True),
            sums[1] + jnp.sum(incoming, axis=0, keepdims=True),
        )

    zero = jnp.zeros((1, src.shape[1]), F32)
    return by_rows(src.shape[0], body, (zero, zero))


def gelu_both(pre):
    square = pre * pre
    bent = jnp.tanh(0.7978845608028654 * pre * (1.0 + 0.044715 * square))
    half = 0.5 + 0.5 * bent
    rise = 0.7978845608028654 * (1.0 + 3 * 0.044715 * square)
    return pre * half, half + 0.5 * pre * (1.0 - bent * bent) * rise


def place_matrix(ids_row, n, cap):
    rows = ids_row.shape[1]
    expert = lax.broadcasted_iota(jnp.int32, (n, rows), 0)
    hit = (expert == ids_row).astype(F32)
    before = lax.broadcasted_iota(jnp.int32, (rows, rows), 0)
    after = lax.broadcasted_iota(jnp.int32, (rows, rows), 1)
    upto = (before <= after).astype(F32).astype(BF)
    count = dot(hit.astype(BF), upto, NN)
    slot = jnp.sum(hit * (count - 1.0), axis=0, keepdims=True)
    target = ids_row * cap + slot.astype(jnp.int32)
    places = lax.broadcasted_iota(jnp.int32, (n * cap, rows), 0)
    return (places == target).astype(F32).astype(BF)


def start_row(len_ref, first, width):
    pos = first + lax.broadcasted_iota(jnp.int32, (1, width), 1)
    start = jnp.zeros((1, width), jnp.int32)
    edge = jnp.int32(0)
    for s in range(len_ref.shape[1] - 1):
        edge = edge + len_ref[0, s]
        start = jnp.where(pos >= edge, edge, start)
    return pos, start


def split_heads(block, heads):
    if heads == 1:
        return [block]
    size = block.shape[1] // heads
    lane = lax.broadcasted_iota(jnp.int32, block.shape, 1)
    zero = jnp.zeros_like(block)
    return [
        jnp.where((lane >= h * size) & (lane < (h + 1) * size), block, zero) for h in range(heads)
    ]


def attend_block(r, i):
    rows, own = r.qkv_heads.shape[2:]
    heads = r.heads
    size = own // heads
    queries = split_heads(r.qkv_heads[0, i] * BF(size**-0.5), heads)
    pos, start = start_row(r.lengths, i * rows, rows)

    def fold(j, carry, diagonal):
        keys = r.qkv_heads[1, j]
        key = j * rows + lax.broadcasted_iota(jnp.int32, (rows, rows), 0)
        allowed = key >= start
        if diagonal:
            allowed = allowed & (key <= pos)
        out = []
        for h in range(heads):
            top, total, accum = carry[h]
            scores = jnp.where(allowed, dot(keys, queries[h], NT), MASKED)
            new_top = jnp.maximum(top, jnp.max(scores, axis=0, keepdims=True))
            weights = jnp.exp(scores - new_top)
            if diagonal:
                weights = jnp.where(allowed, weights, 0.0)
            decay = jnp.exp(top - new_top)
            total = total * decay + jnp.sum(weights, axis=0, keepdims=True)
            values = r.values_t[j, h * size : (h + 1) * size, :]
            accum = accum * decay + dot(values, weights.astype(BF), NN)
            out.append((new_top, total, accum))
        return tuple(out)

    state = tuple(
        (
            jnp.full((1, rows), MASKED, F32),
            jnp.zeros((1, rows), F32),
            jnp.zeros((size, rows), F32),
        )
        for _ in range(heads)
    )
    state = fold(i, state, True)
    state = lax.fori_loop(0, i, lambda j, carry: fold(j, carry, False), state)
    result = jnp.concatenate([accum / total for _, total, accum in state], axis=0)
    r.att_heads[i] = result.T.astype(BF)
    sums = [top + jnp.log(total) for top, total, _ in state]
    r.lse[i] = jnp.concatenate(sums + [jnp.zeros((SMALL - heads, rows), F32)], axis=0)


def attend_back(r, j, n):
    rows, own = r.qkv_heads.shape[2:]
    heads = r.heads
    size = own // heads
    keys, values = r.qkv_heads[1, j], r.qkv_heads[2, j]
    keys_t = keys.astype(F32).T.astype(BF)

    def fold(i, carry, diagonal):
        grad_k, grad_v = carry
        queries = split_heads(r.qkv_heads[0, i] * BF(size**-0.5), heads)
        grads = split_heads(r.grad_att[i], heads)
        pos, start = start_row(r.lengths, i * rows, rows)
        key = j * rows + lax.broadcasted_iota(jnp.int32, (rows, rows), 0)
        allowed = key >= start
        if diagonal:
            allowed = allowed & (key <= pos)
        for h in range(heads):
            scores = dot(keys, queries[h], NT)
            probs = jnp.where(allowed, jnp.exp(scores - r.lse[i, h : h + 1, :]), 0.0)
            grad_probs = dot(values, grads[h], NT)
            grad_scores = (probs * (grad_probs - r.delta[i, h : h + 1, :])).astype(BF)
            grad_v = grad_v + dot(probs.astype(BF), grads[h], NN)
            grad_k = grad_k + dot(grad_scores, queries[h], NN)
            part = slice(h * size, (h + 1) * size)
            r.grad_q_t[i, part, :] += dot(keys_t[part, :], grad_scores, NN)
        return grad_k, grad_v

    zero = jnp.zeros((rows, own), F32)
    carry = fold(j, (zero, zero), True)
    grad_k, grad_v = lax.fori_loop(
        j + 1, n, lambda i, carry: fold(i, carry, False), carry
    )
    r.qkv_send[1, j] = grad_k.astype(BF)
    r.qkv_send[2, j] = grad_v.astype(BF)


class Chain:
    def __init__(self, block, whole, send_sem, recv_sem, at, c):
        self.block, self.whole, self.at, self.c = block, whole, at, c
        self.send_sem, self.recv_sem = send_sem, recv_sem

    def copy(self, way, stage):
        held = self.at - stage if way == 0 else self.at + stage
        target = self.at + 1 if way == 0 else self.at - 1
        src = self.block if stage == 0 else self.whole.at[held]
        return send(
            src,
            self.whole.at[held],
            self.send_sem.at[way, stage],
            self.recv_sem.at[way, stage],
            {"dp": target},
        )

    def sends(self, way, stage):
        if way == 0:
            return (self.at >= stage) & (self.at + 1 < self.c)
        return (self.at + stage < self.c) & (self.at >= 1)

    def gets(self, way, stage):
        return self.at >= stage + 1 if way == 0 else self.at + stage + 1 < self.c

    def start(self, stage):
        for way in range(2):
            if stage:

                @pl.when(self.gets(way, stage - 1))
                def _():
                    self.copy(way, stage - 1).wait_recv()

            @pl.when(self.sends(way, stage))
            def _():
                self.copy(way, stage).start()

    def finish(self):
        for way in range(2):

            @pl.when(self.gets(way, self.c - 2))
            def _():
                self.copy(way, self.c - 2).wait_recv()

            for stage in range(self.c - 1):

                @pl.when(self.sends(way, stage))
                def _():
                    self.copy(way, stage).wait_send()


class Spread:
    def __init__(self, r, name, me, grp, n, c, place):
        self.send_buf, self.recv_buf, self.final = (
            getattr(r, name + part) for part in ("_send", "_recv", "_fin")
        )
        self.ss, self.rs = getattr(r, name + "_ss"), getattr(r, name + "_rs")
        self.ys, self.yr = getattr(r, name + "_ys"), getattr(r, name + "_yr")
        self.me, self.grp, self.n, self.c, self.place = me, grp, n, c, place
        self.local = r.load_sem.at[getattr(r, name + "_slot")]
        self.direct = [k for k in order_of(n) if k % 2 == 0]

    def to_piece(self, t):
        target = lax.rem(self.grp + t, self.c)
        return send(
            self.send_buf.at[target],
            self.recv_buf.at[self.grp],
            self.ss.at[0, t],
            self.rs.at[0, t],
            {"dp": target},
        )

    def to_copies(self, t):
        return send(
            self.final,
            self.place(self.me, self.grp),
            self.ss.at[1, t],
            self.rs.at[1, t],
            {"dp": lax.rem(self.grp + t, self.c)},
        )

    def across(self, k):
        block = self.place(self.me, None)
        return send(
            block, block, self.ys.at[k], self.yr.at[k], {"ep": partner(self.me, k, self.n)}
        )

    def pass_on(self, k):
        block = self.place(partner(self.me, k, self.n), None)
        return send(
            block,
            block,
            self.ys.at[k + 1],
            self.yr.at[k + 1],
            {"ep": partner(self.me, 1, self.n)},
        )

    def scatter(self):
        for t in range(1, self.c):
            self.to_piece(t).start()
        self.recv_buf[self.grp] = self.send_buf[self.grp]

    def total(self):
        for t in range(1, self.c):
            self.to_piece(t).wait_recv()
        total = self.recv_buf[0].astype(F32)
        for s in range(1, self.c):
            total = total + self.recv_buf[s].astype(F32)
        self.final[...] = total.astype(BF)
        for t in range(1, self.c):
            self.to_copies(t).start()
        self.mine = pltpu.make_async_copy(
            self.final, self.place(self.me, self.grp), self.local
        )
        self.mine.start()

    def over(self):
        for t in range(1, self.c):
            self.to_copies(t).wait_recv()
        self.mine.wait()
        for k in self.direct + [1]:
            self.across(k).start()

    def share(self):
        for k in self.direct:
            self.across(k).wait_recv()
            self.pass_on(k).start()

    def finish(self):
        self.across(1).wait()
        for k in self.direct:
            self.across(k).wait_send()
            self.pass_on(k).wait()
        for t in range(1, self.c):
            self.to_piece(t).wait_send()
            self.to_copies(t).wait_send()


def block_kernel(r, n, c):
    me, grp = lax.axis_index("ep"), lax.axis_index("dp")
    rows, width = r.tokens.shape
    own, cap = width // n, 2 * rows // n
    slots = n * cap
    hidden = r.w_in.shape[1]
    part = hidden // c
    order = order_of(n)
    direct = [k for k in order if k % 2 == 0]
    partners = {k: partner(me, k, n) for k in order}
    half = width // 2

    def to_partner(src, dst, send_sem, recv_sem, k):
        return send(src, dst, send_sem, recv_sem, {"ep": partners[k]})

    def blocks_out(buf, dst, sems, k):
        return to_partner(buf.at[partners[k]], dst.at[me], sems[0].at[k], sems[1].at[k], k)

    barrier = pltpu.get_barrier_semaphore()
    for k in order:
        pl.semaphore_signal(barrier, inc=1, device_id={"ep": partners[k]}, device_id_type=MESH)
    for t in range(1, c):
        pl.semaphore_signal(
            barrier, inc=1, device_id={"dp": lax.rem(grp + t, c)}, device_id_type=MESH
        )

    def load_qkv(slot):
        cols = pl.ds(0, 3 * width)
        return [
            pltpu.make_async_copy(
                r.w_qkv.at[pl.ds(0, half), :], r.act.at[:, cols], r.load_sem.at[slot]
            ),
            pltpu.make_async_copy(
                r.w_qkv.at[pl.ds(half, half), :], r.grad_pre.at[:, cols], r.load_sem.at[slot + 1]
            ),
        ]

    first_loads = load_qkv(0)
    load_o = pltpu.make_async_copy(r.w_o, r.w_o_v, r.load_sem.at[2])
    load_out = pltpu.make_async_copy(r.w_out.at[0], r.w_out_v, r.load_sem.at[3])
    load_in = pltpu.make_async_copy(r.w_in.at[0], r.w_in_v, r.load_sem.at[4])
    for load in first_loads + [load_o, load_out, load_in]:
        load.start()

    norm_apply(r.tokens, r.gain_attn, r.shift_attn, r.normed)
    pl.semaphore_wait(barrier, n - 1 + c - 1)

    def to_heads(p, k):
        return to_partner(
            r.qkv_send.at[p, partners[k]],
            r.qkv_heads.at[p, me],
            r.a_ss.at[p, k],
            r.a_rs.at[p, k],
            k,
        )

    for load in first_loads:
        load.wait()
    for p in range(3):
        for t in range(width // TILE):
            cols = slice(p * width + t * TILE, p * width + (t + 1) * TILE)
            block = dot(r.normed[:, :half], r.act[:, cols], NN)
            block = (block + dot(r.normed[:, half:], r.grad_pre[:, cols], NN)).astype(BF)
            for e in range(TILE // own):
                r.qkv_send[p, t * (TILE // own) + e] = block[:, e * own : (e + 1) * own]
        for k in order:
            to_heads(p, k).start()
        r.qkv_heads[p, me] = r.qkv_send[p, me]

    r.place[...] = place_matrix(r.ids[...], n, cap)
    for t in range(width // TILE):
        cols = slice(t * TILE, (t + 1) * TILE)
        r.g_send[:, :, cols] = (
            dot(r.place[...], r.cotangent[:, cols], NN).astype(BF).reshape(n, cap, TILE)
        )
    for p in range(3):
        for k in order:
            to_heads(p, k).wait_recv()
    g_copies = [blocks_out(r.g_send, r.g_own, (r.g_ss, r.g_rs), k) for k in order]
    for copy in g_copies:
        copy.start()
    r.g_own[me] = r.g_send[me]

    def gather(k):
        return to_partner(r.normed, r.normed_all.at[me], r.n_ss.at[k], r.n_rs.at[k], k)

    def pass_on(k):
        src = r.normed_all.at[partners[k]]
        return to_partner(src, src, r.n_ss.at[k + 1], r.n_rs.at[k + 1], 1)

    for k in direct + [1]:
        gather(k).start()
    mine = pltpu.make_async_copy(r.normed, r.normed_all.at[me], r.load_sem.at[5])
    mine.start()

    for i in range(n):
        r.values_t[i] = r.qkv_heads[2, i].astype(F32).T.astype(BF)

    def home(t):
        target = lax.rem(me + t, n)
        return send(
            r.att_heads.at[target],
            r.att_recv.at[me],
            r.o_ss.at[t],
            r.o_rs.at[t],
            {"ep": target},
        )

    attend_block(r, me)
    r.att_recv[me] = r.att_heads[me]

    def block_step(t, _):
        attend_block(r, lax.rem(me + t, n))
        home(t).start()
        return 0

    lax.fori_loop(1, n // 2, block_step, 0)
    for copy in g_copies:
        copy.wait()
    g_chain = Chain(r.g_own, r.g_all, r.gz_ss, r.gz_rs, grp, c)
    x_chain = Chain(r.x_own, r.x_all, r.xz_ss, r.xz_rs, grp, c)
    g_chain.start(0)
    lax.fori_loop(n // 2, n, block_step, 0)
    for k in direct:
        gather(k).wait_recv()
        pass_on(k).start()
    for t in range(1, n):
        home(t).wait_recv()
    for e in range(n):
        r.attended[:, e * own : (e + 1) * own] = r.att_recv[e]

    load_o.wait()
    for t in range(width // TILE):
        cols = slice(t * TILE, (t + 1) * TILE)
        r.hidden[:, cols] = r.tokens[:, cols].astype(F32) + dot(
            r.attended[...], r.w_o_v[:, cols], NN
        )
    norm_apply(r.hidden, r.gain_ffn, r.shift_ffn, r.block_out)
    for t in range(width // TILE):
        cols = slice(t * TILE, (t + 1) * TILE)
        r.x_send[:, :, cols] = (
            dot(r.place[...], r.block_out[:, cols], NN).astype(BF).reshape(n, cap, TILE)
        )
    x_copies = [blocks_out(r.x_send, r.x_own, (r.x_ss, r.x_rs), k) for k in order]
    for copy in x_copies:
        copy.start()
    r.x_own[me] = r.x_send[me]
    g_chain.start(1)

    load_out.wait()

    def act_grad(t, _):
        at = pl.multiple_of(t * TILE, TILE)
        r.grad_pre[:, pl.ds(at, TILE)] = dot(
            flat(r.g_own[...]), r.w_out_v[pl.ds(at, TILE), :], NT
        ).astype(BF)
        return 0

    lax.fori_loop(0, hidden // TILE, act_grad, 0)
    load_in.wait()
    for copy in x_copies:
        copy.wait()
    x_chain.start(0)
    g_chain.start(2) if c > 3 else None
    carried = r.grad_in.at[pl.ds(0, slots), :]
    carried[...] = jnp.zeros((slots, width), F32)

    def expert_step(t, _):
        at = pl.multiple_of(t * TILE, TILE)
        cols = pl.ds(at, TILE)
        pre = dot(flat(r.x_own[...]), r.w_in_v[cols, :], NT)
        for q in range(slots // CHUNK):
            at = slice(q * CHUNK, (q + 1) * CHUNK)
            act, slope = gelu_both(pre[at])
            r.act[at, cols] = act.astype(BF)
            r.grad_pre[at, cols] = (r.grad_pre[at, cols].astype(F32) * slope).astype(BF)
        grad_pre = r.grad_pre[:, cols]
        for s in range(width // TILE):
            part_cols = slice(s * TILE, (s + 1) * TILE)
            carried[:, part_cols] += dot(grad_pre, r.w_in_v[cols, part_cols], NN)
        return 0

    lax.fori_loop(0, hidden // TILE, expert_step, 0)
    r.g_send[...] = carried[...].astype(BF).reshape(n, cap, width)
    r_copies = [blocks_out(r.g_send, r.r_recv, (r.r_ss, r.r_rs), k) for k in order]
    for copy in r_copies:
        copy.start()
    r.r_recv[me] = r.g_send[me]

    def produce(cols):
        r.x_send[:, :, cols] = (
            dot(r.act[...], r.w_out_v[:, cols], NN).astype(BF).reshape(n, cap, TILE)
        )

    tiles(width, produce)
    p_copies = [blocks_out(r.x_send, r.p_recv, (r.p_ss, r.p_rs), k) for k in order]
    for copy in p_copies:
        copy.start()
    r.p_recv[me] = r.x_send[me]
    mine_at = pl.multiple_of(grp * part, part)

    def weight_terms(act_at, x_rows, g_rows, first):
        def one(out):
            from_act = pl.ds(pl.multiple_of(act_at + out.start, TILE), TILE)

            def two(cols):
                term_in = dot(r.grad_pre[:, from_act], x_rows(cols), TN)
                r.grad_in[out, cols] = term_in if first else r.grad_in[out, cols] + term_in
                term_out = dot(r.act[:, from_act], g_rows(cols), TN)
                r.grad_out[out, cols] = term_out if first else r.grad_out[out, cols] + term_out

            tiles(width, two)

        tiles(part, one)

    weight_terms(
        mine_at,
        lambda cols: flat(r.x_own[:, :, cols]),
        lambda cols: flat(r.g_own[:, :, cols]),
        True,
    )

    for copy in r_copies:
        copy.wait()
    for t in range(width // TILE):
        cols = slice(t * TILE, (t + 1) * TILE)
        r.grad_tokens[:, cols] = dot(r.place[...], flat(r.r_recv[:, :, cols]), TN)

    def store_hidden(at, grad_in):
        grad_hidden = r.cotangent[at, :].astype(F32) + grad_in
        r.grad_tokens[at, :] = grad_hidden
        r.block_out[at, :] = grad_hidden.astype(BF)

    sums = norm_back(r.hidden, r.grad_tokens, r.gain_ffn, store_hidden)
    r.small_own[2:3], r.small_own[3:4] = sums
    r.small_own[4:SMALL] = jnp.zeros((SMALL - 4, width), F32)
    for t in range(width // TILE):
        block = dot(r.block_out[...], r.w_o_v[t * TILE : (t + 1) * TILE, :], NT).astype(BF)
        for e in range(TILE // own):
            r.att_recv[t * (TILE // own) + e] = block[:, e * own : (e + 1) * own]
    a_copies = [blocks_out(r.att_recv, r.grad_att, (r.b_ss, r.b_rs), k) for k in order]
    for copy in a_copies:
        copy.start()
    r.grad_att[me] = r.att_recv[me]

    wo_out, wo_in = r.space.at[pl.ds(0, width), :], r.space.at[pl.ds(width, width), :]

    def wo_term(out):
        wo_out[out, :] = dot(r.attended[:, out], r.block_out[...], TN).astype(BF)

    tiles(width, wo_term)

    def to_owner(k):
        src = r.space.at[pl.ds(pl.multiple_of(partners[k] * own, own), own), :]
        dst = r.space.at[pl.ds(pl.multiple_of(width + me * own, own), own), :]
        return to_partner(src, dst, r.w_ss.at[k], r.w_rs.at[k], k)

    for k in order:
        to_owner(k).start()
    at_me = pl.ds(pl.multiple_of(me * own, own), own)
    wo_in[at_me, :] = wo_out[at_me, :]

    for copy in p_copies:
        copy.wait()
    for t in range(width // TILE):
        cols = slice(t * TILE, (t + 1) * TILE)
        r.block_out[:, cols] = (
            r.hidden[:, cols] + dot(r.place[...], flat(r.p_recv[:, :, cols]), TN)
        ).astype(BF)

    for copy in a_copies:
        copy.wait()
    for p in range(3):
        for k in order:
            to_heads(p, k).wait_send()
    for t in range(1, n):
        home(t).wait_send()
    for i in range(n):
        both = (r.grad_att[i].astype(F32) * r.att_heads[i].astype(F32)).T
        size = own // r.heads
        deltas = [
            jnp.sum(both[h * size : (h + 1) * size], axis=0, keepdims=True) for h in range(r.heads)
        ]
        r.delta[i] = jnp.concatenate(
            deltas + [jnp.zeros((SMALL - r.heads, rows), F32)], axis=0
        )
    r.grad_q_t[...] = jnp.zeros(r.grad_q_t.shape, F32)

    def back_home(p, t):
        target = lax.rem(me + t, n)
        return send(
            r.qkv_send.at[p, target],
            r.grad_tok.at[p, me],
            r.d_ss.at[p, t],
            r.d_rs.at[p, t],
            {"ep": target},
        )

    attend_back(r, me, n)
    for p in (1, 2):
        r.grad_tok[p, me] = r.qkv_send[p, me]

    def back_step(t, _):
        attend_back(r, lax.rem(me + t, n), n)
        for p in (1, 2):
            back_home(p, t).start()
        return 0

    lax.fori_loop(1, n // 2, back_step, 0)
    if c > 2:
        x_chain.start(1)
    lax.fori_loop(n // 2, n, back_step, 0)
    for i in range(n):
        r.qkv_send[0, i] = (r.grad_q_t[i].T * ((own // r.heads) ** -0.5)).astype(BF)
    for t in range(1, n):
        back_home(0, t).start()
    r.grad_tok[0, me] = r.qkv_send[0, me]
    for stage in range(3, c - 1):
        g_chain.start(stage)
    for stage in range(2, c - 1):
        x_chain.start(stage)

    piece = width // c
    for k in order:
        to_owner(k).wait()

    def o_place(e, d):
        at = pl.ds(pl.multiple_of(e * own, own), own)
        if d is None:
            return r.o_all.at[at, :]
        return r.o_all.at[at, pl.ds(pl.multiple_of(d * piece, piece), piece)]

    def q_place(e, d):
        if d is None:
            return r.q_all.at[:, e]
        return r.q_all.at[:, e, pl.ds(pl.multiple_of(d * piece, piece), piece), :]

    o_spread = Spread(r, "wo", me, grp, n, c, o_place)
    q_spread = Spread(r, "wq", me, grp, n, c, q_place)
    total = wo_in[0:own, :].astype(F32)
    for e in range(1, n):
        total = total + wo_in[e * own : (e + 1) * own, :].astype(F32)
    for d in range(c):
        r.wo_send[d] = total[:, d * piece : (d + 1) * piece].astype(BF)
    o_spread.scatter()

    for k in direct:
        pass_on(k).wait()
        gather(k).wait_send()
    gather(1).wait()
    mine.wait()
    at_once = width // rows
    turns = n // at_once

    def normed_loads(t):
        out = []
        for b in range(turns):
            spot = (t if turns <= 2 else b // 2) * TILE
            for s in range(at_once):
                out.append(
                    pltpu.make_async_copy(
                        r.normed_all.at[b * at_once + s, :, pl.ds(t * TILE, TILE)],
                        r.space.at[
                            pl.ds((b % 2) * width + s * rows, rows), pl.ds(spot, TILE)
                        ],
                        r.slab_sem.at[t % 2, b * at_once + s],
                    )
                )
        return out

    for t in range(width // TILE if turns <= 2 else 1):
        for load in normed_loads(t):
            load.start()
    for t in range(width // TILE):
        if turns > 2 and t:
            for load in normed_loads(t):
                load.start()
        for load in normed_loads(t):
            load.wait()
        total = None
        for b in range(turns):
            spot = (t if turns <= 2 else b // 2) * TILE
            grads = jnp.concatenate(
                [flat(r.qkv_send[p, b * at_once : (b + 1) * at_once]) for p in range(3)], axis=1
            )
            term = dot(
                r.space[(b % 2) * width : (b % 2 + 1) * width, spot : spot + TILE], grads, TN
            )
            total = term if b == 0 else total + term
        low = total.astype(BF)
        for s in range(TILE // piece):
            for p in range(3):
                r.wq_send[t * (TILE // piece) + s, p] = low[
                    s * piece : (s + 1) * piece, p * own : (p + 1) * own
                ]
    q_spread.scatter()
    last_loads = load_qkv(0)
    for load in last_loads:
        load.start()

    g_chain.finish()
    x_chain.finish()

    def slab_loads(q):
        at = lax.rem(grp + q, c)
        base = (q % 2) * width
        out = []
        for which, src in enumerate((r.x_all, r.g_all)):
            for s in range(n):
                out.append(
                    pltpu.make_async_copy(
                        src.at[at, s],
                        r.space.at[pl.ds(base + which * slots + s * cap, cap), :],
                        r.slab_sem.at[q % 2, which * n + s],
                    )
                )
        return out

    def slab(q):
        base = (q % 2) * width
        for load in slab_loads(q):
            load.wait()
        if q + 1 < c:
            for load in slab_loads(q + 1):
                load.start()
        x_rows, g_rows = r.space.at[pl.ds(base, slots), :], r.space.at[pl.ds(base + slots, slots), :]

        def activate(out):
            at = pl.ds(pl.multiple_of(mine_at + out.start, TILE), TILE)
            cols = pl.ds(pl.multiple_of(3 * width + out.start, TILE), TILE)
            r.grad_pre[:, cols] = dot(g_rows[...], r.w_out_v[at, :], NT).astype(BF)
            pre = dot(x_rows[...], r.w_in_v[at, :], NT)
            for q in range(slots // CHUNK):
                some = slice(q * CHUNK, (q + 1) * CHUNK)
                act, slope = gelu_both(pre[some])
                r.act[some, cols] = act.astype(BF)
                r.grad_pre[some, cols] = (r.grad_pre[some, cols].astype(F32) * slope).astype(BF)

        tiles(part, activate)
        weight_terms(
            3 * width, lambda cols: x_rows[:, cols], lambda cols: g_rows[:, cols], False
        )

    for load in slab_loads(1):
        load.start()
    o_spread.total()
    slab(1)
    q_spread.total()

    for p in (1, 2, 0):
        for t in range(1, n):
            back_home(p, t).wait_recv()
    for load in last_loads:
        load.wait()
    for p in range(3):
        for e in range(n):
            r.attended[:, e * own : (e + 1) * own] = r.grad_tok[p, e]
        cols = slice(p * width, (p + 1) * width)
        for at, weight in enumerate((r.act, r.grad_pre)):
            out = slice(at * half, (at + 1) * half)
            term = dot(r.attended[...], weight[:, cols], NT)
            r.hidden[:, out] = term if p == 0 else r.hidden[:, out] + term

    def store_tokens(at, grad_in):
        r.grad_tokens[at, :] += grad_in

    sums = norm_back(r.tokens, r.hidden, r.gain_attn, store_tokens)
    r.small_own[0:1], r.small_own[1:2] = sums

    def small_ep(k):
        return to_partner(r.small_own, r.small_ep.at[me], r.s_ss.at[0, k], r.s_rs.at[0, k], k)

    def small_dp(t):
        return send(
            r.small_sum,
            r.small_dp.at[grp],
            r.s_ss.at[1, t],
            r.s_rs.at[1, t],
            {"dp": lax.rem(grp + t, c)},
        )

    for k in order:
        small_ep(k).start()
    r.small_ep[me] = r.small_own[...]
    o_spread.over()
    for q in range(2, c):
        slab(q)
        if q == 2:
            q_spread.over()
            o_spread.share()
    if c <= 2:
        q_spread.over()
        o_spread.share()
    for k in order:
        small_ep(k).wait()
    total = r.small_ep[0]
    for e in range(1, n):
        total = total + r.small_ep[e]
    r.small_sum[...] = total
    for t in range(1, c):
        small_dp(t).start()
    r.small_dp[grp] = total
    q_spread.share()
    for t in range(1, c):
        small_dp(t).wait()
    total = r.small_dp[0]
    for d in range(1, c):
        total = total + r.small_dp[d]
    r.small[...] = total
    o_spread.finish()
    q_spread.finish()
    for p in range(3):
        for t in range(1, n):
            back_home(p, t).wait_send()


def block_call(n, c, heads, operands):
    rows, width = operands["tokens"].shape
    hidden = operands["w_in"].shape[1]
    own, cap, part, piece = width // n, 2 * rows // n, hidden // c, width // c
    slots = n * cap
    vm, hb = pl.BlockSpec(memory_space=pltpu.VMEM), pl.BlockSpec(memory_space=pl.ANY)
    sm = pl.BlockSpec(memory_space=pltpu.SMEM)
    inputs = dict(
        lengths=sm, ids=vm, tokens=vm, cotangent=vm, gain_attn=vm, shift_attn=vm, gain_ffn=vm,
        shift_ffn=vm, w_qkv=hb, w_o=hb, w_in=hb, w_out=hb,
    )
    outputs = dict(
        block_out=((rows, width), BF, vm),
        grad_tokens=((rows, width), F32, vm),
        q_all=((3, n, width, own), BF, hb),
        o_all=((width, width), BF, hb),
        small=((SMALL, width), F32, vm),
        grad_in=((part, width), F32, vm),
        grad_out=((part, width), F32, vm),
        g_all=((c, n, cap, width), BF, hb),
        x_all=((c, n, cap, width), BF, hb),
        normed_all=((n, rows, width), BF, hb),
    )

    def v(*shape):
        return pltpu.VMEM(shape, BF)

    def f(*shape):
        return pltpu.VMEM(shape, F32)

    def d(*shape):
        return pltpu.SemaphoreType.DMA(shape)

    heads_shape = (n, rows, own)
    scratch = dict(
        w_o_v=v(width, width), w_in_v=v(hidden, width), w_out_v=v(hidden, width),
        act=v(slots, hidden), grad_pre=v(slots, hidden), space=v(2 * width, width),
        normed=v(rows, width), place=v(slots, rows), hidden=f(rows, width),
        attended=v(rows, width),
        qkv_send=v(3, *heads_shape), qkv_heads=v(3, *heads_shape), grad_tok=v(3, *heads_shape),
        values_t=v(n, own, rows), att_heads=v(*heads_shape), att_recv=v(*heads_shape),
        grad_att=v(*heads_shape), grad_q_t=f(n, own, rows),
        lse=f(n, SMALL, rows), delta=f(n, SMALL, rows),
        g_send=v(n, cap, width), x_send=v(n, cap, width), g_own=v(n, cap, width),
        x_own=v(n, cap, width), r_recv=v(n, cap, width), p_recv=v(n, cap, width),
        wo_send=v(c, own, piece), wo_recv=v(c, own, piece), wo_fin=v(own, piece),
        wq_send=v(c, 3, piece, own), wq_recv=v(c, 3, piece, own),
        wq_fin=v(3, piece, own),
        small_own=f(SMALL, width), small_ep=f(n, SMALL, width), small_sum=f(SMALL, width),
        small_dp=f(c, SMALL, width),
        load_sem=d(8), slab_sem=d(2, 2 * n),
        a_ss=d(3, n), a_rs=d(3, n), g_ss=d(n), g_rs=d(n), n_ss=d(n), n_rs=d(n),
        o_ss=d(n), o_rs=d(n), x_ss=d(n), x_rs=d(n), r_ss=d(n), r_rs=d(n), p_ss=d(n), p_rs=d(n),
        b_ss=d(n), b_rs=d(n), w_ss=d(n), w_rs=d(n), d_ss=d(3, n), d_rs=d(3, n),
        gz_ss=d(2, c), gz_rs=d(2, c), xz_ss=d(2, c), xz_rs=d(2, c),
        wo_ss=d(2, c), wo_rs=d(2, c), wo_ys=d(n), wo_yr=d(n),
        wq_ss=d(2, c), wq_rs=d(2, c), wq_ys=d(n), wq_yr=d(n),
        s_ss=d(2, max(n, c)), s_rs=d(2, max(n, c)),
    )
    names = list(inputs) + list(outputs) + list(scratch)

    def kernel(*refs):
        r = types.SimpleNamespace(**dict(zip(names, refs)))
        r.heads, r.wo_slot, r.wq_slot = heads, 6, 7
        block_kernel(r, n, c)

    result = pl.pallas_call(
        kernel,
        out_shape=[jax.ShapeDtypeStruct(shape, kind) for shape, kind, _ in outputs.values()],
        in_specs=list(inputs.values()),
        out_specs=[spec for _, _, spec in outputs.values()],
        scratch_shapes=list(scratch.values()),
        compiler_params=pltpu.CompilerParams(
            collective_id=0, has_side_effects=True, vmem_limit_bytes=VMEM_LIMIT
        ),
    )(*[operands[name] for name in inputs])
    return dict(zip(outputs, result))


VMEM_LIMIT = 64 << 20


def on_device(
    tokens,
    gain_attn,
    shift_attn,
    w_qkv,
    w_o,
    gain_ffn,
    shift_ffn,
    w_in,
    w_out,
    seq_lengths,
    expert_ids,
    cotangent,
):
    rows, width = tokens.shape
    n, c = lax.axis_size("ep"), lax.axis_size("dp")
    operands = dict(
        lengths=seq_lengths,
        ids=expert_ids.reshape(1, rows),
        tokens=tokens,
        cotangent=cotangent,
        gain_attn=gain_attn[None],
        shift_attn=shift_attn[None],
        gain_ffn=gain_ffn[None],
        shift_ffn=shift_ffn[None],
        w_qkv=w_qkv,
        w_o=w_o,
        w_in=w_in,
        w_out=w_out,
    )
    out = block_call(n, c, HEADS // n, operands)
    grad_w_qkv = out["q_all"].transpose(2, 0, 1, 3).reshape(width, 3 * width).astype(F32)
    grad_w_o = out["o_all"].astype(F32)
    small = out["small"]
    return (
        out["block_out"],
        out["grad_tokens"],
        grad_w_qkv,
        grad_w_o,
        small[0],
        small[1],
        small[2],
        small[3],
        out["grad_in"][None],
        out["grad_out"][None],
    )


def solution(mesh):
    return jax.shard_map(
        on_device,
        mesh=mesh,
        in_specs=(
            P(("dp", "ep"), None),
            P(),
            P(),
            P(),
            P(),
            P(),
            P(),
            P("ep", None, None),
            P("ep", None, None),
            P("dp", None),
            P(("dp", "ep"), None),
            P(("dp", "ep"), None),
        ),
        out_specs=(
            P(("dp", "ep"), None),
            P(("dp", "ep"), None),
            P(),
            P(),
            P(),
            P(),
            P(),
            P(),
            P("ep", "dp", None),
            P("ep", "dp", None),
        ),
        check_vma=False,
    )
```

```python
import functools
import types

import jax
import jax.numpy as jnp
from jax import lax
from jax.experimental import pallas as pl
from jax.experimental.pallas import tpu as pltpu
from jax.sharding import PartitionSpec as P

HEADS = 16
EPSILON = 1e-05
MASKED = -1e30
TILE = 512
SMALL = 8
UNROLLED = 8
AT_ONCE = 4
MESH = pl.DeviceIdType.MESH
F32 = jnp.float32
BF = jnp.bfloat16
NN = (((1,), (0,)), ((), ()))
NT = (((1,), (1,)), ((), ()))
TN = (((0,), (0,)), ((), ()))


def dot(left, right, dims):
    return lax.dot_general(left, right, dims, preferred_element_type=F32)


def partner(me, k, n):
    out, weight = 0, 1
    while weight < n:
        bit = lax.rem(lax.div(me, weight), 2)
        out = out + (lax.rem(bit + 1, 2) if k & weight else bit) * weight
        weight *= 2
    return out


def send(src, dst, send_sem, recv_sem, target):
    return pltpu.make_async_remote_copy(
        src_ref=src,
        dst_ref=dst,
        send_sem=send_sem,
        recv_sem=recv_sem,
        device_id=target,
        device_id_type=MESH,
    )


def order_of(n):
    return sorted(range(1, n), key=lambda k: (-bin(k // 2).count("1"), k))


def flat(value):
    return value.reshape(value.shape[0] * value.shape[1], value.shape[2])


def tiles(count, body):
    def step(t, _):
        body(pl.ds(pl.multiple_of(t * TILE, TILE), TILE))
        return 0

    lax.fori_loop(0, count // TILE, step, 0)


def norm_rows(rows_in):
    average = jnp.mean(rows_in, axis=-1, keepdims=True)
    centered = rows_in - average
    inv_std = lax.rsqrt(jnp.mean(centered * centered, axis=-1, keepdims=True) + EPSILON)
    return centered * inv_std, inv_std


CHUNK = 32


def by_rows(count, body, carry=0):
    def step(i, state):
        return body(pl.ds(pl.multiple_of(i * CHUNK, CHUNK), CHUNK), state)

    return lax.fori_loop(0, count // CHUNK, step, carry)


def norm_apply(src, gain, shift, dst):
    def body(at, _):
        unit, _ = norm_rows(src[at, :].astype(F32))
        dst[at, :] = (unit * gain[...] + shift[...]).astype(BF)
        return 0

    by_rows(src.shape[0], body)


def norm_back(src, grad, gain, store):
    def body(at, sums):
        unit, inv = norm_rows(src[at, :].astype(F32))
        incoming = grad[at, :]
        grad_unit = incoming * gain[...]
        grad_in = inv * (
            grad_unit
            - jnp.mean(grad_unit, axis=-1, keepdims=True)
            - unit * jnp.mean(grad_unit * unit, axis=-1, keepdims=True)
        )
        store(at, grad_in)
        return (
            sums[0] + jnp.sum(incoming * unit, axis=0, keepdims=True),
            sums[1] + jnp.sum(incoming, axis=0, keepdims=True),
        )

    zero = jnp.zeros((1, src.shape[1]), F32)
    return by_rows(src.shape[0], body, (zero, zero))


def gelu_both(pre):
    square = pre * pre
    bent = jnp.tanh(0.7978845608028654 * pre * (1.0 + 0.044715 * square))
    half = 0.5 + 0.5 * bent
    rise = 0.7978845608028654 * (1.0 + 3 * 0.044715 * square)
    return pre * half, half + 0.5 * pre * (1.0 - bent * bent) * rise


def place_matrix(ids_row, n, cap):
    rows = ids_row.shape[1]
    expert = lax.broadcasted_iota(jnp.int32, (n, rows), 0)
    hit = (expert == ids_row).astype(F32)
    before = lax.broadcasted_iota(jnp.int32, (rows, rows), 0)
    after = lax.broadcasted_iota(jnp.int32, (rows, rows), 1)
    upto = (before <= after).astype(F32).astype(BF)
    count = dot(hit.astype(BF), upto, NN)
    slot = jnp.sum(hit * (count - 1.0), axis=0, keepdims=True)
    target = ids_row * cap + slot.astype(jnp.int32)
    places = lax.broadcasted_iota(jnp.int32, (n * cap, rows), 0)
    return (places == target).astype(F32).astype(BF)


def start_row(len_ref, first, width):
    pos = first + lax.broadcasted_iota(jnp.int32, (1, width), 1)
    start = jnp.zeros((1, width), jnp.int32)
    edge = jnp.int32(0)
    for s in range(len_ref.shape[1] - 1):
        edge = edge + len_ref[0, s]
        start = jnp.where(pos >= edge, edge, start)
    return pos, start


def split_heads(block, heads):
    if heads == 1:
        return [block]
    size = block.shape[1] // heads
    lane = lax.broadcasted_iota(jnp.int32, block.shape, 1)
    zero = jnp.zeros_like(block)
    return [
        jnp.where((lane >= h * size) & (lane < (h + 1) * size), block, zero) for h in range(heads)
    ]


def attend_block(r, i):
    rows, own = r.qkv_heads.shape[2:]
    heads = r.heads
    size = own // heads
    queries = split_heads(r.qkv_heads[0, i] * BF(size**-0.5), heads)
    pos, start = start_row(r.lengths, i * rows, rows)
    outs, sums = [], []
    for h in range(heads):
        top = jnp.full((1, rows), MASKED, F32)
        total = jnp.zeros((1, rows), F32)
        accum = jnp.zeros((size, rows), F32)
        for last in range(i, -1, -AT_ONCE):
            scores = []
            blocks = range(last, max(last - AT_ONCE, -1), -1)
            for j in blocks:
                key = j * rows + lax.broadcasted_iota(jnp.int32, (rows, rows), 0)
                allowed = key >= start
                if j == i:
                    allowed = allowed & (key <= pos)
                scores.append(
                    jnp.where(allowed, dot(r.qkv_heads[1, j], queries[h], NT), MASKED)
                )
            peak = functools.reduce(
                jnp.maximum, [jnp.max(s.reshape(rows // 8, 8, rows), axis=0) for s in scores]
            )
            new_top = jnp.maximum(top, jnp.max(peak, axis=0, keepdims=True))
            decay = jnp.exp(top - new_top)
            accum = accum * decay
            part = jnp.zeros((8, rows), F32)
            for j, s in zip(blocks, scores):
                weights = jnp.exp(s - new_top)
                part = part + jnp.sum(weights.reshape(rows // 8, 8, rows), axis=0)
                values = r.values_t[j, h * size : (h + 1) * size, :]
                accum = accum + dot(values, weights.astype(BF), NN)
            total = total * decay + jnp.sum(part, axis=0, keepdims=True)
            top = new_top
        outs.append(accum / total)
        sums.append(top + jnp.log(total))
    r.att_heads[i] = jnp.concatenate(outs, axis=0).T.astype(BF)
    r.lse[i] = jnp.concatenate(sums + [jnp.zeros((SMALL - heads, rows), F32)], axis=0)


def attend_back(r, j, n):
    rows, own = r.qkv_heads.shape[2:]
    heads = r.heads
    size = own // heads
    keys, values = r.qkv_heads[1, j], r.qkv_heads[2, j]
    keys_t = keys.astype(F32).T.astype(BF)

    def fold(at, carry, diagonal):
        grad_k, grad_v = carry
        for i in at:
            queries = split_heads(r.qkv_heads[0, i] * BF(size**-0.5), heads)
            grads = split_heads(r.grad_att[i], heads)
            pos, start = start_row(r.lengths, i * rows, rows)
            key = j * rows + lax.broadcasted_iota(jnp.int32, (rows, rows), 0)
            allowed = key >= start
            if diagonal:
                allowed = allowed & (key <= pos)
            for h in range(heads):
                scores = dot(keys, queries[h], NT)
                probs = jnp.where(allowed, jnp.exp(scores - r.lse[i, h : h + 1, :]), 0.0)
                grad_probs = dot(values, grads[h], NT)
                grad_scores = (probs * (grad_probs - r.delta[i, h : h + 1, :])).astype(BF)
                grad_v = grad_v + dot(probs.astype(BF), grads[h], NN)
                grad_k = grad_k + dot(grad_scores, queries[h], NN)
                part = slice(h * size, (h + 1) * size)
                r.grad_q_t[i, part, :] += dot(keys_t[part, :], grad_scores, NN)
        return grad_k, grad_v

    zero = jnp.zeros((rows, own), F32)
    carry = fold([j], (zero, zero), True)
    left = n - 1 - j
    odd = lax.rem(left, 2)
    carry = lax.fori_loop(j + 1, j + 1 + odd, lambda i, carry: fold([i], carry, False), carry)

    def pair(t, carry):
        i = j + 1 + odd + 2 * t
        return fold([i, i + 1], carry, False)

    grad_k, grad_v = lax.fori_loop(0, lax.div(left, 2), pair, carry)
    r.qkv_send[1, j] = grad_k.astype(BF)
    r.qkv_send[2, j] = grad_v.astype(BF)


def attend_block_loop(r, i):
    rows, own = r.qkv_heads.shape[2:]
    heads = r.heads
    size = own // heads
    queries = split_heads(r.qkv_heads[0, i] * BF(size**-0.5), heads)
    pos, start = start_row(r.lengths, i * rows, rows)

    def fold(j, carry, diagonal):
        keys = r.qkv_heads[1, j]
        key = j * rows + lax.broadcasted_iota(jnp.int32, (rows, rows), 0)
        allowed = key >= start
        if diagonal:
            allowed = allowed & (key <= pos)
        out = []
        for h in range(heads):
            top, total, accum = carry[h]
            scores = jnp.where(allowed, dot(keys, queries[h], NT), MASKED)
            new_top = jnp.maximum(top, jnp.max(scores, axis=0, keepdims=True))
            weights = jnp.exp(scores - new_top)
            if diagonal:
                weights = jnp.where(allowed, weights, 0.0)
            decay = jnp.exp(top - new_top)
            total = total * decay + jnp.sum(weights, axis=0, keepdims=True)
            values = r.values_t[j, h * size : (h + 1) * size, :]
            accum = accum * decay + dot(values, weights.astype(BF), NN)
            out.append((new_top, total, accum))
        return tuple(out)

    state = tuple(
        (
            jnp.full((1, rows), MASKED, F32),
            jnp.zeros((1, rows), F32),
            jnp.zeros((size, rows), F32),
        )
        for _ in range(heads)
    )
    state = fold(i, state, True)
    state = lax.fori_loop(0, i, lambda j, carry: fold(j, carry, False), state)
    result = jnp.concatenate([accum / total for _, total, accum in state], axis=0)
    r.att_heads[i] = result.T.astype(BF)
    sums = [top + jnp.log(total) for top, total, _ in state]
    r.lse[i] = jnp.concatenate(sums + [jnp.zeros((SMALL - heads, rows), F32)], axis=0)


class Line:
    def __init__(self, block, whole, send_sem, recv_sem, at, c):
        self.block, self.whole, self.at, self.c = block, whole, at, c
        self.send_sem, self.recv_sem = send_sem, recv_sem

    def direct(self, way, hops):
        target = self.at + way * hops
        return self.can(target), send(
            self.block,
            self.whole.at[self.at],
            self.send_sem.at[(way + 1) // 2, hops - 1],
            self.recv_sem.at[self.at],
            {"dp": target},
        )

    def can(self, index):
        return (index >= 0) & (index < self.c)

    def onward(self, way, stage):
        held = self.at - way * (2 + stage)
        target = self.at + way
        src = self.whole.at[held]
        return self.can(held) & self.can(target), send(
            src,
            src,
            self.send_sem.at[(way + 1) // 2, 2 + stage],
            self.recv_sem.at[held],
            {"dp": target},
        )

    def start(self):
        for hops in range(1, min(3, self.c)):
            for way in (-1, 1):
                allowed, copy = self.direct(way, hops)
                pl.when(allowed)(copy.start)

    def hand_on(self):
        for stage in range(self.c - 3):
            for way in (-1, 1):
                allowed, copy = self.onward(way, stage)

                @pl.when(allowed)
                def _():
                    copy.wait_recv()
                    copy.start()

    def wait(self, block):
        away = block - self.at
        below, above = away < -1, away > 1
        done = (below & self.can(self.at + 1)) | (above & self.can(self.at - 1))

        @pl.when(jnp.logical_not(done))
        def _():
            src = self.whole.at[block]
            send(src, src, self.send_sem.at[0, 0], self.recv_sem.at[block], {"dp": block}).wait_recv()

    def finish(self):
        for way in (-1, 1):
            for hops in range(1, min(3, self.c)):
                allowed, copy = self.direct(way, hops)
                pl.when(allowed)(copy.wait_send)
            for stage in range(self.c - 3):
                allowed, copy = self.onward(way, stage)
                pl.when(allowed)(copy.wait_send)


class Gather:
    def __init__(self, own, place, halves, send_sem, recv_sem, me, n):
        self.own, self.place, self.halves = own, place, halves
        self.send_sem, self.recv_sem, self.me, self.n = send_sem, recv_sem, me, n
        self.direct = [k for k in order_of(n) if k % 2 == 0]
        self.relayed = n == 8
        self.near = [2, 4] if self.relayed else self.direct

    def to(self, src, dst, at, k):
        return send(
            src, dst, self.send_sem.at[at], self.recv_sem.at[at], {"ep": partner(self.me, k, self.n)}
        )

    def across(self, k):
        return self.to(self.own, self.place(self.me), k, k)

    def relay(self, k):
        half = self.halves(partner(self.me, k, self.n))[k // 4]
        return self.to(half, half, self.n + k // 4, 6 - k)

    def pass_on(self, k):
        block = self.place(partner(self.me, k, self.n))
        return self.to(block, block, k + 1, 1)

    def start(self):
        for k in self.near + [1]:
            self.across(k).start()

    def middle(self):
        for k in self.near:
            self.across(k).wait_recv()
            if self.relayed:
                self.relay(k).start()
            self.pass_on(k).start()

    def last(self):
        if self.relayed:
            for k in (2, 4):
                self.relay(k).wait_recv()
            self.pass_on(6).start()

    def finish(self):
        self.across(1).wait()
        for k in self.near:
            self.across(k).wait_send()
            if self.relayed:
                self.relay(k).wait_send()
        for k in self.direct:
            self.pass_on(k).wait()


class Spread:
    def __init__(self, r, name, me, grp, n, c, place, halves):
        self.send_buf, self.recv_buf, self.final, self.ss, self.rs, ys, yr, self.local = (
            getattr(r, name + part)
            for part in ("_send", "_recv", "_fin", "_ss", "_rs", "_ys", "_yr", "_ls")
        )
        self.me, self.grp, self.c, self.place = me, grp, c, place
        self.gather = Gather(
            place(me, None), lambda e: place(e, None), halves, ys, yr, me, n
        )

    def to_piece(self, t):
        target = lax.rem(self.grp + t, self.c)
        return send(
            self.send_buf.at[target],
            self.recv_buf.at[self.grp],
            self.ss.at[0, t],
            self.rs.at[0, t],
            {"dp": target},
        )

    def to_copies(self, t):
        return send(
            self.final,
            self.place(self.me, self.grp),
            self.ss.at[1, t],
            self.rs.at[1, t],
            {"dp": lax.rem(self.grp + t, self.c)},
        )

    def mine(self):
        return pltpu.make_async_copy(
            self.final, self.place(self.me, self.grp), self.local.at[0]
        )

    def scatter(self):
        for t in range(1, self.c):
            self.to_piece(t).start()
        self.recv_buf[self.grp] = self.send_buf[self.grp]

    def total(self):
        for t in range(1, self.c):
            self.to_piece(t).wait_recv()
        total = self.recv_buf[0].astype(F32)
        for s in range(1, self.c):
            total = total + self.recv_buf[s].astype(F32)
        self.final[...] = total.astype(BF)
        for t in range(1, self.c):
            self.to_copies(t).start()
        self.mine().start()

    def over(self):
        for t in range(1, self.c):
            self.to_copies(t).wait_recv()
        self.mine().wait()
        self.gather.start()

    def finish(self):
        self.gather.finish()
        for t in range(1, self.c):
            self.to_piece(t).wait_send()
            self.to_copies(t).wait_send()


def block_kernel(r, n, c):
    me, grp = lax.axis_index("ep"), lax.axis_index("dp")
    rows, width = r.tokens.shape
    own, cap = width // n, 2 * rows // n
    slots = n * cap
    hidden = r.w_in.shape[1]
    part = hidden // c
    order = order_of(n)
    direct = [k for k in order if k % 2 == 0]
    partners = {k: partner(me, k, n) for k in order}
    half = width // 2

    def to_partner(src, dst, send_sem, recv_sem, k):
        return send(src, dst, send_sem, recv_sem, {"ep": partners[k]})

    def blocks_out(buf, dst, sems, k):
        return to_partner(buf.at[partners[k]], dst.at[me], sems[0].at[k], sems[1].at[k], k)

    barrier = pltpu.get_barrier_semaphore()
    for k in order:
        pl.semaphore_signal(barrier, inc=1, device_id={"ep": partners[k]}, device_id_type=MESH)
    for t in range(1, c):
        pl.semaphore_signal(
            barrier, inc=1, device_id={"dp": lax.rem(grp + t, c)}, device_id_type=MESH
        )

    def load_qkv(slot):
        cols = pl.ds(0, 3 * width)
        return [
            pltpu.make_async_copy(
                r.w_qkv.at[pl.ds(0, half), :], r.act.at[:, cols], r.load_sem.at[slot]
            ),
            pltpu.make_async_copy(
                r.w_qkv.at[pl.ds(half, half), :], r.grad_pre.at[:, cols], r.load_sem.at[slot + 1]
            ),
        ]

    first_loads = load_qkv(0)
    load_o = pltpu.make_async_copy(r.w_o, r.w_o_v, r.load_sem.at[2])
    load_out = pltpu.make_async_copy(r.w_out.at[0], r.w_out_v, r.load_sem.at[3])
    load_in = pltpu.make_async_copy(r.w_in.at[0], r.w_in_v, r.load_sem.at[4])
    for load in first_loads + [load_o, load_out, load_in]:
        load.start()

    r.place[...] = place_matrix(r.ids[...], n, cap)
    for t in range(width // TILE):
        cols = slice(t * TILE, (t + 1) * TILE)
        r.g_send[:, :, cols] = (
            dot(r.place[...], r.cotangent[:, cols], NN).astype(BF).reshape(n, cap, TILE)
        )
    pl.semaphore_wait(barrier, n - 1 + c - 1)
    g_copies = [blocks_out(r.g_send, r.g_own, (r.g_ss, r.g_rs), k) for k in order]
    for copy in g_copies:
        copy.start()
    r.g_own[me] = r.g_send[me]

    norm_apply(r.tokens, r.gain_attn, r.shift_attn, r.normed)

    def to_heads(p, k):
        return to_partner(
            r.qkv_send.at[p, partners[k]],
            r.qkv_heads.at[p, me],
            r.a_ss.at[p, k],
            r.a_rs.at[p, k],
            k,
        )

    for load in first_loads:
        load.wait()
    for p in range(3):
        for t in range(width // TILE):
            cols = slice(p * width + t * TILE, p * width + (t + 1) * TILE)
            block = dot(r.normed[:, :half], r.act[:, cols], NN)
            block = (block + dot(r.normed[:, half:], r.grad_pre[:, cols], NN)).astype(BF)
            for e in range(TILE // own):
                r.qkv_send[p, t * (TILE // own) + e] = block[:, e * own : (e + 1) * own]
        for k in order:
            to_heads(p, k).start()
        r.qkv_heads[p, me] = r.qkv_send[p, me]

    g_line = Line(r.g_own, r.g_all, r.gz_ss, r.gz_rs, grp, c)
    x_line = Line(r.x_own, r.x_all, r.xz_ss, r.xz_rs, grp, c)
    for copy in g_copies:
        copy.wait()
    g_line.start()

    load_out.wait()

    for p in range(3):
        for k in order:
            to_heads(p, k).wait_recv()

    def normed_halves(e):
        return [
            r.normed_all.at[e, pl.ds(0, rows // 2), :],
            r.normed_all.at[e, pl.ds(rows // 2, rows // 2), :],
        ]

    normed_gather = Gather(
        r.normed, lambda e: r.normed_all.at[e], normed_halves, r.n_ss, r.n_rs, me, n
    )
    mine = pltpu.make_async_copy(r.normed, r.normed_all.at[me], r.load_sem.at[5])
    mine.start()

    for i in range(n):
        r.values_t[i] = r.qkv_heads[2, i].astype(F32).T.astype(BF)

    def home(t):
        target = lax.rem(me + t, n)
        return send(
            r.att_heads.at[target],
            r.att_recv.at[me],
            r.o_ss.at[t],
            r.o_rs.at[t],
            {"ep": target},
        )

    def block_step(t, _):
        at = lax.rem(me + t, n)
        if n > UNROLLED:
            attend_block_loop(r, at)
        else:
            lax.switch(at, [functools.partial(attend_block, r, i) for i in range(n)])

        @pl.when(t > 0)
        def _():
            home(t).start()

        return 0

    lax.fori_loop(0, n, block_step, 0)
    r.att_recv[me] = r.att_heads[me]

    for t in range(1, n):
        home(t).wait_recv()
    for e in range(n):
        r.attended[:, e * own : (e + 1) * own] = r.att_recv[e]

    load_o.wait()
    for t in range(width // TILE):
        cols = slice(t * TILE, (t + 1) * TILE)
        r.hidden[:, cols] = r.tokens[:, cols].astype(F32) + dot(
            r.attended[...], r.w_o_v[:, cols], NN
        )
    norm_apply(r.hidden, r.gain_ffn, r.shift_ffn, r.block_out)
    for t in range(width // TILE):
        cols = slice(t * TILE, (t + 1) * TILE)
        r.x_send[:, :, cols] = (
            dot(r.place[...], r.block_out[:, cols], NN).astype(BF).reshape(n, cap, TILE)
        )
    x_copies = [blocks_out(r.x_send, r.x_own, (r.x_ss, r.x_rs), k) for k in order]
    for copy in x_copies:
        copy.start()
    r.x_own[me] = r.x_send[me]

    def act_grad(cols):
        r.grad_pre[:, cols] = dot(flat(r.g_own[...]), r.w_out_v[cols, :], NT).astype(BF)

    tiles(hidden, act_grad)
    g_line.hand_on()
    load_in.wait()

    for copy in x_copies:
        copy.wait()
    x_line.start()
    normed_gather.start()

    def expert_step(cols):
        pre = dot(flat(r.x_own[...]), r.w_in_v[cols, :], NT)
        for q in range(slots // CHUNK):
            at = slice(q * CHUNK, (q + 1) * CHUNK)
            act, slope = gelu_both(pre[at])
            r.act[at, cols] = act.astype(BF)
            r.grad_pre[at, cols] = (r.grad_pre[at, cols].astype(F32) * slope).astype(BF)

    tiles(hidden, expert_step)

    def routed_grad(cols):
        r.g_send[:, :, cols] = (
            dot(r.grad_pre[...], r.w_in_v[:, cols], NN).astype(BF).reshape(n, cap, TILE)
        )

    tiles(width, routed_grad)
    r_copies = [blocks_out(r.g_send, r.r_recv, (r.r_ss, r.r_rs), k) for k in order]
    for copy in r_copies:
        copy.start()
    r.r_recv[me] = r.g_send[me]

    def produce(cols):
        r.x_send[:, :, cols] = (
            dot(r.act[...], r.w_out_v[:, cols], NN).astype(BF).reshape(n, cap, TILE)
        )

    tiles(width, produce)
    r.p_recv[me] = r.x_send[me]
    mine_at = pl.multiple_of(grp * part, part)

    def weight_terms(act_at, x_rows, g_rows, first):
        def one(out):
            from_act = pl.ds(pl.multiple_of(act_at + out.start, TILE), TILE)

            def two(cols):
                term_in = dot(r.grad_pre[:, from_act], x_rows(cols), TN)
                r.sum_in[out, cols] = term_in if first else r.sum_in[out, cols] + term_in
                term_out = dot(r.act[:, from_act], g_rows(cols), TN)
                r.sum_out[out, cols] = term_out if first else r.sum_out[out, cols] + term_out

            tiles(width, two)

        tiles(part, one)

    weight_terms(
        mine_at,
        lambda cols: flat(r.x_own[:, :, cols]),
        lambda cols: flat(r.g_own[:, :, cols]),
        True,
    )

    for copy in r_copies:
        copy.wait()

    normed_gather.middle()

    for t in range(width // TILE):
        cols = slice(t * TILE, (t + 1) * TILE)
        r.grad_tokens[:, cols] = dot(r.place[...], flat(r.r_recv[:, :, cols]), TN)

    def store_hidden(at, grad_in):
        grad_hidden = r.cotangent[at, :].astype(F32) + grad_in
        r.grad_tokens[at, :] = grad_hidden
        r.block_out[at, :] = grad_hidden.astype(BF)

    sums = norm_back(r.hidden, r.grad_tokens, r.gain_ffn, store_hidden)
    r.small_own[2:3], r.small_own[3:4] = sums
    r.small_own[4:SMALL] = jnp.zeros((SMALL - 4, width), F32)
    for t in range(width // TILE):
        block = dot(r.block_out[...], r.w_o_v[t * TILE : (t + 1) * TILE, :], NT).astype(BF)
        for e in range(TILE // own):
            r.att_recv[t * (TILE // own) + e] = block[:, e * own : (e + 1) * own]
    a_copies = [blocks_out(r.att_recv, r.grad_att, (r.b_ss, r.b_rs), k) for k in order]
    for copy in a_copies:
        copy.start()
    r.grad_att[me] = r.att_recv[me]

    def wo_rows(buf, e):
        at = e * own
        return buf.at[
            pl.ds(pl.multiple_of(lax.rem(at, slots), own), own),
            pl.ds(pl.multiple_of(lax.div(at, slots) * width, width), width),
        ]

    for t in range(width // slots):
        out = slice(t * slots, (t + 1) * slots)
        r.act[:, t * width : (t + 1) * width] = dot(
            r.attended[:, out], r.block_out[...], TN
        ).astype(BF)

    def to_owner(k):
        return to_partner(
            wo_rows(r.act, partners[k]), wo_rows(r.grad_pre, me), r.w_ss.at[k], r.w_rs.at[k], k
        )

    for copy in a_copies:
        copy.wait()
    p_copies = [blocks_out(r.x_send, r.p_recv, (r.p_ss, r.p_rs), k) for k in order]
    for copy in p_copies:
        copy.start()
    for k in order:
        to_owner(k).start()
    wo_rows(r.grad_pre, me)[...] = wo_rows(r.act, me)[...]

    for p in range(3):
        for k in order:
            to_heads(p, k).wait_send()
    for t in range(1, n):
        home(t).wait_send()
    for i in range(n):
        both = (r.grad_att[i].astype(F32) * r.att_heads[i].astype(F32)).T
        size = own // r.heads
        deltas = [
            jnp.sum(both[h * size : (h + 1) * size], axis=0, keepdims=True) for h in range(r.heads)
        ]
        r.delta[i] = jnp.concatenate(
            deltas + [jnp.zeros((SMALL - r.heads, rows), F32)], axis=0
        )
    r.grad_q_t[...] = jnp.zeros(r.grad_q_t.shape, F32)

    def back_home(p, t):
        target = lax.rem(me + t, n)
        return send(
            r.qkv_send.at[p, target],
            r.grad_tok.at[p, me],
            r.d_ss.at[p, t],
            r.d_rs.at[p, t],
            {"ep": target},
        )

    def back_step(t, _):
        attend_back(r, lax.rem(me + t, n), n)

        @pl.when(t > 0)
        def _():
            for p in (1, 2):
                back_home(p, t).start()

        return 0

    lax.fori_loop(0, n, back_step, 0)
    for i in range(n):
        r.qkv_send[0, i] = (r.grad_q_t[i].T * ((own // r.heads) ** -0.5)).astype(BF)
    for t in range(1, n):
        back_home(0, t).start()
    for p in range(3):
        r.grad_tok[p, me] = r.qkv_send[p, me]
    normed_gather.last()

    def o_place(e, d):
        at = pl.ds(pl.multiple_of(e * own, own), own)
        piece = width // c
        if d is None:
            return r.o_all.at[at, :]
        return r.o_all.at[at, pl.ds(pl.multiple_of(d * piece, piece), piece)]

    def o_halves(e):
        at = pl.ds(pl.multiple_of(e * own, own), own)
        return [r.o_all.at[at, pl.ds(0, half)], r.o_all.at[at, pl.ds(half, half)]]

    def q_place(first, e, d):
        piece = TILE // c
        if d is None:
            return r.q_all.at[:, e, pl.ds(first, TILE), :]
        return r.q_all.at[:, e, pl.ds(pl.multiple_of(first + d * piece, piece), piece), :]

    def q_halves(first, e):
        return [
            r.q_all.at[:, e, pl.ds(first, TILE // 2), :],
            r.q_all.at[:, e, pl.ds(first + TILE // 2, TILE // 2), :],
        ]

    o_spread = Spread(r, "wo", me, grp, n, c, o_place, o_halves)
    q_spreads = [
        Spread(
            r,
            "wq" + str(t),
            me,
            grp,
            n,
            c,
            functools.partial(q_place, t * TILE),
            functools.partial(q_halves, t * TILE),
        )
        for t in range(width // TILE)
    ]

    normed_gather.finish()
    mine.wait()
    at_once = width // rows
    turns = n // at_once

    def normed_loads(t):
        out = []
        for b in range(turns):
            spot = (t if turns <= 2 else b // 2) * TILE
            for s in range(at_once):
                out.append(
                    pltpu.make_async_copy(
                        r.normed_all.at[b * at_once + s, :, pl.ds(t * TILE, TILE)],
                        r.space.at[
                            pl.ds((b % 2) * width + s * rows, rows), pl.ds(spot, TILE)
                        ],
                        r.slab_sem.at[t % 2, b * at_once + s],
                    )
                )
        return out

    for t in range(width // TILE if turns <= 2 else 1):
        for load in normed_loads(t):
            load.start()
    for t, spread in enumerate(q_spreads):
        if turns > 2 and t:
            for load in normed_loads(t):
                load.start()
        for load in normed_loads(t):
            load.wait()
        total = None
        for b in range(turns):
            spot = (t if turns <= 2 else b // 2) * TILE
            grads = jnp.concatenate(
                [flat(r.qkv_send[p, b * at_once : (b + 1) * at_once]) for p in range(3)], axis=1
            )
            term = dot(
                r.space[(b % 2) * width : (b % 2 + 1) * width, spot : spot + TILE], grads, TN
            )
            total = term if b == 0 else total + term
        low = total.astype(BF)
        piece = TILE // c
        for d in range(c):
            for p in range(3):
                spread.send_buf[d, p] = low[
                    d * piece : (d + 1) * piece, p * own : (p + 1) * own
                ]
        spread.scatter()

    for copy in p_copies:
        copy.wait()
    for t in range(width // TILE):
        cols = slice(t * TILE, (t + 1) * TILE)
        r.block_out[:, cols] = (
            r.hidden[:, cols] + dot(r.place[...], flat(r.p_recv[:, :, cols]), TN)
        ).astype(BF)


    def slab_loads(q):
        at = partner(grp, q, c)
        base = (q % 2) * width
        out = []
        for which, src in enumerate((r.x_all, r.g_all)):
            for s in range(n):
                out.append(
                    pltpu.make_async_copy(
                        src.at[at, s],
                        r.space.at[pl.ds(base + which * slots + s * cap, cap), :],
                        r.slab_sem.at[q % 2, which * n + s],
                    )
                )
        return out

    def slab_start(q):
        g_line.wait(partner(grp, q, c))
        x_line.wait(partner(grp, q, c))
        for load in slab_loads(q):
            load.start()

    def slab(q):
        base = (q % 2) * width
        for load in slab_loads(q):
            load.wait()
        x_rows, g_rows = r.space.at[pl.ds(base, slots), :], r.space.at[pl.ds(base + slots, slots), :]

        def activate(out):
            at = pl.ds(pl.multiple_of(mine_at + out.start, TILE), TILE)
            cols = pl.ds(pl.multiple_of(3 * width + out.start, TILE), TILE)
            r.grad_pre[:, cols] = dot(g_rows[...], r.w_out_v[at, :], NT).astype(BF)
            pre = dot(x_rows[...], r.w_in_v[at, :], NT)
            for q in range(slots // CHUNK):
                some = slice(q * CHUNK, (q + 1) * CHUNK)
                act, slope = gelu_both(pre[some])
                r.act[some, cols] = act.astype(BF)
                r.grad_pre[some, cols] = (r.grad_pre[some, cols].astype(F32) * slope).astype(BF)

        tiles(part, activate)
        weight_terms(
            3 * width, lambda cols: x_rows[:, cols], lambda cols: g_rows[:, cols], False
        )

    slab_start(1)

    slab(1)

    q_spreads[0].total()

    for k in order:
        to_owner(k).wait()
    total = wo_rows(r.grad_pre, 0)[...].astype(F32)
    for e in range(1, n):
        total = total + wo_rows(r.grad_pre, e)[...].astype(F32)
    for d in range(c):
        r.wo_send[d] = total[:, d * (width // c) : (d + 1) * (width // c)].astype(BF)
    o_spread.scatter()
    last_loads = load_qkv(0)
    for load in last_loads:
        load.start()

    for spread in q_spreads[1:]:
        spread.total()
    x_line.hand_on()

    for p in (1, 2, 0):
        for t in range(1, n):
            back_home(p, t).wait_recv()
    for load in last_loads:
        load.wait()

    for p in range(3):
        for e in range(n):
            r.attended[:, e * own : (e + 1) * own] = r.grad_tok[p, e]
        cols = slice(p * width, (p + 1) * width)
        for at, weight in enumerate((r.act, r.grad_pre)):
            out = slice(at * half, (at + 1) * half)
            term = dot(r.attended[...], weight[:, cols], NT)
            r.hidden[:, out] = term if p == 0 else r.hidden[:, out] + term

    def store_tokens(at, grad_in):
        r.grad_tokens[at, :] += grad_in

    sums = norm_back(r.tokens, r.hidden, r.gain_attn, store_tokens)
    r.small_own[0:1], r.small_own[1:2] = sums

    def small_ep(k):
        return to_partner(r.small_own, r.small_ep.at[me], r.s_ss.at[0, k], r.s_rs.at[0, k], k)

    def small_dp(t):
        return send(
            r.small_sum,
            r.small_dp.at[grp],
            r.s_ss.at[1, t],
            r.s_rs.at[1, t],
            {"dp": lax.rem(grp + t, c)},
        )

    for k in order:
        small_ep(k).start()
    r.small_ep[me] = r.small_own[...]

    q_spreads[0].over()

    o_spread.total()
    if c > 2:
        slab_start(2)
        slab(2)

    for spread in q_spreads[1:]:
        spread.over()
    q_spreads[0].gather.middle()
    o_spread.over()

    for q in range(3, c):
        slab_start(q)

        slab(q)

    out_copies = []
    for at, (src, dst) in enumerate(((r.sum_in, r.grad_in), (r.sum_out, r.grad_out))):
        base = at * width
        for s in range(0, part, CHUNK * 4):
            r.space[base + s : base + s + CHUNK * 4, :] = src[s : s + CHUNK * 4, :].astype(BF)
        out_copies.append(
            pltpu.make_async_copy(
                r.space.at[pl.ds(base, part), :], dst, r.load_sem.at[at]
            )
        )
    for copy in out_copies:
        copy.start()

    for k in order:
        small_ep(k).wait()
    total = r.small_ep[0]
    for e in range(1, n):
        total = total + r.small_ep[e]
    r.small_sum[...] = total
    for t in range(1, c):
        small_dp(t).start()
    r.small_dp[grp] = total

    spreads = q_spreads + [o_spread]
    for spread in spreads[1:]:
        spread.gather.middle()
    for spread in spreads:
        spread.gather.last()

    for t in range(1, c):
        small_dp(t).wait()
    total = r.small_dp[0]
    for d in range(1, c):
        total = total + r.small_dp[d]
    r.small[...] = total
    g_line.finish()
    x_line.finish()
    for copy in out_copies:
        copy.wait()
    for spread in spreads:
        spread.finish()
    for p in range(3):
        for t in range(1, n):
            back_home(p, t).wait_send()


def block_call(n, c, heads, operands):
    rows, width = operands["tokens"].shape
    hidden = operands["w_in"].shape[1]
    own, cap, part, piece = width // n, 2 * rows // n, hidden // c, width // c
    slots = n * cap
    vm, hb = pl.BlockSpec(memory_space=pltpu.VMEM), pl.BlockSpec(memory_space=pl.ANY)
    sm = pl.BlockSpec(memory_space=pltpu.SMEM)
    inputs = dict(
        lengths=sm, ids=vm, tokens=vm, cotangent=vm, gain_attn=vm, shift_attn=vm, gain_ffn=vm,
        shift_ffn=vm, w_qkv=hb, w_o=hb, w_in=hb, w_out=hb,
    )
    outputs = dict(
        block_out=((rows, width), BF, vm),
        grad_tokens=((rows, width), F32, vm),
        q_all=((3, n, width, own), BF, hb),
        o_all=((width, width), BF, hb),
        small=((SMALL, width), F32, vm),
        grad_in=((part, width), BF, hb),
        grad_out=((part, width), BF, hb),
        g_all=((c, n, cap, width), BF, hb),
        x_all=((c, n, cap, width), BF, hb),
        normed_all=((n, rows, width), BF, hb),
    )

    def v(*shape):
        return pltpu.VMEM(shape, BF)

    def f(*shape):
        return pltpu.VMEM(shape, F32)

    def d(*shape):
        return pltpu.SemaphoreType.DMA(shape)

    heads_shape = (n, rows, own)
    scratch = dict(
        sum_in=f(part, width), sum_out=f(part, width),
        w_o_v=v(width, width), w_in_v=v(hidden, width), w_out_v=v(hidden, width),
        act=v(slots, hidden), grad_pre=v(slots, hidden), space=v(2 * width, width),
        normed=v(rows, width), place=v(slots, rows), hidden=f(rows, width),
        attended=v(rows, width),
        qkv_send=v(3, *heads_shape), qkv_heads=v(3, *heads_shape), grad_tok=v(3, *heads_shape),
        values_t=v(n, own, rows), att_heads=v(*heads_shape), att_recv=v(*heads_shape),
        grad_att=v(*heads_shape), grad_q_t=f(n, own, rows),
        lse=f(n, SMALL, rows), delta=f(n, SMALL, rows),
        g_send=v(n, cap, width), x_send=v(n, cap, width), g_own=v(n, cap, width),
        x_own=v(n, cap, width), r_recv=v(n, cap, width), p_recv=v(n, cap, width),
        wo_send=v(c, own, piece), wo_recv=v(c, own, piece), wo_fin=v(own, piece),
        small_own=f(SMALL, width), small_ep=f(n, SMALL, width), small_sum=f(SMALL, width),
        small_dp=f(c, SMALL, width),
        load_sem=d(8), slab_sem=d(2, 2 * n),
        a_ss=d(3, n), a_rs=d(3, n), g_ss=d(n), g_rs=d(n), n_ss=d(n + 2), n_rs=d(n + 2),
        o_ss=d(n), o_rs=d(n), x_ss=d(n), x_rs=d(n), r_ss=d(n), r_rs=d(n), p_ss=d(n), p_rs=d(n),
        b_ss=d(n), b_rs=d(n), w_ss=d(n), w_rs=d(n), d_ss=d(3, n), d_rs=d(3, n),
        gz_ss=d(2, c), gz_rs=d(c), xz_ss=d(2, c), xz_rs=d(c),
        wo_ss=d(2, c), wo_rs=d(2, c), wo_ys=d(n + 2), wo_yr=d(n + 2), wo_ls=d(1),
        s_ss=d(2, max(n, c)), s_rs=d(2, max(n, c)),
    )
    for t in range(width // TILE):
        name = "wq" + str(t)
        piece = TILE // c
        scratch[name + "_send"] = scratch[name + "_recv"] = v(c, 3, piece, own)
        scratch[name + "_fin"] = v(3, piece, own)
        scratch[name + "_ss"] = scratch[name + "_rs"] = d(2, c)
        scratch[name + "_ys"] = scratch[name + "_yr"] = d(n + 2)
        scratch[name + "_ls"] = d(1)
    names = list(inputs) + list(outputs) + list(scratch)

    def kernel(*refs):
        r = types.SimpleNamespace(**dict(zip(names, refs)))
        r.heads = heads
        block_kernel(r, n, c)

    result = pl.pallas_call(
        kernel,
        out_shape=[jax.ShapeDtypeStruct(shape, kind) for shape, kind, _ in outputs.values()],
        in_specs=list(inputs.values()),
        out_specs=[spec for _, _, spec in outputs.values()],
        scratch_shapes=list(scratch.values()),
        compiler_params=pltpu.CompilerParams(
            collective_id=0, has_side_effects=True, vmem_limit_bytes=VMEM_LIMIT
        ),
    )(*[operands[name] for name in inputs])
    return dict(zip(outputs, result))


VMEM_LIMIT = 64 << 20
STEPS = 8


def widen_kernel(q_all, o_all, grad_in, grad_out, block, tokens, small, *outs):
    q_out, o_out, in_out, out_out, block_out, tokens_out = outs[:6]
    _, n, _, own = q_all.shape
    for p in range(3):
        for e in range(n):
            at = (p * n + e) * own
            q_out[:, at : at + own] = q_all[p, e].astype(F32)
    o_out[...] = o_all[...].astype(F32)
    in_out[0] = grad_in[...].astype(F32)
    out_out[0] = grad_out[...].astype(F32)
    block_out[...] = block[...]
    tokens_out[...] = tokens[...]
    for at, one in enumerate(outs[6:]):
        one[...] = small[at : at + 1, :]


def widen(out):
    q_all, o_all, grad_in, block = out["q_all"], out["o_all"], out["grad_in"], out["block_out"]
    _, n, width, own = q_all.shape
    part, rows = grad_in.shape[0], block.shape[0]
    S = jax.ShapeDtypeStruct

    def rowwise(count):
        return pl.BlockSpec((count // STEPS, width), lambda i: (i, 0))

    expert = pl.BlockSpec((1, part // STEPS, width), lambda i: (0, i, 0))
    fixed = pl.BlockSpec((1, width), lambda i: (0, 0))
    return pl.pallas_call(
        widen_kernel,
        grid=(STEPS,),
        out_shape=[
            S((width, 3 * width), F32), S((width, width), F32), S((1, part, width), F32),
            S((1, part, width), F32), S((rows, width), BF), S((rows, width), F32),
        ] + [S((1, width), F32)] * 4,
        in_specs=[
            pl.BlockSpec((3, n, width // STEPS, own), lambda i: (0, 0, i, 0)),
            rowwise(width), rowwise(part), rowwise(part), rowwise(rows), rowwise(rows),
            pl.BlockSpec((SMALL, width), lambda i: (0, 0)),
        ],
        out_specs=[
            pl.BlockSpec((width // STEPS, 3 * width), lambda i: (i, 0)),
            rowwise(width), expert, expert, rowwise(rows), rowwise(rows),
        ] + [fixed] * 4,
        compiler_params=pltpu.CompilerParams(vmem_limit_bytes=VMEM_LIMIT),
    )(q_all, o_all, grad_in, out["grad_out"], block, out["grad_tokens"], out["small"])


def on_device(
    tokens,
    gain_attn,
    shift_attn,
    w_qkv,
    w_o,
    gain_ffn,
    shift_ffn,
    w_in,
    w_out,
    seq_lengths,
    expert_ids,
    cotangent,
):
    rows, width = tokens.shape
    n, c = lax.axis_size("ep"), lax.axis_size("dp")
    operands = dict(
        lengths=seq_lengths,
        ids=expert_ids.reshape(1, rows),
        tokens=tokens,
        cotangent=cotangent,
        gain_attn=gain_attn[None],
        shift_attn=shift_attn[None],
        gain_ffn=gain_ffn[None],
        shift_ffn=shift_ffn[None],
        w_qkv=w_qkv,
        w_o=w_o,
        w_in=w_in,
        w_out=w_out,
    )
    out = block_call(n, c, HEADS // n, operands)
    q_out, o_out, in_out, out_out, block, tokens_out, *small = widen(out)
    small = [one.reshape(width) for one in small]
    return (block, tokens_out, q_out, o_out, *small, in_out, out_out)


def solution(mesh):
    return jax.shard_map(
        on_device,
        mesh=mesh,
        in_specs=(
            P(("dp", "ep"), None),
            P(),
            P(),
            P(),
            P(),
            P(),
            P(),
            P("ep", None, None),
            P("ep", None, None),
            P("dp", None),
            P(("dp", "ep"), None),
            P(("dp", "ep"), None),
        ),
        out_specs=(
            P(("dp", "ep"), None),
            P(("dp", "ep"), None),
            P(),
            P(),
            P(),
            P(),
            P(),
            P(),
            P("ep", "dp", None),
            P("ep", "dp", None),
        ),
        check_vma=False,
    )
```

```python
import functools
import types

import jax
import jax.numpy as jnp
from jax import lax
from jax.experimental import pallas as pl
from jax.experimental.pallas import tpu as pltpu
from jax.sharding import PartitionSpec as P

HEADS = 16
EPSILON = 1e-05
MASKED = -1e30
TILE = 512
SMALL = 8
UNROLLED = 8
AT_ONCE = 4
MESH = pl.DeviceIdType.MESH
F32 = jnp.float32
BF = jnp.bfloat16
NN = (((1,), (0,)), ((), ()))
NT = (((1,), (1,)), ((), ()))
TN = (((0,), (0,)), ((), ()))


def dot(left, right, dims):
    return lax.dot_general(left, right, dims, preferred_element_type=F32)


def partner(me, k, n):
    out, weight = 0, 1
    while weight < n:
        bit = lax.rem(lax.div(me, weight), 2)
        out = out + (lax.rem(bit + 1, 2) if k & weight else bit) * weight
        weight *= 2
    return out


def send(src, dst, send_sem, recv_sem, target):
    return pltpu.make_async_remote_copy(
        src_ref=src,
        dst_ref=dst,
        send_sem=send_sem,
        recv_sem=recv_sem,
        device_id=target,
        device_id_type=MESH,
    )


def order_of(n):
    return sorted(range(1, n), key=lambda k: (-bin(k // 2).count("1"), k))


def flat(value):
    return value.reshape(value.shape[0] * value.shape[1], value.shape[2])


def tiles(count, body, beside=None):
    def step(t, _):
        body(pl.ds(pl.multiple_of(t * TILE, TILE), TILE))
        for at, act in (beside or {}).items():
            pl.when(t == at)(act)
        return 0

    lax.fori_loop(0, count // TILE, step, 0)


def norm_rows(rows_in):
    average = jnp.mean(rows_in, axis=-1, keepdims=True)
    centered = rows_in - average
    inv_std = lax.rsqrt(jnp.mean(centered * centered, axis=-1, keepdims=True) + EPSILON)
    return centered * inv_std, inv_std


CHUNK = 32


def by_rows(count, body, carry=0):
    def step(i, state):
        return body(pl.ds(pl.multiple_of(i * CHUNK, CHUNK), CHUNK), state)

    return lax.fori_loop(0, count // CHUNK, step, carry)


def norm_apply(src, gain, shift, dst):
    def body(at, _):
        unit, _ = norm_rows(src[at, :].astype(F32))
        dst[at, :] = (unit * gain[...] + shift[...]).astype(BF)
        return 0

    by_rows(src.shape[0], body)


def norm_back(src, grad, gain, store):
    def body(at, sums):
        unit, inv = norm_rows(src[at, :].astype(F32))
        incoming = grad[at, :]
        grad_unit = incoming * gain[...]
        grad_in = inv * (
            grad_unit
            - jnp.mean(grad_unit, axis=-1, keepdims=True)
            - unit * jnp.mean(grad_unit * unit, axis=-1, keepdims=True)
        )
        store(at, grad_in)
        return (
            sums[0] + jnp.sum(incoming * unit, axis=0, keepdims=True),
            sums[1] + jnp.sum(incoming, axis=0, keepdims=True),
        )

    zero = jnp.zeros((1, src.shape[1]), F32)
    return by_rows(src.shape[0], body, (zero, zero))


def gelu_both(pre):
    square = pre * pre
    bent = jnp.tanh(0.7978845608028654 * pre * (1.0 + 0.044715 * square))
    half = 0.5 + 0.5 * bent
    rise = 0.7978845608028654 * (1.0 + 3 * 0.044715 * square)
    return pre * half, half + 0.5 * pre * (1.0 - bent * bent) * rise


def place_matrix(ids_row, n, cap):
    rows = ids_row.shape[1]
    expert = lax.broadcasted_iota(jnp.int32, (n, rows), 0)
    hit = (expert == ids_row).astype(F32)
    before = lax.broadcasted_iota(jnp.int32, (rows, rows), 0)
    after = lax.broadcasted_iota(jnp.int32, (rows, rows), 1)
    upto = (before <= after).astype(F32).astype(BF)
    count = dot(hit.astype(BF), upto, NN)
    slot = jnp.sum(hit * (count - 1.0), axis=0, keepdims=True)
    target = ids_row * cap + slot.astype(jnp.int32)
    places = lax.broadcasted_iota(jnp.int32, (n * cap, rows), 0)
    return (places == target).astype(F32).astype(BF)


def start_row(len_ref, first, width):
    pos = first + lax.broadcasted_iota(jnp.int32, (1, width), 1)
    start = jnp.zeros((1, width), jnp.int32)
    edge = jnp.int32(0)
    for s in range(len_ref.shape[1] - 1):
        edge = edge + len_ref[0, s]
        start = jnp.where(pos >= edge, edge, start)
    return pos, start


def split_heads(block, heads):
    if heads == 1:
        return [block]
    size = block.shape[1] // heads
    lane = lax.broadcasted_iota(jnp.int32, block.shape, 1)
    zero = jnp.zeros_like(block)
    return [
        jnp.where((lane >= h * size) & (lane < (h + 1) * size), block, zero) for h in range(heads)
    ]


def attend_block(r, i):
    rows, own = r.qkv_heads.shape[2:]
    heads = r.heads
    size = own // heads
    queries = split_heads(r.qkv_heads[0, i] * BF(size**-0.5), heads)
    pos, start = start_row(r.lengths, i * rows, rows)
    outs, sums = [], []
    for h in range(heads):
        top = jnp.full((1, rows), MASKED, F32)
        total = jnp.zeros((1, rows), F32)
        accum = jnp.zeros((size, rows), F32)
        for last in range(i, -1, -AT_ONCE):
            scores = []
            blocks = range(last, max(last - AT_ONCE, -1), -1)
            for j in blocks:
                key = j * rows + lax.broadcasted_iota(jnp.int32, (rows, rows), 0)
                allowed = key >= start
                if j == i:
                    allowed = allowed & (key <= pos)
                scores.append(
                    jnp.where(allowed, dot(r.qkv_heads[1, j], queries[h], NT), MASKED)
                )
            peak = functools.reduce(
                jnp.maximum, [jnp.max(s.reshape(rows // 8, 8, rows), axis=0) for s in scores]
            )
            new_top = jnp.maximum(top, jnp.max(peak, axis=0, keepdims=True))
            decay = jnp.exp(top - new_top)
            accum = accum * decay
            part = jnp.zeros((8, rows), F32)
            for j, s in zip(blocks, scores):
                weights = jnp.exp(s - new_top)
                part = part + jnp.sum(weights.reshape(rows // 8, 8, rows), axis=0)
                values = r.values_t[j, h * size : (h + 1) * size, :]
                accum = accum + dot(values, weights.astype(BF), NN)
            total = total * decay + jnp.sum(part, axis=0, keepdims=True)
            top = new_top
        outs.append(accum / total)
        sums.append(top + jnp.log(total))
    r.att_heads[i] = jnp.concatenate(outs, axis=0).T.astype(BF)
    r.lse[i] = jnp.concatenate(sums + [jnp.zeros((SMALL - heads, rows), F32)], axis=0)


def attend_back(r, j, n):
    rows, own = r.qkv_heads.shape[2:]
    heads = r.heads
    size = own // heads
    keys, values = r.qkv_heads[1, j], r.qkv_heads[2, j]
    keys_t = keys.astype(F32).T.astype(BF)

    def fold(at, carry, diagonal):
        grad_k, grad_v = carry
        for i in at:
            queries = split_heads(r.qkv_heads[0, i] * BF(size**-0.5), heads)
            grads = split_heads(r.grad_att[i], heads)
            pos, start = start_row(r.lengths, i * rows, rows)
            key = j * rows + lax.broadcasted_iota(jnp.int32, (rows, rows), 0)
            allowed = key >= start
            if diagonal:
                allowed = allowed & (key <= pos)
            for h in range(heads):
                scores = dot(keys, queries[h], NT)
                probs = jnp.where(allowed, jnp.exp(scores - r.lse[i, h : h + 1, :]), 0.0)
                grad_probs = dot(values, grads[h], NT)
                grad_scores = (probs * (grad_probs - r.delta[i, h : h + 1, :])).astype(BF)
                grad_v = grad_v + dot(probs.astype(BF), grads[h], NN)
                grad_k = grad_k + dot(grad_scores, queries[h], NN)
                part = slice(h * size, (h + 1) * size)
                r.grad_q_t[i, part, :] += dot(keys_t[part, :], grad_scores, NN)
        return grad_k, grad_v

    zero = jnp.zeros((rows, own), F32)
    carry = fold([j], (zero, zero), True)
    left = n - 1 - j
    odd = lax.rem(left, 2)
    carry = lax.fori_loop(j + 1, j + 1 + odd, lambda i, carry: fold([i], carry, False), carry)

    def pair(t, carry):
        i = j + 1 + odd + 2 * t
        return fold([i, i + 1], carry, False)

    grad_k, grad_v = lax.fori_loop(0, lax.div(left, 2), pair, carry)
    r.qkv_send[1, j] = grad_k.astype(BF)
    r.qkv_send[2, j] = grad_v.astype(BF)


def attend_block_loop(r, i):
    rows, own = r.qkv_heads.shape[2:]
    heads = r.heads
    size = own // heads
    queries = split_heads(r.qkv_heads[0, i] * BF(size**-0.5), heads)
    pos, start = start_row(r.lengths, i * rows, rows)

    def fold(j, carry, diagonal):
        keys = r.qkv_heads[1, j]
        key = j * rows + lax.broadcasted_iota(jnp.int32, (rows, rows), 0)
        allowed = key >= start
        if diagonal:
            allowed = allowed & (key <= pos)
        out = []
        for h in range(heads):
            top, total, accum = carry[h]
            scores = jnp.where(allowed, dot(keys, queries[h], NT), MASKED)
            new_top = jnp.maximum(top, jnp.max(scores, axis=0, keepdims=True))
            weights = jnp.exp(scores - new_top)
            if diagonal:
                weights = jnp.where(allowed, weights, 0.0)
            decay = jnp.exp(top - new_top)
            total = total * decay + jnp.sum(weights, axis=0, keepdims=True)
            values = r.values_t[j, h * size : (h + 1) * size, :]
            accum = accum * decay + dot(values, weights.astype(BF), NN)
            out.append((new_top, total, accum))
        return tuple(out)

    state = tuple(
        (
            jnp.full((1, rows), MASKED, F32),
            jnp.zeros((1, rows), F32),
            jnp.zeros((size, rows), F32),
        )
        for _ in range(heads)
    )
    state = fold(i, state, True)
    state = lax.fori_loop(0, i, lambda j, carry: fold(j, carry, False), state)
    result = jnp.concatenate([accum / total for _, total, accum in state], axis=0)
    r.att_heads[i] = result.T.astype(BF)
    sums = [top + jnp.log(total) for top, total, _ in state]
    r.lse[i] = jnp.concatenate(sums + [jnp.zeros((SMALL - heads, rows), F32)], axis=0)


class Line:
    def __init__(self, block, whole, send_sem, recv_sem, at, c, hops):
        self.block, self.whole, self.at, self.c = block, whole, at, c
        self.send_sem, self.recv_sem, self.hops = send_sem, recv_sem, min(hops, c - 1)

    def can(self, index):
        return (index >= 0) & (index < self.c)

    def first(self, way, hops):
        target = self.at + way * hops
        return self.can(target), send(
            self.block,
            self.whole.at[self.at],
            self.send_sem.at[(way + 1) // 2, hops - 1],
            self.recv_sem.at[self.at],
            {"dp": target},
        )

    def onward(self, way, stage):
        held, target = self.at - way * (self.hops - 1 + stage), self.at + way
        src = self.whole.at[held]
        return self.can(held) & self.can(target), send(
            src,
            src,
            self.send_sem.at[(way + 1) // 2, self.hops - 1 + stage],
            self.recv_sem.at[held],
            {"dp": target},
        )

    def start(self):
        for hops in range(1, self.hops + 1):
            for way in (-1, 1):
                allowed, copy = self.first(way, hops)
                pl.when(allowed)(copy.start)

    def hand_on(self, *stages):
        for stage in stages:
            if stage < self.c - self.hops:
                for way in (-1, 1):
                    allowed, copy = self.onward(way, stage)

                    @pl.when(allowed)
                    def _():
                        copy.wait_recv()
                        copy.start()

    def wait(self, block):
        done = ((block <= self.at - self.hops) & self.can(self.at + 1)) | (
            (block >= self.at + self.hops) & self.can(self.at - 1)
        )

        @pl.when(jnp.logical_not(done))
        def _():
            src = self.whole.at[block]
            send(src, src, self.send_sem.at[0, 0], self.recv_sem.at[block], {"dp": block}).wait_recv()

    def finish(self):
        for way in (-1, 1):
            for hops in range(1, self.hops + 1):
                allowed, copy = self.first(way, hops)
                pl.when(allowed)(copy.wait_send)
            for stage in range(1, self.c - self.hops):
                allowed, copy = self.onward(way, stage)
                pl.when(allowed)(copy.wait_send)


class Gather:
    def __init__(self, own, place, halves, send_sem, recv_sem, me, n):
        self.own, self.place, self.halves = own, place, halves
        self.send_sem, self.recv_sem, self.me, self.n = send_sem, recv_sem, me, n
        self.direct = [k for k in order_of(n) if k % 2 == 0]
        self.relayed = n == 8
        self.near = [2, 4] if self.relayed else self.direct

    def to(self, src, dst, at, k):
        return send(
            src, dst, self.send_sem.at[at], self.recv_sem.at[at], {"ep": partner(self.me, k, self.n)}
        )

    def across(self, k):
        return self.to(self.own, self.place(self.me), k, k)

    def relay(self, k):
        half = self.halves(partner(self.me, k, self.n))[k // 4]
        return self.to(half, half, self.n + k // 4, 6 - k)

    def pass_on(self, k):
        block = self.place(partner(self.me, k, self.n))
        return self.to(block, block, k + 1, 1)

    def start(self):
        for k in self.near + [1]:
            self.across(k).start()

    def middle(self):
        for k in self.near:
            self.across(k).wait_recv()
            if self.relayed:
                self.relay(k).start()
            self.pass_on(k).start()

    def last(self):
        if self.relayed:
            for k in (2, 4):
                self.relay(k).wait_recv()
            self.pass_on(6).start()

    def finish(self):
        self.across(1).wait()
        for k in self.near:
            self.across(k).wait_send()
            if self.relayed:
                self.relay(k).wait_send()
        for k in self.direct:
            self.pass_on(k).wait()


class Spread:
    def __init__(self, r, name, me, grp, n, c, place, halves):
        self.send_buf, self.recv_buf, self.final, self.ss, self.rs, ys, yr, self.local = (
            getattr(r, name + part)
            for part in ("_send", "_recv", "_fin", "_ss", "_rs", "_ys", "_yr", "_ls")
        )
        self.me, self.grp, self.c, self.place = me, grp, c, place
        self.gather = Gather(
            place(me, None), lambda e: place(e, None), halves, ys, yr, me, n
        )

    def to_piece(self, t):
        target = lax.rem(self.grp + t, self.c)
        return send(
            self.send_buf.at[target],
            self.recv_buf.at[self.grp],
            self.ss.at[0, t],
            self.rs.at[0, t],
            {"dp": target},
        )

    def to_copies(self, t):
        return send(
            self.final,
            self.place(self.me, self.grp),
            self.ss.at[1, t],
            self.rs.at[1, t],
            {"dp": lax.rem(self.grp + t, self.c)},
        )

    def mine(self):
        return pltpu.make_async_copy(
            self.final, self.place(self.me, self.grp), self.local.at[0]
        )

    def scatter(self):
        for t in range(1, self.c):
            self.to_piece(t).start()
        self.recv_buf[self.grp] = self.send_buf[self.grp]

    def total(self):
        for t in range(1, self.c):
            self.to_piece(t).wait_recv()
        total = self.recv_buf[0].astype(F32)
        for s in range(1, self.c):
            total = total + self.recv_buf[s].astype(F32)
        self.final[...] = total.astype(BF)
        for t in range(1, self.c):
            self.to_copies(t).start()
        self.mine().start()

    def over(self):
        for t in range(1, self.c):
            self.to_copies(t).wait_recv()
        self.mine().wait()
        self.gather.start()

    def finish(self):
        self.gather.finish()
        for t in range(1, self.c):
            self.to_piece(t).wait_send()
            self.to_copies(t).wait_send()


def block_kernel(r, n, c):
    me, grp = lax.axis_index("ep"), lax.axis_index("dp")
    rows, width = r.tokens.shape
    own, cap = width // n, 2 * rows // n
    slots = n * cap
    hidden = r.w_in.shape[1]
    part = hidden // c
    order = order_of(n)
    direct = [k for k in order if k % 2 == 0]
    partners = {k: partner(me, k, n) for k in range(n)}
    half = width // 2

    def to_partner(src, dst, send_sem, recv_sem, k):
        return send(src, dst, send_sem, recv_sem, {"ep": partners[k]})

    def blocks_out(buf, dst, sems, k):
        return to_partner(buf.at[partners[k]], dst.at[me], sems[0].at[k], sems[1].at[k], k)

    barrier = pltpu.get_barrier_semaphore()
    for k in order:
        pl.semaphore_signal(barrier, inc=1, device_id={"ep": partners[k]}, device_id_type=MESH)
    for t in range(1, c):
        pl.semaphore_signal(
            barrier, inc=1, device_id={"dp": lax.rem(grp + t, c)}, device_id_type=MESH
        )

    def load_qkv(slot):
        cols = pl.ds(0, 3 * width)
        return [
            pltpu.make_async_copy(
                r.w_qkv.at[pl.ds(0, half), :], r.act.at[:, cols], r.load_sem.at[slot]
            ),
            pltpu.make_async_copy(
                r.w_qkv.at[pl.ds(half, half), :], r.grad_pre.at[:, cols], r.load_sem.at[slot + 1]
            ),
        ]

    first_loads = load_qkv(0)
    load_o = pltpu.make_async_copy(r.w_o, r.w_o_v, r.load_sem.at[2])
    load_out = pltpu.make_async_copy(r.w_out.at[0], r.w_out_v, r.load_sem.at[3])
    load_in = pltpu.make_async_copy(r.w_in.at[0], r.w_in_v, r.load_sem.at[4])
    for load in first_loads + [load_o, load_out, load_in]:
        load.start()

    r.place[...] = place_matrix(r.ids[...], n, cap)
    for t in range(width // TILE):
        cols = slice(t * TILE, (t + 1) * TILE)
        r.g_send[:, :, cols] = (
            dot(r.place[...], r.cotangent[:, cols], NN).astype(BF).reshape(n, cap, TILE)
        )
    pl.semaphore_wait(barrier, n - 1 + c - 1)
    g_copies = [blocks_out(r.g_send, r.g_own, (r.g_ss, r.g_rs), k) for k in order]
    for copy in g_copies:
        copy.start()
    r.g_own[me] = r.g_send[me]

    norm_apply(r.tokens, r.gain_attn, r.shift_attn, r.normed)

    def to_heads(p, k):
        return to_partner(
            r.qkv_send.at[p, partners[k]],
            r.qkv_heads.at[p, me],
            r.a_ss.at[p, k],
            r.a_rs.at[p, k],
            k,
        )

    for load in first_loads:
        load.wait()
    for p in range(3):
        for t in range(width // TILE):
            cols = slice(p * width + t * TILE, p * width + (t + 1) * TILE)
            block = dot(r.normed[:, :half], r.act[:, cols], NN)
            block = (block + dot(r.normed[:, half:], r.grad_pre[:, cols], NN)).astype(BF)
            for e in range(TILE // own):
                r.qkv_send[p, t * (TILE // own) + e] = block[:, e * own : (e + 1) * own]
        for k in order:
            to_heads(p, k).start()
        r.qkv_heads[p, me] = r.qkv_send[p, me]

    g_line = Line(r.g_own, r.g_all, r.gz_ss, r.gz_rs, grp, c, 1)
    x_line = Line(r.x_own, r.x_all, r.xz_ss, r.xz_rs, grp, c, 1)
    for copy in g_copies:
        copy.wait()
    g_line.start()

    load_out.wait()

    for p in range(3):
        for k in order:
            to_heads(p, k).wait_recv()

    def normed_halves(e):
        return [
            r.normed_all.at[e, pl.ds(0, rows // 2), :],
            r.normed_all.at[e, pl.ds(rows // 2, rows // 2), :],
        ]

    normed_gather = Gather(
        r.normed, lambda e: r.normed_all.at[e], normed_halves, r.n_ss, r.n_rs, me, n
    )
    mine = pltpu.make_async_copy(r.normed, r.normed_all.at[me], r.load_sem.at[5])
    mine.start()

    for i in range(n):
        r.values_t[i] = r.qkv_heads[2, i].astype(F32).T.astype(BF)

    def home(t):
        target = lax.rem(me + t, n)
        return send(
            r.att_heads.at[target],
            r.att_recv.at[me],
            r.o_ss.at[t],
            r.o_rs.at[t],
            {"ep": target},
        )

    def block_step(t, _):
        at = lax.rem(me + t, n)
        if n > UNROLLED:
            attend_block_loop(r, at)
        else:
            lax.switch(at, [functools.partial(attend_block, r, i) for i in range(n)])

        @pl.when(t > 0)
        def _():
            home(t).start()

        pl.when(t == n // 2)(lambda: g_line.hand_on(1))
        return 0

    lax.fori_loop(0, n, block_step, 0)
    r.att_recv[me] = r.att_heads[me]

    for t in range(1, n):
        home(t).wait_recv()
    for e in range(n):
        r.attended[:, e * own : (e + 1) * own] = r.att_recv[e]

    load_o.wait()
    for t in range(width // TILE):
        cols = slice(t * TILE, (t + 1) * TILE)
        r.hidden[:, cols] = r.tokens[:, cols].astype(F32) + dot(
            r.attended[...], r.w_o_v[:, cols], NN
        )
    norm_apply(r.hidden, r.gain_ffn, r.shift_ffn, r.block_out)
    for t in range(width // TILE):
        cols = slice(t * TILE, (t + 1) * TILE)
        r.x_send[:, :, cols] = (
            dot(r.place[...], r.block_out[:, cols], NN).astype(BF).reshape(n, cap, TILE)
        )
    x_copies = [blocks_out(r.x_send, r.x_own, (r.x_ss, r.x_rs), k) for k in order]
    for copy in x_copies:
        copy.start()
    r.x_own[me] = r.x_send[me]

    def act_grad(cols):
        r.grad_pre[:, cols] = dot(flat(r.g_own[...]), r.w_out_v[cols, :], NT).astype(BF)

    tiles(hidden, act_grad)
    load_in.wait()

    for copy in x_copies:
        copy.wait()
    x_line.start()
    normed_gather.start()

    def expert_step(cols):
        pre = dot(flat(r.x_own[...]), r.w_in_v[cols, :], NT)
        for q in range(slots // CHUNK):
            at = slice(q * CHUNK, (q + 1) * CHUNK)
            act, slope = gelu_both(pre[at])
            r.act[at, cols] = act.astype(BF)
            r.grad_pre[at, cols] = (r.grad_pre[at, cols].astype(F32) * slope).astype(BF)

    tiles(hidden, expert_step, {2: lambda: g_line.hand_on(2)})

    def routed_grad(cols):
        r.g_send[:, :, cols] = (
            dot(r.grad_pre[...], r.w_in_v[:, cols], NN).astype(BF).reshape(n, cap, TILE)
        )

    tiles(width, routed_grad)
    r_copies = [blocks_out(r.g_send, r.r_recv, (r.r_ss, r.r_rs), k) for k in order]
    for copy in r_copies:
        copy.start()
    r.r_recv[me] = r.g_send[me]

    def produce(cols):
        r.x_send[:, :, cols] = (
            dot(r.act[...], r.w_out_v[:, cols], NN).astype(BF).reshape(n, cap, TILE)
        )

    tiles(width, produce)
    r.p_recv[me] = r.x_send[me]
    mine_at = pl.multiple_of(grp * part, part)

    def weight_terms(act_at, x_rows, g_rows, first):
        def one(out):
            from_act = pl.ds(pl.multiple_of(act_at + out.start, TILE), TILE)

            def two(cols):
                term_in = dot(r.grad_pre[:, from_act], x_rows(cols), TN)
                r.sum_in[out, cols] = term_in if first else r.sum_in[out, cols] + term_in
                term_out = dot(r.act[:, from_act], g_rows(cols), TN)
                r.sum_out[out, cols] = term_out if first else r.sum_out[out, cols] + term_out

            tiles(width, two)

        tiles(part, one)

    weight_terms(
        mine_at,
        lambda cols: flat(r.x_own[:, :, cols]),
        lambda cols: flat(r.g_own[:, :, cols]),
        True,
    )

    for copy in r_copies:
        copy.wait()

    x_line.hand_on(1)
    g_line.hand_on(*range(3, c))

    for t in range(width // TILE):
        cols = slice(t * TILE, (t + 1) * TILE)
        r.grad_tokens[:, cols] = dot(r.place[...], flat(r.r_recv[:, :, cols]), TN)

    def store_hidden(at, grad_in):
        grad_hidden = r.cotangent[at, :].astype(F32) + grad_in
        r.grad_tokens[at, :] = grad_hidden
        r.block_out[at, :] = grad_hidden.astype(BF)

    sums = norm_back(r.hidden, r.grad_tokens, r.gain_ffn, store_hidden)
    r.small_own[2:3], r.small_own[3:4] = sums
    r.small_own[4:SMALL] = jnp.zeros((SMALL - 4, width), F32)
    for t in range(width // TILE):
        block = dot(r.block_out[...], r.w_o_v[t * TILE : (t + 1) * TILE, :], NT).astype(BF)
        for e in range(TILE // own):
            r.att_recv[t * (TILE // own) + e] = block[:, e * own : (e + 1) * own]
    a_copies = [blocks_out(r.att_recv, r.grad_att, (r.b_ss, r.b_rs), k) for k in order]
    for copy in a_copies:
        copy.start()
    r.grad_att[me] = r.att_recv[me]

    def wo_rows(buf, e):
        at = e * own
        return buf.at[
            pl.ds(pl.multiple_of(lax.rem(at, slots), own), own),
            pl.ds(pl.multiple_of(lax.div(at, slots) * width, width), width),
        ]

    for t in range(width // slots):
        out = slice(t * slots, (t + 1) * slots)
        r.act[:, t * width : (t + 1) * width] = dot(
            r.attended[:, out], r.block_out[...], TN
        ).astype(BF)

    def to_sibling(k):
        at = partners[k]
        return to_partner(
            wo_rows(r.act, at), wo_rows(r.grad_pre, at), r.w_ss.at[k], r.w_rs.at[k], 1
        )

    def to_owner(k):
        return to_partner(
            wo_rows(r.act, partners[k]),
            wo_rows(r.grad_pre, partners[1]),
            r.w_ss.at[k],
            r.w_rs.at[k],
            k,
        )

    for copy in a_copies:
        copy.wait()
    normed_gather.middle()
    p_copies = [blocks_out(r.x_send, r.p_recv, (r.p_ss, r.p_rs), k) for k in order]
    for copy in p_copies:
        copy.start()

    for k in range(1, n, 2):
        to_sibling(k).start()

    def wo_across():
        for k in range(1, n, 2):
            to_sibling(k).wait()
        for k in [0] + direct:
            mine_k = wo_rows(r.act, partners[k])
            mine_k[...] = (
                mine_k[...].astype(F32) + wo_rows(r.grad_pre, partners[k])[...].astype(F32)
            ).astype(BF)
        for k in direct:
            to_owner(k).start()

    for p in range(3):
        for k in order:
            to_heads(p, k).wait_send()
    for t in range(1, n):
        home(t).wait_send()
    for i in range(n):
        both = (r.grad_att[i].astype(F32) * r.att_heads[i].astype(F32)).T
        size = own // r.heads
        deltas = [
            jnp.sum(both[h * size : (h + 1) * size], axis=0, keepdims=True) for h in range(r.heads)
        ]
        r.delta[i] = jnp.concatenate(
            deltas + [jnp.zeros((SMALL - r.heads, rows), F32)], axis=0
        )
    r.grad_q_t[...] = jnp.zeros(r.grad_q_t.shape, F32)

    def back_home(p, t):
        target = lax.rem(me + t, n)
        return send(
            r.qkv_send.at[p, target],
            r.grad_tok.at[p, me],
            r.d_ss.at[p, t],
            r.d_rs.at[p, t],
            {"ep": target},
        )

    def back_step(t, _):
        attend_back(r, lax.rem(me + t, n), n)
        pl.when(t == 0)(wo_across)

        @pl.when(t > 0)
        def _():
            for p in (1, 2):
                back_home(p, t).start()

        return 0

    lax.fori_loop(0, n, back_step, 0)
    for i in range(n):
        r.qkv_send[0, i] = (r.grad_q_t[i].T * ((own // r.heads) ** -0.5)).astype(BF)
    for t in range(1, n):
        back_home(0, t).start()
    for p in range(3):
        r.grad_tok[p, me] = r.qkv_send[p, me]
    normed_gather.last()

    def o_place(e, d):
        at = pl.ds(pl.multiple_of(e * own, own), own)
        piece = width // c
        if d is None:
            return r.o_all.at[at, :]
        return r.o_all.at[at, pl.ds(pl.multiple_of(d * piece, piece), piece)]

    def o_halves(e):
        at = pl.ds(pl.multiple_of(e * own, own), own)
        return [r.o_all.at[at, pl.ds(0, half)], r.o_all.at[at, pl.ds(half, half)]]

    def q_place(first, e, d):
        piece = TILE // c
        if d is None:
            return r.q_all.at[:, e, pl.ds(first, TILE), :]
        return r.q_all.at[:, e, pl.ds(pl.multiple_of(first + d * piece, piece), piece), :]

    def q_halves(first, e):
        return [
            r.q_all.at[:, e, pl.ds(first, TILE // 2), :],
            r.q_all.at[:, e, pl.ds(first + TILE // 2, TILE // 2), :],
        ]

    o_spread = Spread(r, "wo", me, grp, n, c, o_place, o_halves)
    q_spreads = [
        Spread(
            r,
            "wq" + str(t),
            me,
            grp,
            n,
            c,
            functools.partial(q_place, t * TILE),
            functools.partial(q_halves, t * TILE),
        )
        for t in range(width // TILE)
    ]

    normed_gather.finish()
    mine.wait()
    at_once = width // rows
    turns = n // at_once

    def normed_loads(t):
        out = []
        for b in range(turns):
            spot = (t if turns <= 2 else b // 2) * TILE
            for s in range(at_once):
                out.append(
                    pltpu.make_async_copy(
                        r.normed_all.at[b * at_once + s, :, pl.ds(t * TILE, TILE)],
                        r.space.at[
                            pl.ds((b % 2) * width + s * rows, rows), pl.ds(spot, TILE)
                        ],
                        r.slab_sem.at[t % 2, b * at_once + s],
                    )
                )
        return out

    for t in range(width // TILE if turns <= 2 else 1):
        for load in normed_loads(t):
            load.start()
    for t, spread in enumerate(q_spreads):
        if turns > 2 and t:
            for load in normed_loads(t):
                load.start()
        for load in normed_loads(t):
            load.wait()
        total = None
        for b in range(turns):
            spot = (t if turns <= 2 else b // 2) * TILE
            grads = jnp.concatenate(
                [flat(r.qkv_send[p, b * at_once : (b + 1) * at_once]) for p in range(3)], axis=1
            )
            term = dot(
                r.space[(b % 2) * width : (b % 2 + 1) * width, spot : spot + TILE], grads, TN
            )
            total = term if b == 0 else total + term
        low = total.astype(BF)
        piece = TILE // c
        for d in range(c):
            for p in range(3):
                spread.send_buf[d, p] = low[
                    d * piece : (d + 1) * piece, p * own : (p + 1) * own
                ]
        spread.scatter()

    for copy in p_copies:
        copy.wait()
    for t in range(width // TILE):
        cols = slice(t * TILE, (t + 1) * TILE)
        r.block_out[:, cols] = (
            r.hidden[:, cols] + dot(r.place[...], flat(r.p_recv[:, :, cols]), TN)
        ).astype(BF)


    def slab_loads(q):
        at = partner(grp, q, c)
        base = (q % 2) * width
        out = []
        for which, src in enumerate((r.x_all, r.g_all)):
            for s in range(n):
                out.append(
                    pltpu.make_async_copy(
                        src.at[at, s],
                        r.space.at[pl.ds(base + which * slots + s * cap, cap), :],
                        r.slab_sem.at[q % 2, which * n + s],
                    )
                )
        return out

    def slab_start(q):
        g_line.wait(partner(grp, q, c))
        x_line.wait(partner(grp, q, c))
        for load in slab_loads(q):
            load.start()

    def slab(q):
        base = (q % 2) * width
        for load in slab_loads(q):
            load.wait()
        x_rows, g_rows = r.space.at[pl.ds(base, slots), :], r.space.at[pl.ds(base + slots, slots), :]

        def activate(out):
            at = pl.ds(pl.multiple_of(mine_at + out.start, TILE), TILE)
            cols = pl.ds(pl.multiple_of(3 * width + out.start, TILE), TILE)
            r.grad_pre[:, cols] = dot(g_rows[...], r.w_out_v[at, :], NT).astype(BF)
            pre = dot(x_rows[...], r.w_in_v[at, :], NT)
            for q in range(slots // CHUNK):
                some = slice(q * CHUNK, (q + 1) * CHUNK)
                act, slope = gelu_both(pre[some])
                r.act[some, cols] = act.astype(BF)
                r.grad_pre[some, cols] = (r.grad_pre[some, cols].astype(F32) * slope).astype(BF)

        tiles(part, activate)
        weight_terms(
            3 * width, lambda cols: x_rows[:, cols], lambda cols: g_rows[:, cols], False
        )

    slab_start(1)

    slab(1)

    for k in direct:
        to_owner(k).wait()
    total = wo_rows(r.act, me)[...].astype(F32)
    for k in direct:
        total = total + wo_rows(r.grad_pre, partners[k + 1])[...].astype(F32)
    for d in range(c):
        r.wo_send[d] = total[:, d * (width // c) : (d + 1) * (width // c)].astype(BF)
    o_spread.scatter()
    last_loads = load_qkv(0)
    for load in last_loads:
        load.start()

    for spread in q_spreads:
        spread.total()
    x_line.hand_on(*range(2, c))

    for p in (1, 2, 0):
        for t in range(1, n):
            back_home(p, t).wait_recv()
    for load in last_loads:
        load.wait()

    for p in range(3):
        for e in range(n):
            r.attended[:, e * own : (e + 1) * own] = r.grad_tok[p, e]
        cols = slice(p * width, (p + 1) * width)
        for at, weight in enumerate((r.act, r.grad_pre)):
            out = slice(at * half, (at + 1) * half)
            term = dot(r.attended[...], weight[:, cols], NT)
            r.hidden[:, out] = term if p == 0 else r.hidden[:, out] + term

    def store_tokens(at, grad_in):
        r.grad_tokens[at, :] += grad_in

    sums = norm_back(r.tokens, r.hidden, r.gain_attn, store_tokens)
    r.small_own[0:1], r.small_own[1:2] = sums

    def small_ep(k):
        return to_partner(r.small_own, r.small_ep.at[me], r.s_ss.at[0, k], r.s_rs.at[0, k], k)

    def small_dp(t):
        return send(
            r.small_sum,
            r.small_dp.at[grp],
            r.s_ss.at[1, t],
            r.s_rs.at[1, t],
            {"dp": lax.rem(grp + t, c)},
        )

    for k in order:
        small_ep(k).start()
    r.small_ep[me] = r.small_own[...]

    o_spread.total()
    q_spreads[0].over()

    if c > 2:
        slab_start(2)
        slab(2)

    for spread in q_spreads[1:]:
        spread.over()
    q_spreads[0].gather.middle()
    o_spread.over()

    for q in range(3, c):
        slab_start(q)

        slab(q)

    out_copies = []
    for at, (src, dst) in enumerate(((r.sum_in, r.grad_in), (r.sum_out, r.grad_out))):
        base = at * width
        for s in range(0, part, CHUNK * 4):
            r.space[base + s : base + s + CHUNK * 4, :] = src[s : s + CHUNK * 4, :].astype(BF)
        out_copies.append(
            pltpu.make_async_copy(
                r.space.at[pl.ds(base, part), :], dst, r.load_sem.at[at]
            )
        )
    for copy in out_copies:
        copy.start()

    for k in order:
        small_ep(k).wait()
    total = r.small_ep[0]
    for e in range(1, n):
        total = total + r.small_ep[e]
    r.small_sum[...] = total
    for t in range(1, c):
        small_dp(t).start()
    r.small_dp[grp] = total

    spreads = q_spreads + [o_spread]
    for spread in spreads[1:]:
        spread.gather.middle()
    for spread in spreads:
        spread.gather.last()

    for t in range(1, c):
        small_dp(t).wait()
    total = r.small_dp[0]
    for d in range(1, c):
        total = total + r.small_dp[d]
    r.small[...] = total
    g_line.finish()
    x_line.finish()
    for copy in out_copies:
        copy.wait()
    for spread in spreads:
        spread.finish()
    for p in range(3):
        for t in range(1, n):
            back_home(p, t).wait_send()


def block_call(n, c, heads, operands):
    rows, width = operands["tokens"].shape
    hidden = operands["w_in"].shape[1]
    own, cap, part, piece = width // n, 2 * rows // n, hidden // c, width // c
    slots = n * cap
    vm, hb = pl.BlockSpec(memory_space=pltpu.VMEM), pl.BlockSpec(memory_space=pl.ANY)
    sm = pl.BlockSpec(memory_space=pltpu.SMEM)
    inputs = dict(
        lengths=sm, ids=vm, tokens=vm, cotangent=vm, gain_attn=vm, shift_attn=vm, gain_ffn=vm,
        shift_ffn=vm, w_qkv=hb, w_o=hb, w_in=hb, w_out=hb,
    )
    outputs = dict(
        block_out=((rows, width), BF, vm),
        grad_tokens=((rows, width), F32, vm),
        q_all=((3, n, width, own), BF, hb),
        o_all=((width, width), BF, hb),
        small=((SMALL, width), F32, vm),
        grad_in=((part, width), BF, hb),
        grad_out=((part, width), BF, hb),
        g_all=((c, n, cap, width), BF, hb),
        x_all=((c, n, cap, width), BF, hb),
        normed_all=((n, rows, width), BF, hb),
    )

    def v(*shape):
        return pltpu.VMEM(shape, BF)

    def f(*shape):
        return pltpu.VMEM(shape, F32)

    def d(*shape):
        return pltpu.SemaphoreType.DMA(shape)

    heads_shape = (n, rows, own)
    scratch = dict(
        sum_in=f(part, width), sum_out=f(part, width),
        w_o_v=v(width, width), w_in_v=v(hidden, width), w_out_v=v(hidden, width),
        act=v(slots, hidden), grad_pre=v(slots, hidden), space=v(2 * width, width),
        normed=v(rows, width), place=v(slots, rows), hidden=f(rows, width),
        attended=v(rows, width),
        qkv_send=v(3, *heads_shape), qkv_heads=v(3, *heads_shape), grad_tok=v(3, *heads_shape),
        values_t=v(n, own, rows), att_heads=v(*heads_shape), att_recv=v(*heads_shape),
        grad_att=v(*heads_shape), grad_q_t=f(n, own, rows),
        lse=f(n, SMALL, rows), delta=f(n, SMALL, rows),
        g_send=v(n, cap, width), x_send=v(n, cap, width), g_own=v(n, cap, width),
        x_own=v(n, cap, width), r_recv=v(n, cap, width), p_recv=v(n, cap, width),
        wo_send=v(c, own, piece), wo_recv=v(c, own, piece), wo_fin=v(own, piece),
        small_own=f(SMALL, width), small_ep=f(n, SMALL, width), small_sum=f(SMALL, width),
        small_dp=f(c, SMALL, width),
        load_sem=d(8), slab_sem=d(2, 2 * n),
        a_ss=d(3, n), a_rs=d(3, n), g_ss=d(n), g_rs=d(n), n_ss=d(n + 2), n_rs=d(n + 2),
        o_ss=d(n), o_rs=d(n), x_ss=d(n), x_rs=d(n), r_ss=d(n), r_rs=d(n), p_ss=d(n), p_rs=d(n),
        b_ss=d(n), b_rs=d(n), w_ss=d(n), w_rs=d(n), d_ss=d(3, n), d_rs=d(3, n),
        gz_ss=d(2, c), gz_rs=d(c), xz_ss=d(2, c), xz_rs=d(c),
        wo_ss=d(2, c), wo_rs=d(2, c), wo_ys=d(n + 2), wo_yr=d(n + 2), wo_ls=d(1),
        s_ss=d(2, max(n, c)), s_rs=d(2, max(n, c)),
    )
    for t in range(width // TILE):
        name = "wq" + str(t)
        piece = TILE // c
        scratch[name + "_send"] = scratch[name + "_recv"] = v(c, 3, piece, own)
        scratch[name + "_fin"] = v(3, piece, own)
        scratch[name + "_ss"] = scratch[name + "_rs"] = d(2, c)
        scratch[name + "_ys"] = scratch[name + "_yr"] = d(n + 2)
        scratch[name + "_ls"] = d(1)
    names = list(inputs) + list(outputs) + list(scratch)

    def kernel(*refs):
        r = types.SimpleNamespace(**dict(zip(names, refs)))
        r.heads = heads
        block_kernel(r, n, c)

    result = pl.pallas_call(
        kernel,
        out_shape=[jax.ShapeDtypeStruct(shape, kind) for shape, kind, _ in outputs.values()],
        in_specs=list(inputs.values()),
        out_specs=[spec for _, _, spec in outputs.values()],
        scratch_shapes=list(scratch.values()),
        compiler_params=pltpu.CompilerParams(
            collective_id=0, has_side_effects=True, vmem_limit_bytes=VMEM_LIMIT
        ),
    )(*[operands[name] for name in inputs])
    return dict(zip(outputs, result))


VMEM_LIMIT = 64 << 20
STEPS = 4


def widen_kernel(q_all, o_all, grad_in, grad_out, block, tokens, small, *outs):
    q_out, o_out, in_out, out_out, block_out, tokens_out = outs[:6]
    _, n, _, own = q_all.shape
    for p in range(3):
        for e in range(n):
            at = (p * n + e) * own
            q_out[:, at : at + own] = q_all[p, e].astype(F32)
    o_out[...] = o_all[...].astype(F32)
    in_out[0] = grad_in[...].astype(F32)
    out_out[0] = grad_out[...].astype(F32)
    block_out[...] = block[...]
    tokens_out[...] = tokens[...]
    for at, one in enumerate(outs[6:]):
        one[...] = small[at : at + 1, :]


def widen(out):
    q_all, o_all, grad_in, block = out["q_all"], out["o_all"], out["grad_in"], out["block_out"]
    _, n, width, own = q_all.shape
    part, rows = grad_in.shape[0], block.shape[0]
    S = jax.ShapeDtypeStruct

    def rowwise(count):
        return pl.BlockSpec((count // STEPS, width), lambda i: (i, 0))

    expert = pl.BlockSpec((1, part // STEPS, width), lambda i: (0, i, 0))
    fixed = pl.BlockSpec((1, width), lambda i: (0, 0))
    return pl.pallas_call(
        widen_kernel,
        grid=(STEPS,),
        out_shape=[
            S((width, 3 * width), F32), S((width, width), F32), S((1, part, width), F32),
            S((1, part, width), F32), S((rows, width), BF), S((rows, width), F32),
        ] + [S((1, width), F32)] * 4,
        in_specs=[
            pl.BlockSpec((3, n, width // STEPS, own), lambda i: (0, 0, i, 0)),
            rowwise(width), rowwise(part), rowwise(part), rowwise(rows), rowwise(rows),
            pl.BlockSpec((SMALL, width), lambda i: (0, 0)),
        ],
        out_specs=[
            pl.BlockSpec((width // STEPS, 3 * width), lambda i: (i, 0)),
            rowwise(width), expert, expert, rowwise(rows), rowwise(rows),
        ] + [fixed] * 4,
        compiler_params=pltpu.CompilerParams(vmem_limit_bytes=VMEM_LIMIT),
    )(q_all, o_all, grad_in, out["grad_out"], block, out["grad_tokens"], out["small"])


def on_device(
    tokens,
    gain_attn,
    shift_attn,
    w_qkv,
    w_o,
    gain_ffn,
    shift_ffn,
    w_in,
    w_out,
    seq_lengths,
    expert_ids,
    cotangent,
):
    rows, width = tokens.shape
    n, c = lax.axis_size("ep"), lax.axis_size("dp")
    operands = dict(
        lengths=seq_lengths,
        ids=expert_ids.reshape(1, rows),
        tokens=tokens,
        cotangent=cotangent,
        gain_attn=gain_attn[None],
        shift_attn=shift_attn[None],
        gain_ffn=gain_ffn[None],
        shift_ffn=shift_ffn[None],
        w_qkv=w_qkv,
        w_o=w_o,
        w_in=w_in,
        w_out=w_out,
    )
    out = block_call(n, c, HEADS // n, operands)
    q_out, o_out, in_out, out_out, block, tokens_out, *small = widen(out)
    small = [one.reshape(width) for one in small]
    return (block, tokens_out, q_out, o_out, *small, in_out, out_out)


def solution(mesh):
    return jax.shard_map(
        on_device,
        mesh=mesh,
        in_specs=(
            P(("dp", "ep"), None),
            P(),
            P(),
            P(),
            P(),
            P(),
            P(),
            P("ep", None, None),
            P("ep", None, None),
            P("dp", None),
            P(("dp", "ep"), None),
            P(("dp", "ep"), None),
        ),
        out_specs=(
            P(("dp", "ep"), None),
            P(("dp", "ep"), None),
            P(),
            P(),
            P(),
            P(),
            P(),
            P(),
            P("ep", "dp", None),
            P("ep", "dp", None),
        ),
        check_vma=False,
    )
```

```python
import functools
import types

import jax
import jax.numpy as jnp
from jax import lax
from jax.experimental import pallas as pl
from jax.experimental.pallas import tpu as pltpu
from jax.sharding import PartitionSpec as P

HEADS = 16
EPSILON = 1e-05
MASKED = -1e30
TILE = 512
SMALL = 8
UNROLLED = 8
AT_ONCE = 4
MESH = pl.DeviceIdType.MESH
F32 = jnp.float32
BF = jnp.bfloat16
NN = (((1,), (0,)), ((), ()))
NT = (((1,), (1,)), ((), ()))
TN = (((0,), (0,)), ((), ()))


def dot(left, right, dims):
    return lax.dot_general(left, right, dims, preferred_element_type=F32)


def partner(me, k, n):
    out, weight = 0, 1
    while weight < n:
        bit = lax.rem(lax.div(me, weight), 2)
        out = out + (lax.rem(bit + 1, 2) if k & weight else bit) * weight
        weight *= 2
    return out


def send(src, dst, send_sem, recv_sem, target):
    return pltpu.make_async_remote_copy(
        src_ref=src,
        dst_ref=dst,
        send_sem=send_sem,
        recv_sem=recv_sem,
        device_id=target,
        device_id_type=MESH,
    )


def order_of(n):
    return sorted(range(1, n), key=lambda k: (-bin(k // 2).count("1"), k))


def flat(value):
    return value.reshape(value.shape[0] * value.shape[1], value.shape[2])


def tiles(count, body, beside=None):
    def step(t, _):
        body(pl.ds(pl.multiple_of(t * TILE, TILE), TILE))
        for at, act in (beside or {}).items():
            pl.when(t == at)(act)
        return 0

    lax.fori_loop(0, count // TILE, step, 0)


def norm_rows(rows_in):
    average = jnp.mean(rows_in, axis=-1, keepdims=True)
    centered = rows_in - average
    inv_std = lax.rsqrt(jnp.mean(centered * centered, axis=-1, keepdims=True) + EPSILON)
    return centered * inv_std, inv_std


CHUNK = 32


def by_rows(count, body, carry=0):
    def step(i, state):
        return body(pl.ds(pl.multiple_of(i * CHUNK, CHUNK), CHUNK), state)

    return lax.fori_loop(0, count // CHUNK, step, carry)


def norm_apply(src, gain, shift, dst):
    def body(at, _):
        unit, _ = norm_rows(src[at, :].astype(F32))
        dst[at, :] = (unit * gain[...] + shift[...]).astype(BF)
        return 0

    by_rows(src.shape[0], body)


def norm_back(src, grad, gain, store):
    def body(at, sums):
        unit, inv = norm_rows(src[at, :].astype(F32))
        incoming = grad[at, :]
        grad_unit = incoming * gain[...]
        grad_in = inv * (
            grad_unit
            - jnp.mean(grad_unit, axis=-1, keepdims=True)
            - unit * jnp.mean(grad_unit * unit, axis=-1, keepdims=True)
        )
        store(at, grad_in)
        return (
            sums[0] + jnp.sum(incoming * unit, axis=0, keepdims=True),
            sums[1] + jnp.sum(incoming, axis=0, keepdims=True),
        )

    zero = jnp.zeros((1, src.shape[1]), F32)
    return by_rows(src.shape[0], body, (zero, zero))


def gelu_both(pre):
    square = pre * pre
    bent = jnp.tanh(0.7978845608028654 * pre * (1.0 + 0.044715 * square))
    half = 0.5 + 0.5 * bent
    rise = 0.7978845608028654 * (1.0 + 3 * 0.044715 * square)
    return pre * half, half + 0.5 * pre * (1.0 - bent * bent) * rise


def place_matrix(ids_row, n, cap):
    rows = ids_row.shape[1]
    expert = lax.broadcasted_iota(jnp.int32, (n, rows), 0)
    hit = (expert == ids_row).astype(F32)
    before = lax.broadcasted_iota(jnp.int32, (rows, rows), 0)
    after = lax.broadcasted_iota(jnp.int32, (rows, rows), 1)
    upto = (before <= after).astype(F32).astype(BF)
    count = dot(hit.astype(BF), upto, NN)
    slot = jnp.sum(hit * (count - 1.0), axis=0, keepdims=True)
    target = ids_row * cap + slot.astype(jnp.int32)
    places = lax.broadcasted_iota(jnp.int32, (n * cap, rows), 0)
    return (places == target).astype(F32).astype(BF)


def start_row(len_ref, first, width):
    pos = first + lax.broadcasted_iota(jnp.int32, (1, width), 1)
    start = jnp.zeros((1, width), jnp.int32)
    edge = jnp.int32(0)
    for s in range(len_ref.shape[1] - 1):
        edge = edge + len_ref[0, s]
        start = jnp.where(pos >= edge, edge, start)
    return pos, start


def split_heads(block, heads):
    if heads == 1:
        return [block]
    size = block.shape[1] // heads
    lane = lax.broadcasted_iota(jnp.int32, block.shape, 1)
    zero = jnp.zeros_like(block)
    return [
        jnp.where((lane >= h * size) & (lane < (h + 1) * size), block, zero) for h in range(heads)
    ]


def attend_block(r, i):
    rows, own = r.qkv_heads.shape[2:]
    heads = r.heads
    size = own // heads
    queries = split_heads(r.qkv_heads[0, i] * BF(size**-0.5), heads)
    pos, start = start_row(r.lengths, i * rows, rows)
    outs, sums = [], []
    for h in range(heads):
        top = jnp.full((1, rows), MASKED, F32)
        total = jnp.zeros((1, rows), F32)
        accum = jnp.zeros((size, rows), F32)
        for last in range(i, -1, -AT_ONCE):
            scores = []
            blocks = range(last, max(last - AT_ONCE, -1), -1)
            for j in blocks:
                key = j * rows + lax.broadcasted_iota(jnp.int32, (rows, rows), 0)
                allowed = key >= start
                if j == i:
                    allowed = allowed & (key <= pos)
                scores.append(
                    jnp.where(allowed, dot(r.qkv_heads[1, j], queries[h], NT), MASKED)
                )
            peak = functools.reduce(
                jnp.maximum, [jnp.max(s.reshape(rows // 8, 8, rows), axis=0) for s in scores]
            )
            new_top = jnp.maximum(top, jnp.max(peak, axis=0, keepdims=True))
            decay = jnp.exp(top - new_top)
            accum = accum * decay
            part = jnp.zeros((8, rows), F32)
            for j, s in zip(blocks, scores):
                weights = jnp.exp(s - new_top)
                part = part + jnp.sum(weights.reshape(rows // 8, 8, rows), axis=0)
                values = r.values_t[j, h * size : (h + 1) * size, :]
                accum = accum + dot(values, weights.astype(BF), NN)
            total = total * decay + jnp.sum(part, axis=0, keepdims=True)
            top = new_top
        outs.append(accum / total)
        sums.append(top + jnp.log(total))
    r.att_heads[i] = jnp.concatenate(outs, axis=0).T.astype(BF)
    r.lse[i] = jnp.concatenate(sums + [jnp.zeros((SMALL - heads, rows), F32)], axis=0)


def attend_back(r, j, n):
    rows, own = r.qkv_heads.shape[2:]
    heads = r.heads
    size = own // heads
    keys, values = r.qkv_heads[1, j], r.qkv_heads[2, j]
    keys_t = keys.astype(F32).T.astype(BF)

    def fold(at, carry, diagonal):
        grad_k, grad_v = carry
        for i in at:
            queries = split_heads(r.qkv_heads[0, i] * BF(size**-0.5), heads)
            grads = split_heads(r.grad_att[i], heads)
            pos, start = start_row(r.lengths, i * rows, rows)
            key = j * rows + lax.broadcasted_iota(jnp.int32, (rows, rows), 0)
            allowed = key >= start
            if diagonal:
                allowed = allowed & (key <= pos)
            for h in range(heads):
                scores = dot(keys, queries[h], NT)
                probs = jnp.where(allowed, jnp.exp(scores - r.lse[i, h : h + 1, :]), 0.0)
                grad_probs = dot(values, grads[h], NT)
                grad_scores = (probs * (grad_probs - r.delta[i, h : h + 1, :])).astype(BF)
                grad_v = grad_v + dot(probs.astype(BF), grads[h], NN)
                grad_k = grad_k + dot(grad_scores, queries[h], NN)
                part = slice(h * size, (h + 1) * size)
                r.grad_q_t[i, part, :] += dot(keys_t[part, :], grad_scores, NN)
        return grad_k, grad_v

    zero = jnp.zeros((rows, own), F32)
    carry = fold([j], (zero, zero), True)
    left = n - 1 - j
    odd = lax.rem(left, 2)
    carry = lax.fori_loop(j + 1, j + 1 + odd, lambda i, carry: fold([i], carry, False), carry)

    def pair(t, carry):
        i = j + 1 + odd + 2 * t
        return fold([i, i + 1], carry, False)

    grad_k, grad_v = lax.fori_loop(0, lax.div(left, 2), pair, carry)
    r.qkv_send[1, j] = grad_k.astype(BF)
    r.qkv_send[2, j] = grad_v.astype(BF)


def attend_block_loop(r, i):
    rows, own = r.qkv_heads.shape[2:]
    heads = r.heads
    size = own // heads
    queries = split_heads(r.qkv_heads[0, i] * BF(size**-0.5), heads)
    pos, start = start_row(r.lengths, i * rows, rows)

    def fold(j, carry, diagonal):
        keys = r.qkv_heads[1, j]
        key = j * rows + lax.broadcasted_iota(jnp.int32, (rows, rows), 0)
        allowed = key >= start
        if diagonal:
            allowed = allowed & (key <= pos)
        out = []
        for h in range(heads):
            top, total, accum = carry[h]
            scores = jnp.where(allowed, dot(keys, queries[h], NT), MASKED)
            new_top = jnp.maximum(top, jnp.max(scores, axis=0, keepdims=True))
            weights = jnp.exp(scores - new_top)
            if diagonal:
                weights = jnp.where(allowed, weights, 0.0)
            decay = jnp.exp(top - new_top)
            total = total * decay + jnp.sum(weights, axis=0, keepdims=True)
            values = r.values_t[j, h * size : (h + 1) * size, :]
            accum = accum * decay + dot(values, weights.astype(BF), NN)
            out.append((new_top, total, accum))
        return tuple(out)

    state = tuple(
        (
            jnp.full((1, rows), MASKED, F32),
            jnp.zeros((1, rows), F32),
            jnp.zeros((size, rows), F32),
        )
        for _ in range(heads)
    )
    state = fold(i, state, True)
    state = lax.fori_loop(0, i, lambda j, carry: fold(j, carry, False), state)
    result = jnp.concatenate([accum / total for _, total, accum in state], axis=0)
    r.att_heads[i] = result.T.astype(BF)
    sums = [top + jnp.log(total) for top, total, _ in state]
    r.lse[i] = jnp.concatenate(sums + [jnp.zeros((SMALL - heads, rows), F32)], axis=0)


class Line:
    def __init__(self, block, whole, send_sem, recv_sem, at, c, parts):
        self.block, self.whole, self.at, self.c = block, whole, at, c
        self.send_sem, self.recv_sem, self.parts = send_sem, recv_sem, parts

    def can(self, index):
        return (index >= 0) & (index < self.c)

    def rows(self, ref, part):
        size = self.block.shape[1] // self.parts
        return ref.at[:, pl.ds(part * size, size), :]

    def copy(self, way, stage, part):
        held, target = self.at - way * stage, self.at + way
        dst = self.rows(self.whole.at[held], part)
        return self.can(held) & self.can(target), send(
            dst if stage else self.rows(self.block, part),
            dst,
            self.send_sem.at[(way + 1) // 2, stage, part],
            self.recv_sem.at[held, part],
            {"dp": target},
        )

    def each(self, stages):
        for stage in stages:
            for part in range(self.parts):
                for way in (-1, 1):
                    yield self.copy(way, stage, part)

    def start(self, part):
        for way in (-1, 1):
            allowed, copy = self.copy(way, 0, part)
            pl.when(allowed)(copy.start)

    def hand_on(self, *stages):
        for allowed, copy in self.each([s for s in stages if s < self.c - 1]):

            @pl.when(allowed)
            def _():
                copy.wait_recv()
                copy.start()

    def wait(self, block):
        done = ((block < self.at) & self.can(self.at + 1)) | (
            (block > self.at) & self.can(self.at - 1)
        )

        @pl.when(jnp.logical_not(done))
        def _():
            for part in range(self.parts):
                src = self.rows(self.whole.at[block], part)
                recv = self.recv_sem.at[block, part]
                send(src, src, self.send_sem.at[0, 0, 0], recv, {"dp": block}).wait_recv()

    def finish(self):
        for allowed, copy in self.each(range(self.c - 1)):
            pl.when(allowed)(copy.wait_send)


class Gather:
    def __init__(self, own, place, halves, send_sem, recv_sem, me, n):
        self.own, self.place, self.halves = own, place, halves
        self.send_sem, self.recv_sem, self.me, self.n = send_sem, recv_sem, me, n
        self.direct = [k for k in order_of(n) if k % 2 == 0]
        self.relayed = n == 8
        self.near = [2, 4] if self.relayed else self.direct

    def to(self, src, dst, at, k):
        return send(
            src, dst, self.send_sem.at[at], self.recv_sem.at[at], {"ep": partner(self.me, k, self.n)}
        )

    def across(self, k):
        return self.to(self.own, self.place(self.me), k, k)

    def relay(self, k):
        half = self.halves(partner(self.me, k, self.n))[k // 4]
        return self.to(half, half, self.n + k // 4, 6 - k)

    def pass_on(self, k):
        block = self.place(partner(self.me, k, self.n))
        return self.to(block, block, k + 1, 1)

    def start(self):
        for k in self.near + [1]:
            self.across(k).start()

    def middle(self):
        for k in self.near:
            self.across(k).wait_recv()
            if self.relayed:
                self.relay(k).start()
            self.pass_on(k).start()

    def last(self):
        if self.relayed:
            for k in (2, 4):
                self.relay(k).wait_recv()
            self.pass_on(6).start()

    def finish(self):
        self.across(1).wait()
        for k in self.near:
            self.across(k).wait_send()
            if self.relayed:
                self.relay(k).wait_send()
        for k in self.direct:
            self.pass_on(k).wait()


class Spread:
    def __init__(self, r, name, me, grp, n, c, place, halves):
        self.send_buf, self.recv_buf, self.final, self.ss, self.rs, ys, yr, self.local = (
            getattr(r, name + part)
            for part in ("_send", "_recv", "_fin", "_ss", "_rs", "_ys", "_yr", "_ls")
        )
        self.me, self.grp, self.c, self.place = me, grp, c, place
        self.gather = Gather(
            place(me, None), lambda e: place(e, None), halves, ys, yr, me, n
        )

    def to_piece(self, t):
        target = lax.rem(self.grp + t, self.c)
        return send(
            self.send_buf.at[target],
            self.recv_buf.at[self.grp],
            self.ss.at[0, t],
            self.rs.at[0, t],
            {"dp": target},
        )

    def to_copies(self, t):
        return send(
            self.final,
            self.place(self.me, self.grp),
            self.ss.at[1, t],
            self.rs.at[1, t],
            {"dp": lax.rem(self.grp + t, self.c)},
        )

    def mine(self):
        return pltpu.make_async_copy(
            self.final, self.place(self.me, self.grp), self.local.at[0]
        )

    def scatter(self):
        for t in range(1, self.c):
            self.to_piece(t).start()
        self.recv_buf[self.grp] = self.send_buf[self.grp]

    def total(self):
        for t in range(1, self.c):
            self.to_piece(t).wait_recv()
        total = self.recv_buf[0].astype(F32)
        for s in range(1, self.c):
            total = total + self.recv_buf[s].astype(F32)
        self.final[...] = total.astype(BF)
        for t in range(1, self.c):
            self.to_copies(t).start()
        self.mine().start()

    def over(self):
        for t in range(1, self.c):
            self.to_copies(t).wait_recv()
        self.mine().wait()
        self.gather.start()

    def finish(self):
        self.gather.finish()
        for t in range(1, self.c):
            self.to_piece(t).wait_send()
            self.to_copies(t).wait_send()


def block_kernel(r, n, c):
    me, grp = lax.axis_index("ep"), lax.axis_index("dp")
    rows, width = r.tokens.shape
    own, cap = width // n, 2 * rows // n
    slots = n * cap
    hidden = r.w_in.shape[1]
    part = hidden // c
    order = order_of(n)
    direct = [k for k in order if k % 2 == 0]
    partners = {k: partner(me, k, n) for k in range(n)}
    half = width // 2

    def to_partner(src, dst, send_sem, recv_sem, k):
        return send(src, dst, send_sem, recv_sem, {"ep": partners[k]})

    def blocks_out(buf, dst, sems, k):
        return to_partner(buf.at[partners[k]], dst.at[me], sems[0].at[k], sems[1].at[k], k)

    barrier = pltpu.get_barrier_semaphore()
    for k in order:
        pl.semaphore_signal(barrier, inc=1, device_id={"ep": partners[k]}, device_id_type=MESH)
    for t in range(1, c):
        pl.semaphore_signal(
            barrier, inc=1, device_id={"dp": lax.rem(grp + t, c)}, device_id_type=MESH
        )

    def load_qkv(slot):
        cols = pl.ds(0, 3 * width)
        return [
            pltpu.make_async_copy(
                r.w_qkv.at[pl.ds(0, half), :], r.act.at[:, cols], r.load_sem.at[slot]
            ),
            pltpu.make_async_copy(
                r.w_qkv.at[pl.ds(half, half), :], r.grad_pre.at[:, cols], r.load_sem.at[slot + 1]
            ),
        ]

    first_loads = load_qkv(0)
    load_o = pltpu.make_async_copy(r.w_o, r.w_o_v, r.load_sem.at[2])
    load_out = pltpu.make_async_copy(r.w_out.at[0], r.w_out_v, r.load_sem.at[3])
    load_in = pltpu.make_async_copy(r.w_in.at[0], r.w_in_v, r.load_sem.at[4])
    for load in first_loads + [load_o, load_out, load_in]:
        load.start()

    r.place[...] = place_matrix(r.ids[...], n, cap)
    for t in range(width // TILE):
        cols = slice(t * TILE, (t + 1) * TILE)
        r.g_send[:, :, cols] = (
            dot(r.place[...], r.cotangent[:, cols], NN).astype(BF).reshape(n, cap, TILE)
        )
    pl.semaphore_wait(barrier, n - 1 + c - 1)
    half_cap = cap // 2
    g_halves = [
        [
            to_partner(
                r.g_send.at[partners[k], pl.ds(h * half_cap, half_cap), :],
                r.g_own.at[me, pl.ds(h * half_cap, half_cap), :],
                r.g_ss.at[h, k],
                r.g_rs.at[h, k],
                k,
            )
            for k in order
        ]
        for h in range(2)
    ]
    for copy in g_halves[0]:
        copy.start()
    r.g_own[me] = r.g_send[me]

    norm_apply(r.tokens, r.gain_attn, r.shift_attn, r.normed)

    def to_heads(p, k):
        return to_partner(
            r.qkv_send.at[p, partners[k]],
            r.qkv_heads.at[p, me],
            r.a_ss.at[p, k],
            r.a_rs.at[p, k],
            k,
        )

    for load in first_loads:
        load.wait()
    for p in range(3):
        for t in range(width // TILE):
            cols = slice(p * width + t * TILE, p * width + (t + 1) * TILE)
            block = dot(r.normed[:, :half], r.act[:, cols], NN)
            block = (block + dot(r.normed[:, half:], r.grad_pre[:, cols], NN)).astype(BF)
            for e in range(TILE // own):
                r.qkv_send[p, t * (TILE // own) + e] = block[:, e * own : (e + 1) * own]
        r.qkv_heads[p, me] = r.qkv_send[p, me]
    for copy in g_halves[1]:
        copy.start()

    g_line = Line(r.g_own, r.g_all, r.gz_ss, r.gz_rs, grp, c, 2)
    x_line = Line(r.x_own, r.x_all, r.xz_ss, r.xz_rs, grp, c, 1)
    for copy in g_halves[0]:
        copy.wait()
    g_line.start(0)
    for p in range(3):
        for k in order:
            to_heads(p, k).start()
    for copy in g_halves[1]:
        copy.wait()
    g_line.start(1)

    load_out.wait()
    for p in range(3):
        for k in order:
            to_heads(p, k).wait_recv()

    def normed_halves(e):
        return [
            r.normed_all.at[e, pl.ds(0, rows // 2), :],
            r.normed_all.at[e, pl.ds(rows // 2, rows // 2), :],
        ]

    normed_gather = Gather(
        r.normed, lambda e: r.normed_all.at[e], normed_halves, r.n_ss, r.n_rs, me, n
    )
    mine = pltpu.make_async_copy(r.normed, r.normed_all.at[me], r.load_sem.at[5])
    mine.start()

    for i in range(n):
        r.values_t[i] = r.qkv_heads[2, i].astype(F32).T.astype(BF)

    def home(t):
        target = lax.rem(me + t, n)
        return send(
            r.att_heads.at[target],
            r.att_recv.at[me],
            r.o_ss.at[t],
            r.o_rs.at[t],
            {"ep": target},
        )

    def block_step(t, _):
        at = lax.rem(me + t, n)
        if n > UNROLLED:
            attend_block_loop(r, at)
        else:
            lax.switch(at, [functools.partial(attend_block, r, i) for i in range(n)])

        @pl.when(t > 0)
        def _():
            home(t).start()

        pl.when(t == 2)(lambda: g_line.hand_on(1))
        return 0

    lax.fori_loop(0, n, block_step, 0)
    r.att_recv[me] = r.att_heads[me]

    for t in range(1, n):
        home(t).wait_recv()
    for e in range(n):
        r.attended[:, e * own : (e + 1) * own] = r.att_recv[e]

    load_o.wait()
    for t in range(width // TILE):
        cols = slice(t * TILE, (t + 1) * TILE)
        r.hidden[:, cols] = r.tokens[:, cols].astype(F32) + dot(
            r.attended[...], r.w_o_v[:, cols], NN
        )
    norm_apply(r.hidden, r.gain_ffn, r.shift_ffn, r.block_out)
    for t in range(width // TILE):
        cols = slice(t * TILE, (t + 1) * TILE)
        r.x_send[:, :, cols] = (
            dot(r.place[...], r.block_out[:, cols], NN).astype(BF).reshape(n, cap, TILE)
        )
    x_copies = [blocks_out(r.x_send, r.x_own, (r.x_ss, r.x_rs), k) for k in order]
    for copy in x_copies:
        copy.start()
    r.x_own[me] = r.x_send[me]

    def act_grad(cols):
        r.grad_pre[:, cols] = dot(flat(r.g_own[...]), r.w_out_v[cols, :], NT).astype(BF)

    tiles(hidden, act_grad)
    load_in.wait()
    g_line.hand_on(2)

    for copy in x_copies:
        copy.wait()
    x_line.start(0)
    normed_gather.start()

    def expert_step(cols):
        pre = dot(flat(r.x_own[...]), r.w_in_v[cols, :], NT)
        for q in range(slots // CHUNK):
            at = slice(q * CHUNK, (q + 1) * CHUNK)
            act, slope = gelu_both(pre[at])
            r.act[at, cols] = act.astype(BF)
            r.grad_pre[at, cols] = (r.grad_pre[at, cols].astype(F32) * slope).astype(BF)

    tiles(hidden, expert_step)

    def routed_grad(cols):
        r.g_send[:, :, cols] = (
            dot(r.grad_pre[...], r.w_in_v[:, cols], NN).astype(BF).reshape(n, cap, TILE)
        )

    tiles(width, routed_grad)
    r_copies = [blocks_out(r.g_send, r.r_recv, (r.r_ss, r.r_rs), k) for k in order]
    for copy in r_copies:
        copy.start()
    r.r_recv[me] = r.g_send[me]

    def produce(cols):
        r.x_send[:, :, cols] = (
            dot(r.act[...], r.w_out_v[:, cols], NN).astype(BF).reshape(n, cap, TILE)
        )

    tiles(width, produce)
    r.p_recv[me] = r.x_send[me]
    mine_at = pl.multiple_of(grp * part, part)

    def weight_terms(act_at, x_rows, g_rows, first):
        def one(out):
            from_act = pl.ds(pl.multiple_of(act_at + out.start, TILE), TILE)

            def two(cols):
                term_in = dot(r.grad_pre[:, from_act], x_rows(cols), TN)
                r.sum_in[out, cols] = term_in if first else r.sum_in[out, cols] + term_in
                term_out = dot(r.act[:, from_act], g_rows(cols), TN)
                r.sum_out[out, cols] = term_out if first else r.sum_out[out, cols] + term_out

            tiles(width, two)

        tiles(part, one)

    weight_terms(
        mine_at,
        lambda cols: flat(r.x_own[:, :, cols]),
        lambda cols: flat(r.g_own[:, :, cols]),
        True,
    )

    for copy in r_copies:
        copy.wait()

    x_line.hand_on(1)
    g_line.hand_on(*range(3, c))

    for t in range(width // TILE):
        cols = slice(t * TILE, (t + 1) * TILE)
        r.grad_tokens[:, cols] = dot(r.place[...], flat(r.r_recv[:, :, cols]), TN)

    def store_hidden(at, grad_in):
        grad_hidden = r.cotangent[at, :].astype(F32) + grad_in
        r.grad_tokens[at, :] = grad_hidden
        r.block_out[at, :] = grad_hidden.astype(BF)

    sums = norm_back(r.hidden, r.grad_tokens, r.gain_ffn, store_hidden)
    r.small_own[2:3], r.small_own[3:4] = sums
    r.small_own[4:SMALL] = jnp.zeros((SMALL - 4, width), F32)
    for t in range(width // TILE):
        block = dot(r.block_out[...], r.w_o_v[t * TILE : (t + 1) * TILE, :], NT).astype(BF)
        for e in range(TILE // own):
            r.att_recv[t * (TILE // own) + e] = block[:, e * own : (e + 1) * own]
    a_copies = [blocks_out(r.att_recv, r.grad_att, (r.b_ss, r.b_rs), k) for k in order]
    for copy in a_copies:
        copy.start()
    r.grad_att[me] = r.att_recv[me]

    def wo_rows(buf, e):
        at = e * own
        return buf.at[
            pl.ds(pl.multiple_of(lax.rem(at, slots), own), own),
            pl.ds(pl.multiple_of(lax.div(at, slots) * width, width), width),
        ]

    for t in range(width // slots):
        out = slice(t * slots, (t + 1) * slots)
        r.act[:, t * width : (t + 1) * width] = dot(
            r.attended[:, out], r.block_out[...], TN
        ).astype(BF)

    def to_sibling(k):
        at = partners[k]
        return to_partner(
            wo_rows(r.act, at), wo_rows(r.grad_pre, at), r.w_ss.at[k], r.w_rs.at[k], 1
        )

    def to_owner(k):
        return to_partner(
            wo_rows(r.act, partners[k]),
            wo_rows(r.grad_pre, partners[1]),
            r.w_ss.at[k],
            r.w_rs.at[k],
            k,
        )

    for copy in a_copies:
        copy.wait()
    normed_gather.middle()
    p_copies = [blocks_out(r.x_send, r.p_recv, (r.p_ss, r.p_rs), k) for k in order]
    for copy in p_copies:
        copy.start()

    for k in range(1, n, 2):
        to_sibling(k).start()

    def wo_across():
        for k in range(1, n, 2):
            to_sibling(k).wait()
        for k in [0] + direct:
            mine_k = wo_rows(r.act, partners[k])
            mine_k[...] = (
                mine_k[...].astype(F32) + wo_rows(r.grad_pre, partners[k])[...].astype(F32)
            ).astype(BF)
        for k in direct:
            to_owner(k).start()

    for p in range(3):
        for k in order:
            to_heads(p, k).wait_send()
    for t in range(1, n):
        home(t).wait_send()
    for i in range(n):
        both = (r.grad_att[i].astype(F32) * r.att_heads[i].astype(F32)).T
        size = own // r.heads
        deltas = [
            jnp.sum(both[h * size : (h + 1) * size], axis=0, keepdims=True) for h in range(r.heads)
        ]
        r.delta[i] = jnp.concatenate(
            deltas + [jnp.zeros((SMALL - r.heads, rows), F32)], axis=0
        )
    r.grad_q_t[...] = jnp.zeros(r.grad_q_t.shape, F32)

    def back_home(p, t):
        target = lax.rem(me + t, n)
        return send(
            r.qkv_send.at[p, target],
            r.grad_tok.at[p, me],
            r.d_ss.at[p, t],
            r.d_rs.at[p, t],
            {"ep": target},
        )

    def back_step(t, _):
        attend_back(r, lax.rem(me + t, n), n)
        pl.when(t == 1)(wo_across)

        @pl.when(t > 0)
        def _():
            for p in (1, 2):
                back_home(p, t).start()

        return 0

    lax.fori_loop(0, n, back_step, 0)
    for i in range(n):
        r.qkv_send[0, i] = (r.grad_q_t[i].T * ((own // r.heads) ** -0.5)).astype(BF)
    for t in range(1, n):
        back_home(0, t).start()
    for p in range(3):
        r.grad_tok[p, me] = r.qkv_send[p, me]
    normed_gather.last()

    def o_place(e, d):
        at = pl.ds(pl.multiple_of(e * own, own), own)
        piece = width // c
        if d is None:
            return r.o_all.at[at, :]
        return r.o_all.at[at, pl.ds(pl.multiple_of(d * piece, piece), piece)]

    def o_halves(e):
        at = pl.ds(pl.multiple_of(e * own, own), own)
        return [r.o_all.at[at, pl.ds(0, half)], r.o_all.at[at, pl.ds(half, half)]]

    def q_place(first, e, d):
        piece = TILE // c
        if d is None:
            return r.q_all.at[:, e, pl.ds(first, TILE), :]
        return r.q_all.at[:, e, pl.ds(pl.multiple_of(first + d * piece, piece), piece), :]

    def q_halves(first, e):
        return [
            r.q_all.at[:, e, pl.ds(first, TILE // 2), :],
            r.q_all.at[:, e, pl.ds(first + TILE // 2, TILE // 2), :],
        ]

    o_spread = Spread(r, "wo", me, grp, n, c, o_place, o_halves)
    q_spreads = [
        Spread(
            r,
            "wq" + str(t),
            me,
            grp,
            n,
            c,
            functools.partial(q_place, t * TILE),
            functools.partial(q_halves, t * TILE),
        )
        for t in range(width // TILE)
    ]

    normed_gather.finish()
    mine.wait()
    at_once = width // rows
    turns = n // at_once

    def normed_loads(t):
        out = []
        for b in range(turns):
            spot = (t if turns <= 2 else b // 2) * TILE
            for s in range(at_once):
                out.append(
                    pltpu.make_async_copy(
                        r.normed_all.at[b * at_once + s, :, pl.ds(t * TILE, TILE)],
                        r.space.at[
                            pl.ds((b % 2) * width + s * rows, rows), pl.ds(spot, TILE)
                        ],
                        r.slab_sem.at[t % 2, b * at_once + s],
                    )
                )
        return out

    for t in range(width // TILE if turns <= 2 else 1):
        for load in normed_loads(t):
            load.start()
    for t, spread in enumerate(q_spreads):
        if turns > 2 and t:
            for load in normed_loads(t):
                load.start()
        for load in normed_loads(t):
            load.wait()
        total = None
        for b in range(turns):
            spot = (t if turns <= 2 else b // 2) * TILE
            grads = jnp.concatenate(
                [flat(r.qkv_send[p, b * at_once : (b + 1) * at_once]) for p in range(3)], axis=1
            )
            term = dot(
                r.space[(b % 2) * width : (b % 2 + 1) * width, spot : spot + TILE], grads, TN
            )
            total = term if b == 0 else total + term
        low = total.astype(BF)
        piece = TILE // c
        for d in range(c):
            for p in range(3):
                spread.send_buf[d, p] = low[
                    d * piece : (d + 1) * piece, p * own : (p + 1) * own
                ]
        if t == 0:
            spread.scatter()

    for k in direct:
        to_owner(k).wait()
    total = wo_rows(r.act, me)[...].astype(F32)
    for k in direct:
        total = total + wo_rows(r.grad_pre, partners[k + 1])[...].astype(F32)
    for d in range(c):
        r.wo_send[d] = total[:, d * (width // c) : (d + 1) * (width // c)].astype(BF)
    o_spread.scatter()

    for copy in p_copies:
        copy.wait()
    for t in range(width // TILE):
        cols = slice(t * TILE, (t + 1) * TILE)
        r.block_out[:, cols] = (
            r.hidden[:, cols] + dot(r.place[...], flat(r.p_recv[:, :, cols]), TN)
        ).astype(BF)


    def slab_loads(q):
        at = partner(grp, q, c)
        base = (q % 2) * width
        out = []
        for which, src in enumerate((r.x_all, r.g_all)):
            for s in range(n):
                out.append(
                    pltpu.make_async_copy(
                        src.at[at, s],
                        r.space.at[pl.ds(base + which * slots + s * cap, cap), :],
                        r.slab_sem.at[q % 2, which * n + s],
                    )
                )
        return out

    def slab_start(q):
        g_line.wait(partner(grp, q, c))
        x_line.wait(partner(grp, q, c))
        for load in slab_loads(q):
            load.start()

    def slab(q, beside=lambda: None):
        base = (q % 2) * width
        for load in slab_loads(q):
            load.wait()
        x_rows, g_rows = r.space.at[pl.ds(base, slots), :], r.space.at[pl.ds(base + slots, slots), :]

        def activate(out):
            at = pl.ds(pl.multiple_of(mine_at + out.start, TILE), TILE)
            cols = pl.ds(pl.multiple_of(3 * width + out.start, TILE), TILE)
            r.grad_pre[:, cols] = dot(g_rows[...], r.w_out_v[at, :], NT).astype(BF)
            pre = dot(x_rows[...], r.w_in_v[at, :], NT)
            for q in range(slots // CHUNK):
                some = slice(q * CHUNK, (q + 1) * CHUNK)
                act, slope = gelu_both(pre[some])
                r.act[some, cols] = act.astype(BF)
                r.grad_pre[some, cols] = (r.grad_pre[some, cols].astype(F32) * slope).astype(BF)

        tiles(part, activate)
        beside()
        weight_terms(
            3 * width, lambda cols: x_rows[:, cols], lambda cols: g_rows[:, cols], False
        )

    slab_start(1)

    slab(1)

    q_spreads[0].total()
    for spread in q_spreads[1:]:
        spread.scatter()
    o_spread.total()
    last_loads = load_qkv(0)
    for load in last_loads:
        load.start()

    for p in (1, 2, 0):
        for t in range(1, n):
            back_home(p, t).wait_recv()
    for load in last_loads:
        load.wait()

    for p in range(3):
        for e in range(n):
            r.attended[:, e * own : (e + 1) * own] = r.grad_tok[p, e]
        cols = slice(p * width, (p + 1) * width)
        for at, weight in enumerate((r.act, r.grad_pre)):
            out = slice(at * half, (at + 1) * half)
            term = dot(r.attended[...], weight[:, cols], NT)
            r.hidden[:, out] = term if p == 0 else r.hidden[:, out] + term

    def store_tokens(at, grad_in):
        r.grad_tokens[at, :] += grad_in

    sums = norm_back(r.tokens, r.hidden, r.gain_attn, store_tokens)
    r.small_own[0:1], r.small_own[1:2] = sums

    def small_ep(k):
        return to_partner(r.small_own, r.small_ep.at[me], r.s_ss.at[0, k], r.s_rs.at[0, k], k)

    def small_dp(t):
        return send(
            r.small_sum,
            r.small_dp.at[grp],
            r.s_ss.at[1, t],
            r.s_rs.at[1, t],
            {"dp": lax.rem(grp + t, c)},
        )

    for k in order:
        small_ep(k).start()
    r.small_ep[me] = r.small_own[...]

    q_spreads[0].over()

    for spread in q_spreads[1:]:
        spread.total()
    x_line.hand_on(*range(2, c))

    if c > 3:
        slab_start(2)
        slab(2, q_spreads[0].gather.middle)
    else:
        q_spreads[0].gather.middle()

    for spread in [o_spread] + q_spreads[1:]:
        spread.over()

    for q in range(3, c - 1):
        slab_start(q)
        slab(q)
    out_copies = []
    for at, (src, dst) in enumerate(((r.sum_in, r.grad_in), (r.sum_out, r.grad_out))):
        base = at * width
        for s in range(0, part, CHUNK * 4):
            r.space[base + s : base + s + CHUNK * 4, :] = src[s : s + CHUNK * 4, :].astype(BF)
        out_copies.append(
            pltpu.make_async_copy(
                r.space.at[pl.ds(base, part), :], dst, r.load_sem.at[at]
            )
        )
    for copy in out_copies:
        copy.start()

    for k in order:
        small_ep(k).wait()
    total = r.small_ep[0]
    for e in range(1, n):
        total = total + r.small_ep[e]
    r.small_sum[...] = total
    for t in range(1, c):
        small_dp(t).start()
    r.small_dp[grp] = total

    spreads = q_spreads + [o_spread]
    q_spreads[0].gather.last()

    for spread in spreads[1:]:
        spread.gather.middle()

    for spread in spreads[1:]:
        spread.gather.last()

    for t in range(1, c):
        small_dp(t).wait()
    total = r.small_dp[0]
    for d in range(1, c):
        total = total + r.small_dp[d]
    r.small[...] = total
    last = partner(grp, c - 1, c)
    g_line.wait(last)
    x_line.wait(last)
    g_line.finish()
    x_line.finish()
    for copy in out_copies:
        copy.wait()
    for spread in spreads:
        spread.finish()
    for p in range(3):
        for t in range(1, n):
            back_home(p, t).wait_send()


def block_call(n, c, heads, operands):
    rows, width = operands["tokens"].shape
    hidden = operands["w_in"].shape[1]
    own, cap, part, piece = width // n, 2 * rows // n, hidden // c, width // c
    slots = n * cap
    vm, hb = pl.BlockSpec(memory_space=pltpu.VMEM), pl.BlockSpec(memory_space=pl.ANY)
    sm = pl.BlockSpec(memory_space=pltpu.SMEM)
    inputs = dict(
        lengths=sm, ids=vm, tokens=vm, cotangent=vm, gain_attn=vm, shift_attn=vm, gain_ffn=vm,
        shift_ffn=vm, w_qkv=hb, w_o=hb, w_in=hb, w_out=hb,
    )
    outputs = dict(
        block_out=((rows, width), BF, vm),
        grad_tokens=((rows, width), F32, vm),
        q_all=((3, n, width, own), BF, hb),
        o_all=((width, width), BF, hb),
        small=((SMALL, width), F32, vm),
        grad_in=((part, width), BF, hb),
        grad_out=((part, width), BF, hb),
        g_all=((c, n, cap, width), BF, hb),
        x_all=((c, n, cap, width), BF, hb),
        normed_all=((n, rows, width), BF, hb),
    )

    def v(*shape):
        return pltpu.VMEM(shape, BF)

    def f(*shape):
        return pltpu.VMEM(shape, F32)

    def d(*shape):
        return pltpu.SemaphoreType.DMA(shape)

    heads_shape = (n, rows, own)
    scratch = dict(
        sum_in=f(part, width), sum_out=f(part, width),
        w_o_v=v(width, width), w_in_v=v(hidden, width), w_out_v=v(hidden, width),
        act=v(slots, hidden), grad_pre=v(slots, hidden), space=v(2 * width, width),
        normed=v(rows, width), place=v(slots, rows), hidden=f(rows, width),
        attended=v(rows, width),
        qkv_send=v(3, *heads_shape), qkv_heads=v(3, *heads_shape), grad_tok=v(3, *heads_shape),
        values_t=v(n, own, rows), att_heads=v(*heads_shape), att_recv=v(*heads_shape),
        grad_att=v(*heads_shape), grad_q_t=f(n, own, rows),
        lse=f(n, SMALL, rows), delta=f(n, SMALL, rows),
        g_send=v(n, cap, width), x_send=v(n, cap, width), g_own=v(n, cap, width),
        x_own=v(n, cap, width), r_recv=v(n, cap, width), p_recv=v(n, cap, width),
        wo_send=v(c, own, piece), wo_recv=v(c, own, piece), wo_fin=v(own, piece),
        small_own=f(SMALL, width), small_ep=f(n, SMALL, width), small_sum=f(SMALL, width),
        small_dp=f(c, SMALL, width),
        load_sem=d(8), slab_sem=d(2, 2 * n),
        a_ss=d(3, n), a_rs=d(3, n), g_ss=d(2, n), g_rs=d(2, n), n_ss=d(n + 2), n_rs=d(n + 2),
        o_ss=d(n), o_rs=d(n), x_ss=d(n), x_rs=d(n), r_ss=d(n), r_rs=d(n), p_ss=d(n), p_rs=d(n),
        b_ss=d(n), b_rs=d(n), w_ss=d(n), w_rs=d(n), d_ss=d(3, n), d_rs=d(3, n),
        gz_ss=d(2, c, 2), gz_rs=d(c, 2), xz_ss=d(2, c, 1), xz_rs=d(c, 1),
        wo_ss=d(2, c), wo_rs=d(2, c), wo_ys=d(n + 2), wo_yr=d(n + 2), wo_ls=d(1),
        s_ss=d(2, max(n, c)), s_rs=d(2, max(n, c)),
    )
    for t in range(width // TILE):
        name = "wq" + str(t)
        piece = TILE // c
        scratch[name + "_send"] = scratch[name + "_recv"] = v(c, 3, piece, own)
        scratch[name + "_fin"] = v(3, piece, own)
        scratch[name + "_ss"] = scratch[name + "_rs"] = d(2, c)
        scratch[name + "_ys"] = scratch[name + "_yr"] = d(n + 2)
        scratch[name + "_ls"] = d(1)
    names = list(inputs) + list(outputs) + list(scratch)

    def kernel(*refs):
        r = types.SimpleNamespace(**dict(zip(names, refs)))
        r.heads = heads
        block_kernel(r, n, c)

    result = pl.pallas_call(
        kernel,
        out_shape=[jax.ShapeDtypeStruct(shape, kind) for shape, kind, _ in outputs.values()],
        in_specs=list(inputs.values()),
        out_specs=[spec for _, _, spec in outputs.values()],
        scratch_shapes=list(scratch.values()),
        compiler_params=pltpu.CompilerParams(
            collective_id=0, has_side_effects=True, vmem_limit_bytes=VMEM_LIMIT
        ),
    )(*[operands[name] for name in inputs])
    return dict(zip(outputs, result))


VMEM_LIMIT = 64 << 20
STEPS = 2


def widen_kernel(where, q_all, o_all, sum_in, sum_out, block, tokens, small, *rest):
    x_rows, g_rows, w_in, w_out, q_out, o_out, grad_in, grad_out, block_out, tokens_out = rest[:10]
    n, own = q_all.shape[1], q_all.shape[3]
    x_rows, g_rows = flat(x_rows[0]), flat(g_rows[0])
    pre = dot(x_rows, w_in[0], NT)
    grad_act = dot(g_rows, w_out[0], NT)
    acts, grads = [], []
    for q in range(x_rows.shape[0] // CHUNK):
        at = slice(q * CHUNK, (q + 1) * CHUNK)
        act, slope = gelu_both(pre[at])
        acts.append(act.astype(BF))
        grads.append((grad_act[at] * slope).astype(BF))
    grad_in[0] = sum_in[...].astype(F32) + dot(jnp.concatenate(grads, axis=0), x_rows, TN)
    grad_out[0] = sum_out[...].astype(F32) + dot(jnp.concatenate(acts, axis=0), g_rows, TN)
    for p in range(3):
        for e in range(n):
            at = (p * n + e) * own
            q_out[:, at : at + own] = q_all[p, e].astype(F32)
    o_out[...] = o_all[...].astype(F32)
    block_out[...] = block[...]
    tokens_out[...] = tokens[...]
    for at, one in enumerate(rest[10:]):
        one[...] = small[at : at + 1, :]


def widen(out, w_in, w_out):
    q_all, o_all, sum_in, block = out["q_all"], out["o_all"], out["grad_in"], out["block_out"]
    x_all = out["x_all"]
    c = x_all.shape[0]
    _, n, width, own = q_all.shape
    part, rows = sum_in.shape[0], block.shape[0]
    S = jax.ShapeDtypeStruct
    grp = lax.axis_index("dp")
    where = jnp.stack([partner(grp, c - 1, c), grp * STEPS]).astype(jnp.int32)

    def rowwise(count):
        return pl.BlockSpec((count // STEPS, width), lambda i, w: (i, 0))

    expert = pl.BlockSpec((1, part // STEPS, width), lambda i, w: (0, i, 0))
    weight = pl.BlockSpec((1, part // STEPS, width), lambda i, w: (0, w[1] + i, 0))
    group = pl.BlockSpec((1, *x_all.shape[1:]), lambda i, w: (w[0], 0, 0, 0))
    fixed = pl.BlockSpec((1, width), lambda i, w: (0, 0))
    return pl.pallas_call(
        widen_kernel,
        grid_spec=pltpu.PrefetchScalarGridSpec(
            num_scalar_prefetch=1,
            grid=(STEPS,),
            in_specs=[
                pl.BlockSpec((3, n, width // STEPS, own), lambda i, w: (0, 0, i, 0)),
                rowwise(width), rowwise(part), rowwise(part), rowwise(rows), rowwise(rows),
                pl.BlockSpec((SMALL, width), lambda i, w: (0, 0)), group, group, weight, weight,
            ],
            out_specs=[
                pl.BlockSpec((width // STEPS, 3 * width), lambda i, w: (i, 0)),
                rowwise(width), expert, expert, rowwise(rows), rowwise(rows),
            ] + [fixed] * 4,
        ),
        out_shape=[
            S((width, 3 * width), F32), S((width, width), F32), S((1, part, width), F32),
            S((1, part, width), F32), S((rows, width), BF), S((rows, width), F32),
        ] + [S((1, width), F32)] * 4,
        compiler_params=pltpu.CompilerParams(vmem_limit_bytes=VMEM_LIMIT),
    )(
        where, q_all, o_all, sum_in, out["grad_out"], block, out["grad_tokens"], out["small"],
        x_all, out["g_all"], w_in, w_out,
    )


def on_device(
    tokens,
    gain_attn,
    shift_attn,
    w_qkv,
    w_o,
    gain_ffn,
    shift_ffn,
    w_in,
    w_out,
    seq_lengths,
    expert_ids,
    cotangent,
):
    rows, width = tokens.shape
    n, c = lax.axis_size("ep"), lax.axis_size("dp")
    operands = dict(
        lengths=seq_lengths,
        ids=expert_ids.reshape(1, rows),
        tokens=tokens,
        cotangent=cotangent,
        gain_attn=gain_attn[None],
        shift_attn=shift_attn[None],
        gain_ffn=gain_ffn[None],
        shift_ffn=shift_ffn[None],
        w_qkv=w_qkv,
        w_o=w_o,
        w_in=w_in,
        w_out=w_out,
    )
    out = block_call(n, c, HEADS // n, operands)
    q_out, o_out, in_out, out_out, block, tokens_out, *small = widen(out, w_in, w_out)
    small = [one.reshape(width) for one in small]
    return (block, tokens_out, q_out, o_out, *small, in_out, out_out)


def solution(mesh):
    return jax.shard_map(
        on_device,
        mesh=mesh,
        in_specs=(
            P(("dp", "ep"), None),
            P(),
            P(),
            P(),
            P(),
            P(),
            P(),
            P("ep", None, None),
            P("ep", None, None),
            P("dp", None),
            P(("dp", "ep"), None),
            P(("dp", "ep"), None),
        ),
        out_specs=(
            P(("dp", "ep"), None),
            P(("dp", "ep"), None),
            P(),
            P(),
            P(),
            P(),
            P(),
            P(),
            P("ep", "dp", None),
            P("ep", "dp", None),
        ),
        check_vma=False,
    )
```

```python
import functools
import types

import jax
import jax.numpy as jnp
from jax import lax
from jax.experimental import pallas as pl
from jax.experimental.pallas import tpu as pltpu
from jax.sharding import PartitionSpec as P

HEADS = 16
EPSILON = 1e-05
MASKED = -1e30
TILE = 512
SMALL = 8
UNROLLED = 8
AT_ONCE = 4
MESH = pl.DeviceIdType.MESH
F32 = jnp.float32
BF = jnp.bfloat16
NN = (((1,), (0,)), ((), ()))
NT = (((1,), (1,)), ((), ()))
TN = (((0,), (0,)), ((), ()))


def dot(left, right, dims):
    return lax.dot_general(left, right, dims, preferred_element_type=F32)


def partner(me, k, n):
    out, weight = 0, 1
    while weight < n:
        bit = lax.rem(lax.div(me, weight), 2)
        out = out + (lax.rem(bit + 1, 2) if k & weight else bit) * weight
        weight *= 2
    return out


def send(src, dst, send_sem, recv_sem, target):
    return pltpu.make_async_remote_copy(
        src_ref=src,
        dst_ref=dst,
        send_sem=send_sem,
        recv_sem=recv_sem,
        device_id=target,
        device_id_type=MESH,
    )


def order_of(n):
    return sorted(range(1, n), key=lambda k: (-bin(k // 2).count("1"), k))


def flat(value):
    return value.reshape(value.shape[0] * value.shape[1], value.shape[2])


def tiles(count, body, beside=None):
    def step(t, _):
        body(pl.ds(pl.multiple_of(t * TILE, TILE), TILE))
        for at, act in (beside or {}).items():
            pl.when(t == at)(act)
        return 0

    lax.fori_loop(0, count // TILE, step, 0)


def norm_rows(rows_in):
    average = jnp.mean(rows_in, axis=-1, keepdims=True)
    centered = rows_in - average
    inv_std = lax.rsqrt(jnp.mean(centered * centered, axis=-1, keepdims=True) + EPSILON)
    return centered * inv_std, inv_std


CHUNK = 32


def by_rows(count, body, carry=0):
    def step(i, state):
        return body(pl.ds(pl.multiple_of(i * CHUNK, CHUNK), CHUNK), state)

    return lax.fori_loop(0, count // CHUNK, step, carry)


def norm_apply(src, gain, shift, dst):
    def body(at, _):
        unit, _ = norm_rows(src[at, :].astype(F32))
        dst[at, :] = (unit * gain[...] + shift[...]).astype(BF)
        return 0

    by_rows(src.shape[0], body)


def norm_back(src, grad, gain, store):
    def body(at, sums):
        unit, inv = norm_rows(src[at, :].astype(F32))
        incoming = grad[at, :]
        grad_unit = incoming * gain[...]
        grad_in = inv * (
            grad_unit
            - jnp.mean(grad_unit, axis=-1, keepdims=True)
            - unit * jnp.mean(grad_unit * unit, axis=-1, keepdims=True)
        )
        store(at, grad_in)
        return (
            sums[0] + jnp.sum(incoming * unit, axis=0, keepdims=True),
            sums[1] + jnp.sum(incoming, axis=0, keepdims=True),
        )

    zero = jnp.zeros((1, src.shape[1]), F32)
    return by_rows(src.shape[0], body, (zero, zero))


def gelu_both(pre):
    square = pre * pre
    bent = jnp.tanh(0.7978845608028654 * pre * (1.0 + 0.044715 * square))
    half = 0.5 + 0.5 * bent
    rise = 0.7978845608028654 * (1.0 + 3 * 0.044715 * square)
    return pre * half, half + 0.5 * pre * (1.0 - bent * bent) * rise


def place_matrix(ids_row, n, cap):
    rows = ids_row.shape[1]
    expert = lax.broadcasted_iota(jnp.int32, (n, rows), 0)
    hit = (expert == ids_row).astype(F32)
    before = lax.broadcasted_iota(jnp.int32, (rows, rows), 0)
    after = lax.broadcasted_iota(jnp.int32, (rows, rows), 1)
    upto = (before <= after).astype(F32).astype(BF)
    count = dot(hit.astype(BF), upto, NN)
    slot = jnp.sum(hit * (count - 1.0), axis=0, keepdims=True)
    target = ids_row * cap + slot.astype(jnp.int32)
    places = lax.broadcasted_iota(jnp.int32, (n * cap, rows), 0)
    return (places == target).astype(F32).astype(BF)


def start_row(len_ref, first, width):
    pos = first + lax.broadcasted_iota(jnp.int32, (1, width), 1)
    start = jnp.zeros((1, width), jnp.int32)
    edge = jnp.int32(0)
    for s in range(len_ref.shape[1] - 1):
        edge = edge + len_ref[0, s]
        start = jnp.where(pos >= edge, edge, start)
    return pos, start


def split_heads(block, heads):
    if heads == 1:
        return [block]
    size = block.shape[1] // heads
    lane = lax.broadcasted_iota(jnp.int32, block.shape, 1)
    zero = jnp.zeros_like(block)
    return [
        jnp.where((lane >= h * size) & (lane < (h + 1) * size), block, zero) for h in range(heads)
    ]


def attend_block(r, i):
    rows, own = r.qkv_heads.shape[2:]
    heads = r.heads
    size = own // heads
    queries = split_heads(r.qkv_heads[0, i] * BF(size**-0.5), heads)
    pos, start = start_row(r.lengths, i * rows, rows)
    outs, sums = [], []
    for h in range(heads):
        top = jnp.full((1, rows), MASKED, F32)
        total = jnp.zeros((1, rows), F32)
        accum = jnp.zeros((size, rows), F32)
        for last in range(i, -1, -AT_ONCE):
            scores = []
            blocks = range(last, max(last - AT_ONCE, -1), -1)
            for j in blocks:
                key = j * rows + lax.broadcasted_iota(jnp.int32, (rows, rows), 0)
                allowed = key >= start
                if j == i:
                    allowed = allowed & (key <= pos)
                scores.append(
                    jnp.where(allowed, dot(r.qkv_heads[1, j], queries[h], NT), MASKED)
                )
            peak = functools.reduce(
                jnp.maximum, [jnp.max(s.reshape(rows // 8, 8, rows), axis=0) for s in scores]
            )
            new_top = jnp.maximum(top, jnp.max(peak, axis=0, keepdims=True))
            decay = jnp.exp(top - new_top)
            accum = accum * decay
            part = jnp.zeros((8, rows), F32)
            for j, s in zip(blocks, scores):
                weights = jnp.exp(s - new_top)
                part = part + jnp.sum(weights.reshape(rows // 8, 8, rows), axis=0)
                values = r.values_t[j, h * size : (h + 1) * size, :]
                accum = accum + dot(values, weights.astype(BF), NN)
            total = total * decay + jnp.sum(part, axis=0, keepdims=True)
            top = new_top
        outs.append(accum / total)
        sums.append(top + jnp.log(total))
    r.att_heads[i] = jnp.concatenate(outs, axis=0).T.astype(BF)
    r.lse[i] = jnp.concatenate(sums + [jnp.zeros((SMALL - heads, rows), F32)], axis=0)


def attend_back(r, j, n):
    rows, own = r.qkv_heads.shape[2:]
    heads = r.heads
    size = own // heads
    keys, values = r.qkv_heads[1, j], r.qkv_heads[2, j]
    keys_t = keys.astype(F32).T.astype(BF)

    def fold(at, carry, diagonal):
        grad_k, grad_v = carry
        for i in at:
            queries = split_heads(r.qkv_heads[0, i] * BF(size**-0.5), heads)
            grads = split_heads(r.grad_att[i], heads)
            pos, start = start_row(r.lengths, i * rows, rows)
            key = j * rows + lax.broadcasted_iota(jnp.int32, (rows, rows), 0)
            allowed = key >= start
            if diagonal:
                allowed = allowed & (key <= pos)
            for h in range(heads):
                scores = dot(keys, queries[h], NT)
                probs = jnp.where(allowed, jnp.exp(scores - r.lse[i, h : h + 1, :]), 0.0)
                grad_probs = dot(values, grads[h], NT)
                grad_scores = (probs * (grad_probs - r.delta[i, h : h + 1, :])).astype(BF)
                grad_v = grad_v + dot(probs.astype(BF), grads[h], NN)
                grad_k = grad_k + dot(grad_scores, queries[h], NN)
                part = slice(h * size, (h + 1) * size)
                r.grad_q_t[i, part, :] += dot(keys_t[part, :], grad_scores, NN)
        return grad_k, grad_v

    zero = jnp.zeros((rows, own), F32)
    carry = fold([j], (zero, zero), True)
    left = n - 1 - j
    odd = lax.rem(left, 2)
    carry = lax.fori_loop(j + 1, j + 1 + odd, lambda i, carry: fold([i], carry, False), carry)

    def pair(t, carry):
        i = j + 1 + odd + 2 * t
        return fold([i, i + 1], carry, False)

    grad_k, grad_v = lax.fori_loop(0, lax.div(left, 2), pair, carry)
    r.qkv_send[1, j] = grad_k.astype(BF)
    r.qkv_send[2, j] = grad_v.astype(BF)


def attend_block_loop(r, i):
    rows, own = r.qkv_heads.shape[2:]
    heads = r.heads
    size = own // heads
    queries = split_heads(r.qkv_heads[0, i] * BF(size**-0.5), heads)
    pos, start = start_row(r.lengths, i * rows, rows)

    def fold(j, carry, diagonal):
        keys = r.qkv_heads[1, j]
        key = j * rows + lax.broadcasted_iota(jnp.int32, (rows, rows), 0)
        allowed = key >= start
        if diagonal:
            allowed = allowed & (key <= pos)
        out = []
        for h in range(heads):
            top, total, accum = carry[h]
            scores = jnp.where(allowed, dot(keys, queries[h], NT), MASKED)
            new_top = jnp.maximum(top, jnp.max(scores, axis=0, keepdims=True))
            weights = jnp.exp(scores - new_top)
            if diagonal:
                weights = jnp.where(allowed, weights, 0.0)
            decay = jnp.exp(top - new_top)
            total = total * decay + jnp.sum(weights, axis=0, keepdims=True)
            values = r.values_t[j, h * size : (h + 1) * size, :]
            accum = accum * decay + dot(values, weights.astype(BF), NN)
            out.append((new_top, total, accum))
        return tuple(out)

    state = tuple(
        (
            jnp.full((1, rows), MASKED, F32),
            jnp.zeros((1, rows), F32),
            jnp.zeros((size, rows), F32),
        )
        for _ in range(heads)
    )
    state = fold(i, state, True)
    state = lax.fori_loop(0, i, lambda j, carry: fold(j, carry, False), state)
    result = jnp.concatenate([accum / total for _, total, accum in state], axis=0)
    r.att_heads[i] = result.T.astype(BF)
    sums = [top + jnp.log(total) for top, total, _ in state]
    r.lse[i] = jnp.concatenate(sums + [jnp.zeros((SMALL - heads, rows), F32)], axis=0)


class Line:
    def __init__(self, block, whole, send_sem, recv_sem, at, c, parts):
        self.block, self.whole, self.at, self.c = block, whole, at, c
        self.send_sem, self.recv_sem, self.parts = send_sem, recv_sem, parts

    def can(self, index):
        return (index >= 0) & (index < self.c)

    def rows(self, ref, part):
        size = self.block.shape[1] // self.parts
        return ref.at[:, pl.ds(part * size, size), :]

    def copy(self, way, stage, part):
        held, target = self.at - way * stage, self.at + way
        dst = self.rows(self.whole.at[held], part)
        return self.can(held) & self.can(target), send(
            dst if stage else self.rows(self.block, part),
            dst,
            self.send_sem.at[(way + 1) // 2, stage, part],
            self.recv_sem.at[held, part],
            {"dp": target},
        )

    def each(self, stages):
        for stage in stages:
            for part in range(self.parts):
                for way in (-1, 1):
                    yield self.copy(way, stage, part)

    def start(self, part):
        for way in (-1, 1):
            allowed, copy = self.copy(way, 0, part)
            pl.when(allowed)(copy.start)

    def hand_on(self, *stages):
        for allowed, copy in self.each([s for s in stages if s < self.c - 1]):

            @pl.when(allowed)
            def _():
                copy.wait_recv()
                copy.start()

    def wait(self, block):
        done = ((block < self.at) & self.can(self.at + 1)) | (
            (block > self.at) & self.can(self.at - 1)
        )

        @pl.when(jnp.logical_not(done))
        def _():
            for part in range(self.parts):
                src = self.rows(self.whole.at[block], part)
                recv = self.recv_sem.at[block, part]
                send(src, src, self.send_sem.at[0, 0, 0], recv, {"dp": block}).wait_recv()

    def finish(self):
        for allowed, copy in self.each(range(self.c - 1)):
            pl.when(allowed)(copy.wait_send)


class Gather:
    def __init__(self, own, place, halves, send_sem, recv_sem, me, n):
        self.own, self.place, self.halves = own, place, halves
        self.send_sem, self.recv_sem, self.me, self.n = send_sem, recv_sem, me, n
        self.direct = [k for k in order_of(n) if k % 2 == 0]
        self.relayed = n == 8
        self.near = [2, 4] if self.relayed else self.direct

    def to(self, src, dst, at, k):
        return send(
            src, dst, self.send_sem.at[at], self.recv_sem.at[at], {"ep": partner(self.me, k, self.n)}
        )

    def across(self, k):
        return self.to(self.own, self.place(self.me), k, k)

    def relay(self, k):
        half = self.halves(partner(self.me, k, self.n))[k // 4]
        return self.to(half, half, self.n + k // 4, 6 - k)

    def pass_on(self, k):
        block = self.place(partner(self.me, k, self.n))
        return self.to(block, block, k + 1, 1)

    def start(self):
        for k in self.near + [1]:
            self.across(k).start()

    def middle(self):
        for k in self.near:
            self.across(k).wait_recv()
            if self.relayed:
                self.relay(k).start()
            self.pass_on(k).start()

    def last(self):
        if self.relayed:
            for k in (2, 4):
                self.relay(k).wait_recv()
            self.pass_on(6).start()

    def finish(self):
        self.across(1).wait()
        for k in self.near:
            self.across(k).wait_send()
            if self.relayed:
                self.relay(k).wait_send()
        for k in self.direct:
            self.pass_on(k).wait()


def owners_of(c):
    return (c // 2 - 1, c // 2) if c <= 4 else tuple(range(c))


class Spread:
    def __init__(self, r, name, me, grp, n, c, place, halves, source):
        self.recv_buf, self.final, self.ss, self.rs, ys, yr, self.local = (
            getattr(r, name + part) for part in ("_recv", "_fin", "_ss", "_rs", "_ys", "_yr", "_ls")
        )
        self.source = source
        self.me, self.grp, self.c, self.place = me, grp, c, place
        self.owners = owners_of(c)
        self.gather = Gather(
            place(me, None), lambda e: place(e, None), halves, ys, yr, me, n
        )

    def to_owner(self, half):
        return send(
            self.source(half),
            self.recv_buf.at[self.grp],
            self.ss.at[0, half],
            self.rs.at[0, self.grp],
            {"dp": self.owners[half]},
        )

    def from_source(self, source):
        return send(
            self.source(0),
            self.recv_buf.at[source],
            self.ss.at[0, 0],
            self.rs.at[0, source],
            {"dp": source},
        )

    def to_copies(self, half, target):
        return send(
            self.final,
            self.place(self.me, half),
            self.ss.at[1, target],
            self.rs.at[1, half],
            {"dp": target},
        )

    def mine(self, half):
        return pltpu.make_async_copy(self.final, self.place(self.me, half), self.local.at[0])

    def scatter(self):
        for half, owner in enumerate(self.owners):
            pl.when(self.grp != owner)(self.to_owner(half).start)

            @pl.when(self.grp == owner)
            def _():
                self.recv_buf[owner] = self.source(half)[...]

    def total(self):
        for half, owner in enumerate(self.owners):

            @pl.when(self.grp == owner)
            def _():
                for s in range(self.c):
                    if s != owner:
                        self.from_source(s).wait_recv()
                total = self.recv_buf[0].astype(F32)
                for s in range(1, self.c):
                    total = total + self.recv_buf[s].astype(F32)
                self.final[...] = total.astype(BF)
                for s in range(self.c):
                    if s != owner:
                        self.to_copies(half, s).start()
                self.mine(half).start()

    def over(self):
        for half, owner in enumerate(self.owners):
            pl.when(self.grp != owner)(self.to_copies(half, owner).wait_recv)
            pl.when(self.grp == owner)(self.mine(half).wait)
        self.gather.start()

    def finish(self):
        self.gather.finish()
        for half, owner in enumerate(self.owners):
            pl.when(self.grp != owner)(self.to_owner(half).wait_send)

            @pl.when(self.grp == owner)
            def _():
                for s in range(self.c):
                    if s != owner:
                        self.to_copies(half, s).wait_send()


def block_kernel(r, n, c):
    me, grp = lax.axis_index("ep"), lax.axis_index("dp")
    rows, width = r.tokens.shape
    own, cap = width // n, 2 * rows // n
    slots = n * cap
    hidden = r.w_in.shape[1]
    part = hidden // c
    order = order_of(n)
    direct = [k for k in order if k % 2 == 0]
    partners = {k: partner(me, k, n) for k in range(n)}
    half = width // 2
    listed = [0, 1, 6, 7, 2, 3, 4, 5] if n == 8 else list(range(n))
    spot = {k: at for at, k in enumerate(listed)}

    def to_partner(src, dst, send_sem, recv_sem, k):
        return send(src, dst, send_sem, recv_sem, {"ep": partners[k]})

    def blocks_out(buf, dst, sems, k):
        return to_partner(buf.at[partners[k]], dst.at[me], sems[0].at[k], sems[1].at[k], k)

    def to_expert(buf, dst, sems, k):
        return to_partner(buf.at[partners[k]], dst.at[spot[k]], sems[0].at[k], sems[1].at[k], k)

    def from_expert(buf, dst, sems, k):
        return to_partner(buf.at[spot[k]], dst.at[me], sems[0].at[k], sems[1].at[k], k)

    barrier = pltpu.get_barrier_semaphore()
    for k in order:
        pl.semaphore_signal(barrier, inc=1, device_id={"ep": partners[k]}, device_id_type=MESH)
    for t in range(1, c):
        pl.semaphore_signal(
            barrier, inc=1, device_id={"dp": lax.rem(grp + t, c)}, device_id_type=MESH
        )

    def load_qkv(slot):
        cols = pl.ds(0, 3 * width)
        return [
            pltpu.make_async_copy(
                r.w_qkv.at[pl.ds(0, half), :], r.act.at[:, cols], r.load_sem.at[slot]
            ),
            pltpu.make_async_copy(
                r.w_qkv.at[pl.ds(half, half), :], r.grad_pre.at[:, cols], r.load_sem.at[slot + 1]
            ),
        ]

    first_loads = load_qkv(0)
    load_o = pltpu.make_async_copy(r.w_o, r.w_o_v, r.load_sem.at[2])
    load_out = pltpu.make_async_copy(r.w_out.at[0], r.w_out_v, r.load_sem.at[3])
    load_in = pltpu.make_async_copy(r.w_in.at[0], r.w_in_v, r.load_sem.at[4])
    for load in first_loads + [load_o, load_out, load_in]:
        load.start()

    r.place[...] = place_matrix(r.ids[...], n, cap)
    for t in range(width // TILE):
        cols = slice(t * TILE, (t + 1) * TILE)
        r.g_send[:, :, cols] = (
            dot(r.place[...], r.cotangent[:, cols], NN).astype(BF).reshape(n, cap, TILE)
        )
    pl.semaphore_wait(barrier, n - 1 + c - 1)
    half_cap = cap // 2
    g_halves = [
        [
            to_partner(
                r.g_send.at[partners[k], pl.ds(h * half_cap, half_cap), :],
                r.g_own.at[spot[k], pl.ds(h * half_cap, half_cap), :],
                r.g_ss.at[h, k],
                r.g_rs.at[h, k],
                k,
            )
            for k in order
        ]
        for h in range(2)
    ]
    for copy in g_halves[0]:
        copy.start()
    r.g_own[0] = r.g_send[me]

    norm_apply(r.tokens, r.gain_attn, r.shift_attn, r.normed)

    def to_heads(p, k):
        return to_partner(
            r.qkv_send.at[p, partners[k]],
            r.qkv_heads.at[p, me],
            r.a_ss.at[p, k],
            r.a_rs.at[p, k],
            k,
        )

    for load in first_loads:
        load.wait()
    for p in range(3):
        for t in range(width // TILE):
            cols = slice(p * width + t * TILE, p * width + (t + 1) * TILE)
            block = dot(r.normed[:, :half], r.act[:, cols], NN)
            block = (block + dot(r.normed[:, half:], r.grad_pre[:, cols], NN)).astype(BF)
            for e in range(TILE // own):
                r.qkv_send[p, t * (TILE // own) + e] = block[:, e * own : (e + 1) * own]
        r.qkv_heads[p, me] = r.qkv_send[p, me]
    for copy in g_halves[1]:
        copy.start()

    g_line = Line(r.g_own, r.g_all, r.gz_ss, r.gz_rs, grp, c, 2)
    x_line = Line(r.x_own, r.x_all, r.xz_ss, r.xz_rs, grp, c, 1)
    for copy in g_halves[0]:
        copy.wait()
    g_line.start(0)
    for p in range(3):
        for k in order:
            to_heads(p, k).start()
    for copy in g_halves[1]:
        copy.wait()
    g_line.start(1)

    load_out.wait()
    for p in range(3):
        for k in order:
            to_heads(p, k).wait_recv()

    def normed_halves(e):
        return [
            r.normed_all.at[e, pl.ds(0, rows // 2), :],
            r.normed_all.at[e, pl.ds(rows // 2, rows // 2), :],
        ]

    normed_gather = Gather(
        r.normed, lambda e: r.normed_all.at[e], normed_halves, r.n_ss, r.n_rs, me, n
    )
    mine = pltpu.make_async_copy(r.normed, r.normed_all.at[me], r.load_sem.at[5])
    mine.start()
    normed_gather.start()

    for i in range(n):
        r.values_t[i] = r.qkv_heads[2, i].astype(F32).T.astype(BF)

    def home(t):
        target = lax.rem(me + t, n)
        return send(
            r.att_heads.at[target],
            r.att_recv.at[me],
            r.o_ss.at[t],
            r.o_rs.at[t],
            {"ep": target},
        )

    def block_step(t, _):
        at = lax.rem(me + t, n)
        if n > UNROLLED:
            attend_block_loop(r, at)
        else:
            lax.switch(at, [functools.partial(attend_block, r, i) for i in range(n)])

        @pl.when(t > 0)
        def _():
            home(t).start()

        pl.when(t == 2)(lambda: g_line.hand_on(1))
        return 0

    lax.fori_loop(0, n, block_step, 0)
    r.att_recv[me] = r.att_heads[me]

    for t in range(1, n):
        home(t).wait_recv()
    for e in range(n):
        r.attended[:, e * own : (e + 1) * own] = r.att_recv[e]

    load_o.wait()
    for t in range(width // TILE):
        cols = slice(t * TILE, (t + 1) * TILE)
        r.hidden[:, cols] = r.tokens[:, cols].astype(F32) + dot(
            r.attended[...], r.w_o_v[:, cols], NN
        )
    norm_apply(r.hidden, r.gain_ffn, r.shift_ffn, r.block_out)
    for t in range(width // TILE):
        cols = slice(t * TILE, (t + 1) * TILE)
        r.x_send[:, :, cols] = (
            dot(r.place[...], r.block_out[:, cols], NN).astype(BF).reshape(n, cap, TILE)
        )
    x_copies = {k: to_expert(r.x_send, r.x_own, (r.x_ss, r.x_rs), k) for k in listed[1:]}
    for copy in x_copies.values():
        copy.start()
    r.x_own[0] = r.x_send[me]

    def act_grad(cols):
        r.grad_pre[:, cols] = dot(flat(r.g_own[...]), r.w_out_v[cols, :], NT).astype(BF)

    tiles(hidden, act_grad)
    load_in.wait()
    normed_gather.middle()
    g_line.hand_on(2)

    some = n // 2
    r_copies = {k: from_expert(r.g_send, r.r_recv, (r.r_ss, r.r_rs), k) for k in listed[1:]}

    def expert_half(at):
        mine_rows = slice(at * slots // 2, (at + 1) * slots // 2)
        blocks = slice(at * some, (at + 1) * some)
        for k in listed[blocks]:
            if k:
                x_copies[k].wait()
        if at:
            x_line.start(0)

        def expert_step(cols):
            pre = dot(flat(r.x_own[blocks]), r.w_in_v[cols, :], NT)
            for q in range(slots // 2 // CHUNK):
                part_at = slice(q * CHUNK, (q + 1) * CHUNK)
                rows_at = slice(mine_rows.start + q * CHUNK, mine_rows.start + (q + 1) * CHUNK)
                act, slope = gelu_both(pre[part_at])
                r.act[rows_at, cols] = act.astype(BF)
                r.grad_pre[rows_at, cols] = (
                    r.grad_pre[rows_at, cols].astype(F32) * slope
                ).astype(BF)

        tiles(hidden, expert_step)

        def routed_grad(cols):
            r.g_send[blocks, :, cols] = (
                dot(r.grad_pre[mine_rows, :], r.w_in_v[:, cols], NN)
                .astype(BF)
                .reshape(some, cap, TILE)
            )

        tiles(width, routed_grad)
        for k in listed[blocks]:
            if k:
                r_copies[k].start()

    expert_half(0)
    r.r_recv[me] = r.g_send[0]

    expert_half(1)

    def produce(cols):
        r.x_send[:, :, cols] = (
            dot(r.act[...], r.w_out_v[:, cols], NN).astype(BF).reshape(n, cap, TILE)
        )

    tiles(width, produce)
    mine_at = pl.multiple_of(grp * part, part)

    def weight_terms(act_at, x_rows, g_rows, first):
        def one(out):
            from_act = pl.ds(pl.multiple_of(act_at + out.start, TILE), TILE)

            def two(cols):
                term_in = dot(r.grad_pre[:, from_act], x_rows(cols), TN)
                r.sum_in[out, cols] = term_in if first else r.sum_in[out, cols] + term_in
                term_out = dot(r.act[:, from_act], g_rows(cols), TN)
                r.sum_out[out, cols] = term_out if first else r.sum_out[out, cols] + term_out

            tiles(width, two)

        tiles(part, one)

    weight_terms(
        mine_at,
        lambda cols: flat(r.x_own[:, :, cols]),
        lambda cols: flat(r.g_own[:, :, cols]),
        True,
    )

    normed_gather.last()

    for copy in r_copies.values():
        copy.wait()

    g_line.hand_on(*range(3, c))

    for t in range(width // TILE):
        cols = slice(t * TILE, (t + 1) * TILE)
        r.grad_tokens[:, cols] = dot(r.place[...], flat(r.r_recv[:, :, cols]), TN)

    def store_hidden(at, grad_in):
        grad_hidden = r.cotangent[at, :].astype(F32) + grad_in
        r.grad_tokens[at, :] = grad_hidden
        r.block_out[at, :] = grad_hidden.astype(BF)

    sums = norm_back(r.hidden, r.grad_tokens, r.gain_ffn, store_hidden)
    r.small_own[2:3], r.small_own[3:4] = sums
    r.small_own[4:SMALL] = jnp.zeros((SMALL - 4, width), F32)
    for t in range(width // TILE):
        block = dot(r.block_out[...], r.w_o_v[t * TILE : (t + 1) * TILE, :], NT).astype(BF)
        for e in range(TILE // own):
            r.att_recv[t * (TILE // own) + e] = block[:, e * own : (e + 1) * own]
    a_copies = [blocks_out(r.att_recv, r.grad_att, (r.b_ss, r.b_rs), k) for k in order]
    for copy in a_copies:
        copy.start()
    r.grad_att[me] = r.att_recv[me]

    def wo_rows(buf, e):
        at = e * own
        return buf.at[
            pl.ds(pl.multiple_of(lax.rem(at, slots), own), own),
            pl.ds(pl.multiple_of(lax.div(at, slots) * width, width), width),
        ]

    for t in range(width // slots):
        out = slice(t * slots, (t + 1) * slots)
        r.act[:, t * width : (t + 1) * width] = dot(
            r.attended[:, out], r.block_out[...], TN
        ).astype(BF)

    def to_sibling(k):
        at = partners[k]
        return to_partner(
            wo_rows(r.act, at), wo_rows(r.grad_pre, at), r.w_ss.at[k], r.w_rs.at[k], 1
        )

    def to_owner(k):
        return to_partner(
            wo_rows(r.act, partners[k]),
            wo_rows(r.grad_pre, partners[1]),
            r.w_ss.at[k],
            r.w_rs.at[k],
            k,
        )

    for copy in a_copies:
        copy.wait()

    for k in range(1, n, 2):
        to_sibling(k).start()

    def wo_across():
        for k in range(1, n, 2):
            to_sibling(k).wait()
        for k in [0] + direct:
            mine_k = wo_rows(r.act, partners[k])
            mine_k[...] = (
                mine_k[...].astype(F32) + wo_rows(r.grad_pre, partners[k])[...].astype(F32)
            ).astype(BF)
        for k in direct:
            to_owner(k).start()

    for p in range(3):
        for k in order:
            to_heads(p, k).wait_send()
    for t in range(1, n):
        home(t).wait_send()
    for i in range(n):
        both = (r.grad_att[i].astype(F32) * r.att_heads[i].astype(F32)).T
        size = own // r.heads
        deltas = [
            jnp.sum(both[h * size : (h + 1) * size], axis=0, keepdims=True) for h in range(r.heads)
        ]
        r.delta[i] = jnp.concatenate(
            deltas + [jnp.zeros((SMALL - r.heads, rows), F32)], axis=0
        )
    r.grad_q_t[...] = jnp.zeros(r.grad_q_t.shape, F32)

    def back_home(p, t):
        target = lax.rem(me + t, n)
        return send(
            r.qkv_send.at[p, target],
            r.grad_tok.at[p, me],
            r.d_ss.at[p, t],
            r.d_rs.at[p, t],
            {"ep": target},
        )

    def back_step(t, _):
        attend_back(r, lax.rem(me + t, n), n)
        pl.when(t == 0)(lambda: x_line.hand_on(1))
        pl.when(t == 1)(wo_across)

        @pl.when(t > 0)
        def _():
            for p in (1, 2):
                back_home(p, t).start()

        return 0

    lax.fori_loop(0, n, back_step, 0)
    for i in range(n):
        r.qkv_send[0, i] = (r.grad_q_t[i].T * ((own // r.heads) ** -0.5)).astype(BF)
    for t in range(1, n):
        back_home(0, t).start()
    for p in range(3):
        r.grad_tok[p, me] = r.qkv_send[p, me]
    p_copies = [from_expert(r.x_send, r.r_recv, (r.p_ss, r.p_rs), k) for k in order]
    for copy in p_copies:
        copy.start()
    r.r_recv[me] = r.x_send[0]

    def o_place(e, d):
        at = pl.ds(pl.multiple_of(e * own, own), own)
        piece = width // len(owners_of(c))
        if d is None:
            return r.o_all.at[at, :]
        return r.o_all.at[at, pl.ds(pl.multiple_of(d * piece, piece), piece)]

    def o_halves(e):
        at = pl.ds(pl.multiple_of(e * own, own), own)
        return [r.o_all.at[at, pl.ds(0, half)], r.o_all.at[at, pl.ds(half, half)]]

    def q_place(first, e, d):
        piece = TILE // len(owners_of(c))
        if d is None:
            return r.q_all.at[:, e, pl.ds(first, TILE), :]
        return r.q_all.at[:, e, pl.ds(pl.multiple_of(first + d * piece, piece), piece), :]

    def q_halves(first, e):
        return [
            r.q_all.at[:, e, pl.ds(first, TILE // 2), :],
            r.q_all.at[:, e, pl.ds(first + TILE // 2, TILE // 2), :],
        ]

    o_spread = Spread(
        r, "wo", me, grp, n, c, o_place, o_halves, lambda half: r.wo_send.at[half]
    )

    def q_source(t, half):
        if r.lent:
            return (r.grad_att, r.att_heads)[t].at[pl.ds(3 * half, 3)]
        return getattr(r, "wq" + str(t) + "_send").at[half]

    q_spreads = [
        Spread(
            r,
            "wq" + str(t),
            me,
            grp,
            n,
            c,
            functools.partial(q_place, t * TILE),
            functools.partial(q_halves, t * TILE),
            functools.partial(q_source, t),
        )
        for t in range(width // TILE)
    ]

    normed_gather.finish()
    mine.wait()
    at_once = width // rows
    turns = n // at_once

    def normed_loads(t):
        out = []
        for b in range(turns):
            spot = (t if turns <= 2 else b // 2) * TILE
            for s in range(at_once):
                out.append(
                    pltpu.make_async_copy(
                        r.normed_all.at[b * at_once + s, :, pl.ds(t * TILE, TILE)],
                        r.space.at[
                            pl.ds((b % 2) * width + s * rows, rows), pl.ds(spot, TILE)
                        ],
                        r.slab_sem.at[t % 2, b * at_once + s],
                    )
                )
        return out

    for t in range(width // TILE if turns <= 2 else 1):
        for load in normed_loads(t):
            load.start()
    for t, spread in enumerate(q_spreads):
        if turns > 2 and t:
            for load in normed_loads(t):
                load.start()
        for load in normed_loads(t):
            load.wait()
        total = None
        for b in range(turns):
            spot = (t if turns <= 2 else b // 2) * TILE
            grads = jnp.concatenate(
                [flat(r.qkv_send[p, b * at_once : (b + 1) * at_once]) for p in range(3)], axis=1
            )
            term = dot(
                r.space[(b % 2) * width : (b % 2 + 1) * width, spot : spot + TILE], grads, TN
            )
            total = term if b == 0 else total + term
        low = total.astype(BF)
        piece = TILE // len(owners_of(c))
        for d in range(len(owners_of(c))):
            for p in range(3):
                spread.source(d)[p] = low[
                    d * piece : (d + 1) * piece, p * own : (p + 1) * own
                ]
        if t == 0:
            spread.scatter()

    for k in direct:
        to_owner(k).wait()
    total = wo_rows(r.act, me)[...].astype(F32)
    for k in direct:
        total = total + wo_rows(r.grad_pre, partners[k + 1])[...].astype(F32)
    pieces = len(owners_of(c))
    for d in range(pieces):
        cols = slice(d * width // pieces, (d + 1) * width // pieces)
        r.wo_send[d] = total[:, cols].astype(BF)
    o_spread.scatter()


    def slab_loads(q):
        at = partner(grp, q, c)
        base = (q % 2) * width
        out = []
        for which, src in enumerate((r.x_all, r.g_all)):
            for s in range(n):
                out.append(
                    pltpu.make_async_copy(
                        src.at[at, s],
                        r.space.at[pl.ds(base + which * slots + s * cap, cap), :],
                        r.slab_sem.at[q % 2, which * n + s],
                    )
                )
        return out

    def slab_start(q):
        g_line.wait(partner(grp, q, c))
        x_line.wait(partner(grp, q, c))
        for load in slab_loads(q):
            load.start()

    def slab(q, beside=lambda: None):
        base = (q % 2) * width
        for load in slab_loads(q):
            load.wait()
        x_rows, g_rows = r.space.at[pl.ds(base, slots), :], r.space.at[pl.ds(base + slots, slots), :]

        def activate(out):
            at = pl.ds(pl.multiple_of(mine_at + out.start, TILE), TILE)
            cols = pl.ds(pl.multiple_of(3 * width + out.start, TILE), TILE)
            r.grad_pre[:, cols] = dot(g_rows[...], r.w_out_v[at, :], NT).astype(BF)
            pre = dot(x_rows[...], r.w_in_v[at, :], NT)
            for q in range(slots // CHUNK):
                some = slice(q * CHUNK, (q + 1) * CHUNK)
                act, slope = gelu_both(pre[some])
                r.act[some, cols] = act.astype(BF)
                r.grad_pre[some, cols] = (r.grad_pre[some, cols].astype(F32) * slope).astype(BF)

        tiles(part, activate)
        beside()
        weight_terms(
            3 * width, lambda cols: x_rows[:, cols], lambda cols: g_rows[:, cols], False
        )

    slab_start(1)

    def first_total():
        q_spreads[0].total()
        for spread in q_spreads[1:]:
            spread.scatter()

    slab(1, first_total)

    o_spread.total()
    last_loads = load_qkv(0)
    for load in last_loads:
        load.start()

    for p in (1, 2, 0):
        for t in range(1, n):
            back_home(p, t).wait_recv()
    for load in last_loads:
        load.wait()

    for copy in p_copies:
        copy.wait()
    for t in range(width // TILE):
        cols = slice(t * TILE, (t + 1) * TILE)
        r.block_out[:, cols] = (
            r.hidden[:, cols] + dot(r.place[...], flat(r.r_recv[:, :, cols]), TN)
        ).astype(BF)

    for p in range(3):
        for e in range(n):
            r.attended[:, e * own : (e + 1) * own] = r.grad_tok[p, e]
        cols = slice(p * width, (p + 1) * width)
        for at, weight in enumerate((r.act, r.grad_pre)):
            out = slice(at * half, (at + 1) * half)
            term = dot(r.attended[...], weight[:, cols], NT)
            r.hidden[:, out] = term if p == 0 else r.hidden[:, out] + term

    def store_tokens(at, grad_in):
        r.grad_tokens[at, :] += grad_in

    sums = norm_back(r.tokens, r.hidden, r.gain_attn, store_tokens)
    r.small_own[0:1], r.small_own[1:2] = sums

    def small_ep(k):
        return to_partner(r.small_own, r.small_ep.at[me], r.s_ss.at[0, k], r.s_rs.at[0, k], k)

    def small_dp(t):
        return send(
            r.small_sum,
            r.small_dp.at[grp],
            r.s_ss.at[1, t],
            r.s_rs.at[1, t],
            {"dp": lax.rem(grp + t, c)},
        )

    for k in order:
        small_ep(k).start()
    r.small_ep[me] = r.small_own[...]

    q_spreads[0].over()

    for spread in q_spreads[1:]:
        spread.total()
    x_line.hand_on(*range(2, c))

    if c > 3:
        slab_start(2)
        slab(2, q_spreads[0].gather.middle)
    else:
        q_spreads[0].gather.middle()

    for spread in [o_spread] + q_spreads[1:]:
        spread.over()

    for q in range(3, c - 1):
        slab_start(q)
        slab(q)
    out_copies = []
    for at, (src, dst) in enumerate(((r.sum_in, r.grad_in), (r.sum_out, r.grad_out))):
        base = at * width
        for s in range(0, part, CHUNK * 4):
            r.space[base + s : base + s + CHUNK * 4, :] = src[s : s + CHUNK * 4, :].astype(BF)
        out_copies.append(
            pltpu.make_async_copy(
                r.space.at[pl.ds(base, part), :], dst, r.load_sem.at[at]
            )
        )
    for copy in out_copies:
        copy.start()

    for k in order:
        small_ep(k).wait()
    total = r.small_ep[0]
    for e in range(1, n):
        total = total + r.small_ep[e]
    r.small_sum[...] = total
    for t in range(1, c):
        small_dp(t).start()
    r.small_dp[grp] = total

    spreads = q_spreads + [o_spread]
    q_spreads[0].gather.last()

    for spread in spreads[1:]:
        spread.gather.middle()

    for spread in spreads[1:]:
        spread.gather.last()

    for t in range(1, c):
        small_dp(t).wait()
    total = r.small_dp[0]
    for d in range(1, c):
        total = total + r.small_dp[d]
    r.small[...] = total
    last = partner(grp, c - 1, c)
    g_line.wait(last)
    x_line.wait(last)
    g_line.finish()
    x_line.finish()
    for copy in out_copies:
        copy.wait()
    for spread in spreads:
        spread.finish()
    for p in range(3):
        for t in range(1, n):
            back_home(p, t).wait_send()


def block_call(n, c, heads, operands):
    rows, width = operands["tokens"].shape
    hidden = operands["w_in"].shape[1]
    own, cap, part = width // n, 2 * rows // n, hidden // c
    slots, pieces = n * cap, len(owners_of(c))
    vm, hb = pl.BlockSpec(memory_space=pltpu.VMEM), pl.BlockSpec(memory_space=pl.ANY)
    sm = pl.BlockSpec(memory_space=pltpu.SMEM)
    inputs = dict(
        lengths=sm, ids=vm, tokens=vm, cotangent=vm, gain_attn=vm, shift_attn=vm, gain_ffn=vm,
        shift_ffn=vm, w_qkv=hb, w_o=hb, w_in=hb, w_out=hb,
    )
    outputs = dict(
        block_out=((rows, width), BF, vm),
        grad_tokens=((rows, width), F32, vm),
        q_all=((3, n, width, own), BF, hb),
        o_all=((width, width), BF, hb),
        small=((SMALL, width), F32, vm),
        grad_in=((part, width), BF, hb),
        grad_out=((part, width), BF, hb),
        g_all=((c, n, cap, width), BF, hb),
        x_all=((c, n, cap, width), BF, hb),
        normed_all=((n, rows, width), BF, hb),
    )

    def v(*shape):
        return pltpu.VMEM(shape, BF)

    def f(*shape):
        return pltpu.VMEM(shape, F32)

    def d(*shape):
        return pltpu.SemaphoreType.DMA(shape)

    heads_shape = (n, rows, own)
    scratch = dict(
        sum_in=f(part, width), sum_out=f(part, width),
        w_o_v=v(width, width), w_in_v=v(hidden, width), w_out_v=v(hidden, width),
        act=v(slots, hidden), grad_pre=v(slots, hidden), space=v(2 * width, width),
        normed=v(rows, width), place=v(slots, rows), hidden=f(rows, width),
        attended=v(rows, width),
        qkv_send=v(3, *heads_shape), qkv_heads=v(3, *heads_shape), grad_tok=v(3, *heads_shape),
        values_t=v(n, own, rows), att_heads=v(*heads_shape), att_recv=v(*heads_shape),
        grad_att=v(*heads_shape), grad_q_t=f(n, own, rows),
        lse=f(n, SMALL, rows), delta=f(n, SMALL, rows),
        g_send=v(n, cap, width), x_send=v(n, cap, width), g_own=v(n, cap, width),
        x_own=v(n, cap, width), r_recv=v(n, cap, width),
        wo_send=v(pieces, own, width // pieces), wo_recv=v(c, own, width // pieces),
        wo_fin=v(own, width // pieces),
        small_own=f(SMALL, width), small_ep=f(n, SMALL, width), small_sum=f(SMALL, width),
        small_dp=f(c, SMALL, width),
        load_sem=d(8), slab_sem=d(2, 2 * n),
        a_ss=d(3, n), a_rs=d(3, n), g_ss=d(2, n), g_rs=d(2, n), n_ss=d(n + 2), n_rs=d(n + 2),
        o_ss=d(n), o_rs=d(n), x_ss=d(n), x_rs=d(n), r_ss=d(n), r_rs=d(n), p_ss=d(n), p_rs=d(n),
        b_ss=d(n), b_rs=d(n), w_ss=d(n), w_rs=d(n), d_ss=d(3, n), d_rs=d(3, n),
        gz_ss=d(2, c, 2), gz_rs=d(c, 2), xz_ss=d(2, c, 1), xz_rs=d(c, 1),
        wo_ss=d(2, c), wo_rs=d(2, c), wo_ys=d(n + 2), wo_yr=d(n + 2), wo_ls=d(1),
        s_ss=d(2, max(n, c)), s_rs=d(2, max(n, c)),
    )
    for t in range(width // TILE):
        name = "wq" + str(t)
        piece = TILE // pieces
        lent = pieces == 2 and n >= 6 and piece == rows and width == 2 * TILE
        if not lent:
            scratch[name + "_send"] = v(pieces, 3, piece, own)
        scratch[name + "_recv"] = v(c, 3, piece, own)
        scratch[name + "_fin"] = v(3, piece, own)
        scratch[name + "_ss"] = scratch[name + "_rs"] = d(2, c)
        scratch[name + "_ys"] = scratch[name + "_yr"] = d(n + 2)
        scratch[name + "_ls"] = d(1)
    names = list(inputs) + list(outputs) + list(scratch)

    def kernel(*refs):
        r = types.SimpleNamespace(**dict(zip(names, refs)))
        r.heads, r.lent = heads, lent
        block_kernel(r, n, c)

    result = pl.pallas_call(
        kernel,
        out_shape=[jax.ShapeDtypeStruct(shape, kind) for shape, kind, _ in outputs.values()],
        in_specs=list(inputs.values()),
        out_specs=[spec for _, _, spec in outputs.values()],
        scratch_shapes=list(scratch.values()),
        compiler_params=pltpu.CompilerParams(
            collective_id=0, has_side_effects=True, vmem_limit_bytes=VMEM_LIMIT
        ),
    )(*[operands[name] for name in inputs])
    return dict(zip(outputs, result))


VMEM_LIMIT = 64 << 20
STEPS = 4


def widen_kernel(where, q_all, o_all, sum_in, sum_out, block, tokens, small, *rest):
    x_rows, g_rows, w_in, w_out, q_out, o_out, grad_in, grad_out, block_out, tokens_out = rest[:10]
    n, own = q_all.shape[1], q_all.shape[3]
    x_rows, g_rows = flat(x_rows[0]), flat(g_rows[0])
    pre = dot(x_rows, w_in[0], NT)
    grad_act = dot(g_rows, w_out[0], NT)
    acts, grads = [], []
    for q in range(x_rows.shape[0] // CHUNK):
        at = slice(q * CHUNK, (q + 1) * CHUNK)
        act, slope = gelu_both(pre[at])
        acts.append(act.astype(BF))
        grads.append((grad_act[at] * slope).astype(BF))
    grad_in[0] = sum_in[...].astype(F32) + dot(jnp.concatenate(grads, axis=0), x_rows, TN)
    grad_out[0] = sum_out[...].astype(F32) + dot(jnp.concatenate(acts, axis=0), g_rows, TN)
    for p in range(3):
        for e in range(n):
            at = (p * n + e) * own
            q_out[:, at : at + own] = q_all[p, e].astype(F32)
    o_out[...] = o_all[...].astype(F32)
    block_out[...] = block[...]
    tokens_out[...] = tokens[...]
    for at, one in enumerate(rest[10:]):
        one[...] = small[at : at + 1, :]


def widen(out, w_in, w_out):
    q_all, o_all, sum_in, block = out["q_all"], out["o_all"], out["grad_in"], out["block_out"]
    x_all = out["x_all"]
    c = x_all.shape[0]
    _, n, width, own = q_all.shape
    part, rows = sum_in.shape[0], block.shape[0]
    S = jax.ShapeDtypeStruct
    grp = lax.axis_index("dp")
    where = jnp.stack([partner(grp, c - 1, c), grp * STEPS]).astype(jnp.int32)

    def rowwise(count):
        return pl.BlockSpec((count // STEPS, width), lambda i, w: (i, 0))

    expert = pl.BlockSpec((1, part // STEPS, width), lambda i, w: (0, i, 0))
    weight = pl.BlockSpec((1, part // STEPS, width), lambda i, w: (0, w[1] + i, 0))
    group = pl.BlockSpec((1, *x_all.shape[1:]), lambda i, w: (w[0], 0, 0, 0))
    fixed = pl.BlockSpec((1, width), lambda i, w: (0, 0))
    return pl.pallas_call(
        widen_kernel,
        grid_spec=pltpu.PrefetchScalarGridSpec(
            num_scalar_prefetch=1,
            grid=(STEPS,),
            in_specs=[
                pl.BlockSpec((3, n, width // STEPS, own), lambda i, w: (0, 0, i, 0)),
                rowwise(width), rowwise(part), rowwise(part), rowwise(rows), rowwise(rows),
                pl.BlockSpec((SMALL, width), lambda i, w: (0, 0)), group, group, weight, weight,
            ],
            out_specs=[
                pl.BlockSpec((width // STEPS, 3 * width), lambda i, w: (i, 0)),
                rowwise(width), expert, expert, rowwise(rows), rowwise(rows),
            ] + [fixed] * 4,
        ),
        out_shape=[
            S((width, 3 * width), F32), S((width, width), F32), S((1, part, width), F32),
            S((1, part, width), F32), S((rows, width), BF), S((rows, width), F32),
        ] + [S((1, width), F32)] * 4,
        compiler_params=pltpu.CompilerParams(vmem_limit_bytes=VMEM_LIMIT),
    )(
        where, q_all, o_all, sum_in, out["grad_out"], block, out["grad_tokens"], out["small"],
        x_all, out["g_all"], w_in, w_out,
    )


def on_device(
    tokens,
    gain_attn,
    shift_attn,
    w_qkv,
    w_o,
    gain_ffn,
    shift_ffn,
    w_in,
    w_out,
    seq_lengths,
    expert_ids,
    cotangent,
):
    rows, width = tokens.shape
    n, c = lax.axis_size("ep"), lax.axis_size("dp")
    operands = dict(
        lengths=seq_lengths,
        ids=expert_ids.reshape(1, rows),
        tokens=tokens,
        cotangent=cotangent,
        gain_attn=gain_attn[None],
        shift_attn=shift_attn[None],
        gain_ffn=gain_ffn[None],
        shift_ffn=shift_ffn[None],
        w_qkv=w_qkv,
        w_o=w_o,
        w_in=w_in,
        w_out=w_out,
    )
    out = block_call(n, c, HEADS // n, operands)
    q_out, o_out, in_out, out_out, block, tokens_out, *small = widen(out, w_in, w_out)
    small = [one.reshape(width) for one in small]
    return (block, tokens_out, q_out, o_out, *small, in_out, out_out)


def solution(mesh):
    return jax.shard_map(
        on_device,
        mesh=mesh,
        in_specs=(
            P(("dp", "ep"), None),
            P(),
            P(),
            P(),
            P(),
            P(),
            P(),
            P("ep", None, None),
            P("ep", None, None),
            P("dp", None),
            P(("dp", "ep"), None),
            P(("dp", "ep"), None),
        ),
        out_specs=(
            P(("dp", "ep"), None),
            P(("dp", "ep"), None),
            P(),
            P(),
            P(),
            P(),
            P(),
            P(),
            P("ep", "dp", None),
            P("ep", "dp", None),
        ),
        check_vma=False,
    )
```

```python
import functools
import types

import jax
import jax.numpy as jnp
from jax import lax
from jax.experimental import pallas as pl
from jax.experimental.pallas import tpu as pltpu
from jax.sharding import PartitionSpec as P

HEADS = 16
EPSILON = 1e-05
MASKED = -1e30
TILE = 512
SMALL = 8
UNROLLED = 8
AT_ONCE = 4
MESH = pl.DeviceIdType.MESH
F32 = jnp.float32
BF = jnp.bfloat16
NN = (((1,), (0,)), ((), ()))
NT = (((1,), (1,)), ((), ()))
TN = (((0,), (0,)), ((), ()))


def dot(left, right, dims):
    return lax.dot_general(left, right, dims, preferred_element_type=F32)


def partner(me, k, n):
    out, weight = 0, 1
    while weight < n:
        bit = lax.rem(lax.div(me, weight), 2)
        out = out + (lax.rem(bit + 1, 2) if k & weight else bit) * weight
        weight *= 2
    return out


def send(src, dst, send_sem, recv_sem, target):
    return pltpu.make_async_remote_copy(
        src_ref=src,
        dst_ref=dst,
        send_sem=send_sem,
        recv_sem=recv_sem,
        device_id=target,
        device_id_type=MESH,
    )


def order_of(n):
    return sorted(range(1, n), key=lambda k: (-bin(k // 2).count("1"), k))


def flat(value):
    return value.reshape(value.shape[0] * value.shape[1], value.shape[2])


def tiles(count, body, beside=None):
    def step(t, _):
        body(pl.ds(pl.multiple_of(t * TILE, TILE), TILE))
        for at, act in (beside or {}).items():
            pl.when(t == at)(act)
        return 0

    lax.fori_loop(0, count // TILE, step, 0)


def norm_rows(rows_in):
    average = jnp.mean(rows_in, axis=-1, keepdims=True)
    centered = rows_in - average
    inv_std = lax.rsqrt(jnp.mean(centered * centered, axis=-1, keepdims=True) + EPSILON)
    return centered * inv_std, inv_std


CHUNK = 32


def by_rows(count, body, carry=0):
    def step(i, state):
        return body(pl.ds(pl.multiple_of(i * CHUNK, CHUNK), CHUNK), state)

    return lax.fori_loop(0, count // CHUNK, step, carry)


def norm_apply(src, gain, shift, dst):
    def body(at, _):
        unit, _ = norm_rows(src[at, :].astype(F32))
        dst[at, :] = (unit * gain[...] + shift[...]).astype(BF)
        return 0

    by_rows(src.shape[0], body)


def norm_back(src, grad, gain, store):
    def body(at, sums):
        unit, inv = norm_rows(src[at, :].astype(F32))
        incoming = grad[at, :]
        grad_unit = incoming * gain[...]
        grad_in = inv * (
            grad_unit
            - jnp.mean(grad_unit, axis=-1, keepdims=True)
            - unit * jnp.mean(grad_unit * unit, axis=-1, keepdims=True)
        )
        store(at, grad_in)
        return (
            sums[0] + jnp.sum(incoming * unit, axis=0, keepdims=True),
            sums[1] + jnp.sum(incoming, axis=0, keepdims=True),
        )

    zero = jnp.zeros((1, src.shape[1]), F32)
    return by_rows(src.shape[0], body, (zero, zero))


def gelu_both(pre):
    square = pre * pre
    bent = jnp.tanh(0.7978845608028654 * pre * (1.0 + 0.044715 * square))
    half = 0.5 + 0.5 * bent
    rise = 0.7978845608028654 * (1.0 + 3 * 0.044715 * square)
    return pre * half, half + 0.5 * pre * (1.0 - bent * bent) * rise


def place_matrix(ids_row, n, cap):
    rows = ids_row.shape[1]
    expert = lax.broadcasted_iota(jnp.int32, (n, rows), 0)
    hit = (expert == ids_row).astype(F32)
    before = lax.broadcasted_iota(jnp.int32, (rows, rows), 0)
    after = lax.broadcasted_iota(jnp.int32, (rows, rows), 1)
    upto = (before <= after).astype(F32).astype(BF)
    count = dot(hit.astype(BF), upto, NN)
    slot = jnp.sum(hit * (count - 1.0), axis=0, keepdims=True)
    target = ids_row * cap + slot.astype(jnp.int32)
    places = lax.broadcasted_iota(jnp.int32, (n * cap, rows), 0)
    return (places == target).astype(F32).astype(BF)


def start_row(len_ref, first, width):
    pos = first + lax.broadcasted_iota(jnp.int32, (1, width), 1)
    start = jnp.zeros((1, width), jnp.int32)
    edge = jnp.int32(0)
    for s in range(len_ref.shape[1] - 1):
        edge = edge + len_ref[0, s]
        start = jnp.where(pos >= edge, edge, start)
    return pos, start


def split_heads(block, heads):
    if heads == 1:
        return [block]
    size = block.shape[1] // heads
    lane = lax.broadcasted_iota(jnp.int32, block.shape, 1)
    zero = jnp.zeros_like(block)
    return [
        jnp.where((lane >= h * size) & (lane < (h + 1) * size), block, zero) for h in range(heads)
    ]


def attend_block(r, i):
    rows, own = r.qkv_heads.shape[2:]
    heads = r.heads
    size = own // heads
    queries = split_heads(r.qkv_heads[0, i] * BF(size**-0.5), heads)
    pos, start = start_row(r.lengths, i * rows, rows)
    outs, sums = [], []
    for h in range(heads):
        top = jnp.full((1, rows), MASKED, F32)
        total = jnp.zeros((1, rows), F32)
        accum = jnp.zeros((size, rows), F32)
        for last in range(i, -1, -AT_ONCE):
            scores = []
            blocks = range(last, max(last - AT_ONCE, -1), -1)
            for j in blocks:
                key = j * rows + lax.broadcasted_iota(jnp.int32, (rows, rows), 0)
                allowed = key >= start
                if j == i:
                    allowed = allowed & (key <= pos)
                scores.append(
                    jnp.where(allowed, dot(r.qkv_heads[1, j], queries[h], NT), MASKED)
                )
            peak = functools.reduce(
                jnp.maximum, [jnp.max(s.reshape(rows // 8, 8, rows), axis=0) for s in scores]
            )
            new_top = jnp.maximum(top, jnp.max(peak, axis=0, keepdims=True))
            decay = jnp.exp(top - new_top)
            accum = accum * decay
            part = jnp.zeros((8, rows), F32)
            for j, s in zip(blocks, scores):
                weights = jnp.exp(s - new_top)
                part = part + jnp.sum(weights.reshape(rows // 8, 8, rows), axis=0)
                values = r.values_t[j, h * size : (h + 1) * size, :]
                accum = accum + dot(values, weights.astype(BF), NN)
            total = total * decay + jnp.sum(part, axis=0, keepdims=True)
            top = new_top
        outs.append(accum / total)
        sums.append(top + jnp.log(total))
    r.att_heads[i] = jnp.concatenate(outs, axis=0).T.astype(BF)
    r.lse[i] = jnp.concatenate(sums + [jnp.zeros((SMALL - heads, rows), F32)], axis=0)


def attend_back(r, j, n):
    rows, own = r.qkv_heads.shape[2:]
    heads = r.heads
    size = own // heads
    keys, values = r.qkv_heads[1, j], r.qkv_heads[2, j]
    keys_t = keys.astype(F32).T.astype(BF)

    def fold(at, carry, diagonal):
        grad_k, grad_v = carry
        for i in at:
            queries = split_heads(r.qkv_heads[0, i] * BF(size**-0.5), heads)
            grads = split_heads(r.grad_att[i], heads)
            pos, start = start_row(r.lengths, i * rows, rows)
            key = j * rows + lax.broadcasted_iota(jnp.int32, (rows, rows), 0)
            allowed = key >= start
            if diagonal:
                allowed = allowed & (key <= pos)
            for h in range(heads):
                scores = dot(keys, queries[h], NT)
                probs = jnp.where(allowed, jnp.exp(scores - r.lse[i, h : h + 1, :]), 0.0)
                grad_probs = dot(values, grads[h], NT)
                grad_scores = (probs * (grad_probs - r.delta[i, h : h + 1, :])).astype(BF)
                grad_v = grad_v + dot(probs.astype(BF), grads[h], NN)
                grad_k = grad_k + dot(grad_scores, queries[h], NN)
                part = slice(h * size, (h + 1) * size)
                r.grad_q_t[i, part, :] += dot(keys_t[part, :], grad_scores, NN)
        return grad_k, grad_v

    zero = jnp.zeros((rows, own), F32)
    carry = fold([j], (zero, zero), True)
    left = n - 1 - j
    odd = lax.rem(left, 2)
    carry = lax.fori_loop(j + 1, j + 1 + odd, lambda i, carry: fold([i], carry, False), carry)

    def pair(t, carry):
        i = j + 1 + odd + 2 * t
        return fold([i, i + 1], carry, False)

    grad_k, grad_v = lax.fori_loop(0, lax.div(left, 2), pair, carry)
    r.qkv_send[1, j] = grad_k.astype(BF)
    r.qkv_send[2, j] = grad_v.astype(BF)


def attend_block_loop(r, i):
    rows, own = r.qkv_heads.shape[2:]
    heads = r.heads
    size = own // heads
    queries = split_heads(r.qkv_heads[0, i] * BF(size**-0.5), heads)
    pos, start = start_row(r.lengths, i * rows, rows)

    def fold(j, carry, diagonal):
        keys = r.qkv_heads[1, j]
        key = j * rows + lax.broadcasted_iota(jnp.int32, (rows, rows), 0)
        allowed = key >= start
        if diagonal:
            allowed = allowed & (key <= pos)
        out = []
        for h in range(heads):
            top, total, accum = carry[h]
            scores = jnp.where(allowed, dot(keys, queries[h], NT), MASKED)
            new_top = jnp.maximum(top, jnp.max(scores, axis=0, keepdims=True))
            weights = jnp.exp(scores - new_top)
            if diagonal:
                weights = jnp.where(allowed, weights, 0.0)
            decay = jnp.exp(top - new_top)
            total = total * decay + jnp.sum(weights, axis=0, keepdims=True)
            values = r.values_t[j, h * size : (h + 1) * size, :]
            accum = accum * decay + dot(values, weights.astype(BF), NN)
            out.append((new_top, total, accum))
        return tuple(out)

    state = tuple(
        (
            jnp.full((1, rows), MASKED, F32),
            jnp.zeros((1, rows), F32),
            jnp.zeros((size, rows), F32),
        )
        for _ in range(heads)
    )
    state = fold(i, state, True)
    state = lax.fori_loop(0, i, lambda j, carry: fold(j, carry, False), state)
    result = jnp.concatenate([accum / total for _, total, accum in state], axis=0)
    r.att_heads[i] = result.T.astype(BF)
    sums = [top + jnp.log(total) for top, total, _ in state]
    r.lse[i] = jnp.concatenate(sums + [jnp.zeros((SMALL - heads, rows), F32)], axis=0)


class Line:
    def __init__(self, block, whole, send_sem, recv_sem, at, c, parts):
        self.block, self.whole, self.at, self.c = block, whole, at, c
        self.send_sem, self.recv_sem, self.parts = send_sem, recv_sem, parts

    def can(self, index):
        return (index >= 0) & (index < self.c)

    def rows(self, ref, part):
        size = self.block.shape[1] // self.parts
        return ref.at[:, pl.ds(part * size, size), :]

    def copy(self, way, stage, part):
        held, target = self.at - way * stage, self.at + way
        dst = self.rows(self.whole.at[held], part)
        return self.can(held) & self.can(target), send(
            dst if stage else self.rows(self.block, part),
            dst,
            self.send_sem.at[(way + 1) // 2, stage, part],
            self.recv_sem.at[held, part],
            {"dp": target},
        )

    def each(self, stages):
        for stage in stages:
            for part in range(self.parts):
                for way in (-1, 1):
                    yield self.copy(way, stage, part)

    def start(self, part):
        for way in (-1, 1):
            allowed, copy = self.copy(way, 0, part)
            pl.when(allowed)(copy.start)

    def hand_on(self, *stages):
        for allowed, copy in self.each([s for s in stages if s < self.c - 1]):

            @pl.when(allowed)
            def _():
                copy.wait_recv()
                copy.start()

    def wait(self, block):
        done = ((block < self.at) & self.can(self.at + 1)) | (
            (block > self.at) & self.can(self.at - 1)
        )

        @pl.when(jnp.logical_not(done))
        def _():
            for part in range(self.parts):
                src = self.rows(self.whole.at[block], part)
                recv = self.recv_sem.at[block, part]
                send(src, src, self.send_sem.at[0, 0, 0], recv, {"dp": block}).wait_recv()

    def finish(self):
        for allowed, copy in self.each(range(self.c - 1)):
            pl.when(allowed)(copy.wait_send)


class Gather:
    def __init__(self, own, place, halves, send_sem, recv_sem, me, n):
        self.own, self.place, self.halves = own, place, halves
        self.send_sem, self.recv_sem, self.me, self.n = send_sem, recv_sem, me, n
        self.direct = [k for k in order_of(n) if k % 2 == 0]
        self.relayed = n == 8
        self.near = [2, 4] if self.relayed else self.direct

    def to(self, src, dst, at, k):
        return send(
            src, dst, self.send_sem.at[at], self.recv_sem.at[at], {"ep": partner(self.me, k, self.n)}
        )

    def across(self, k):
        return self.to(self.own, self.place(self.me), k, k)

    def relay(self, k):
        half = self.halves(partner(self.me, k, self.n))[k // 4]
        return self.to(half, half, self.n + k // 4, 6 - k)

    def pass_on(self, k):
        block = self.place(partner(self.me, k, self.n))
        return self.to(block, block, k + 1, 1)

    def start(self):
        for k in self.near + [1]:
            self.across(k).start()

    def middle(self):
        for k in self.near:
            self.across(k).wait_recv()
            if self.relayed:
                self.relay(k).start()
            self.pass_on(k).start()

    def last(self):
        if self.relayed:
            for k in (2, 4):
                self.relay(k).wait_recv()
            self.pass_on(6).start()

    def finish(self):
        self.across(1).wait()
        for k in self.near:
            self.across(k).wait_send()
            if self.relayed:
                self.relay(k).wait_send()
        for k in self.direct:
            self.pass_on(k).wait()


def owners_of(c):
    return (c // 2 - 1, c // 2) if c <= 4 else tuple(range(c))


class Spread:
    def __init__(self, r, name, me, grp, n, c, place, halves, source):
        self.recv_buf, self.final, self.ss, self.rs, ys, yr, self.local = (
            getattr(r, name + part) for part in ("_recv", "_fin", "_ss", "_rs", "_ys", "_yr", "_ls")
        )
        self.source = source
        self.me, self.grp, self.c, self.place = me, grp, c, place
        self.owners = owners_of(c)
        self.gather = Gather(
            place(me, None), lambda e: place(e, None), halves, ys, yr, me, n
        )

    def to_owner(self, half):
        return send(
            self.source(half),
            self.recv_buf.at[self.grp],
            self.ss.at[0, half],
            self.rs.at[0, self.grp],
            {"dp": self.owners[half]},
        )

    def from_source(self, source):
        return send(
            self.source(0),
            self.recv_buf.at[source],
            self.ss.at[0, 0],
            self.rs.at[0, source],
            {"dp": source},
        )

    def to_copies(self, half, target):
        return send(
            self.final,
            self.place(self.me, half),
            self.ss.at[1, target],
            self.rs.at[1, half],
            {"dp": target},
        )

    def mine(self, half):
        return pltpu.make_async_copy(self.final, self.place(self.me, half), self.local.at[0])

    def scatter(self):
        for half, owner in enumerate(self.owners):
            pl.when(self.grp != owner)(self.to_owner(half).start)

            @pl.when(self.grp == owner)
            def _():
                self.recv_buf[owner] = self.source(half)[...]

    def total(self):
        for half, owner in enumerate(self.owners):

            @pl.when(self.grp == owner)
            def _():
                for s in range(self.c):
                    if s != owner:
                        self.from_source(s).wait_recv()
                total = self.recv_buf[0].astype(F32)
                for s in range(1, self.c):
                    total = total + self.recv_buf[s].astype(F32)
                self.final[...] = total.astype(BF)
                for s in range(self.c):
                    if s != owner:
                        self.to_copies(half, s).start()
                self.mine(half).start()

    def over(self):
        for half, owner in enumerate(self.owners):
            pl.when(self.grp != owner)(self.to_copies(half, owner).wait_recv)
            pl.when(self.grp == owner)(self.mine(half).wait)
        self.gather.start()

    def finish(self):
        self.gather.finish()
        for half, owner in enumerate(self.owners):
            pl.when(self.grp != owner)(self.to_owner(half).wait_send)

            @pl.when(self.grp == owner)
            def _():
                for s in range(self.c):
                    if s != owner:
                        self.to_copies(half, s).wait_send()


def block_kernel(r, n, c):
    me, grp = lax.axis_index("ep"), lax.axis_index("dp")
    rows, width = r.tokens.shape
    own, cap = width // n, 2 * rows // n
    slots = n * cap
    hidden = r.w_in.shape[1]
    part = hidden // c
    order = order_of(n)
    direct = [k for k in order if k % 2 == 0]
    partners = {k: partner(me, k, n) for k in range(n)}
    half = width // 2
    listed = [0, 1, 6, 7, 2, 3, 4, 5] if n == 8 else list(range(n))
    spot = {k: at for at, k in enumerate(listed)}

    def to_partner(src, dst, send_sem, recv_sem, k):
        return send(src, dst, send_sem, recv_sem, {"ep": partners[k]})

    def blocks_out(buf, dst, sems, k):
        return to_partner(buf.at[partners[k]], dst.at[me], sems[0].at[k], sems[1].at[k], k)

    def to_expert(buf, dst, sems, k):
        return to_partner(buf.at[partners[k]], dst.at[spot[k]], sems[0].at[k], sems[1].at[k], k)

    def from_expert(buf, dst, sems, k):
        return to_partner(buf.at[spot[k]], dst.at[me], sems[0].at[k], sems[1].at[k], k)

    barrier = pltpu.get_barrier_semaphore()
    for k in order:
        pl.semaphore_signal(barrier, inc=1, device_id={"ep": partners[k]}, device_id_type=MESH)
    for t in range(1, c):
        pl.semaphore_signal(
            barrier, inc=1, device_id={"dp": lax.rem(grp + t, c)}, device_id_type=MESH
        )

    def load_qkv(slot):
        cols = pl.ds(0, 3 * width)
        return [
            pltpu.make_async_copy(
                r.w_qkv.at[pl.ds(0, half), :], r.act.at[:, cols], r.load_sem.at[slot]
            ),
            pltpu.make_async_copy(
                r.w_qkv.at[pl.ds(half, half), :], r.grad_pre.at[:, cols], r.load_sem.at[slot + 1]
            ),
        ]

    first_loads = load_qkv(0)
    load_o = pltpu.make_async_copy(r.w_o, r.w_o_v, r.load_sem.at[2])
    load_out = pltpu.make_async_copy(r.w_out.at[0], r.w_out_v, r.load_sem.at[3])
    load_in = pltpu.make_async_copy(r.w_in.at[0], r.w_in_v, r.load_sem.at[4])
    for load in first_loads + [load_o, load_out, load_in]:
        load.start()

    r.place[...] = place_matrix(r.ids[...], n, cap)
    for t in range(width // TILE):
        cols = slice(t * TILE, (t + 1) * TILE)
        r.g_send[:, :, cols] = (
            dot(r.place[...], r.cotangent[:, cols], NN).astype(BF).reshape(n, cap, TILE)
        )
    pl.semaphore_wait(barrier, n - 1 + c - 1)
    half_cap = cap // 2
    g_halves = [
        [
            to_partner(
                r.g_send.at[partners[k], pl.ds(h * half_cap, half_cap), :],
                r.g_own.at[spot[k], pl.ds(h * half_cap, half_cap), :],
                r.g_ss.at[h, k],
                r.g_rs.at[h, k],
                k,
            )
            for k in order
        ]
        for h in range(2)
    ]
    for copy in g_halves[0]:
        copy.start()
    r.g_own[0] = r.g_send[me]

    norm_apply(r.tokens, r.gain_attn, r.shift_attn, r.normed)

    def to_heads(p, k):
        return to_partner(
            r.qkv_send.at[p, partners[k]],
            r.qkv_heads.at[p, me],
            r.a_ss.at[p, k],
            r.a_rs.at[p, k],
            k,
        )

    for load in first_loads:
        load.wait()
    for p in range(3):
        for t in range(width // TILE):
            cols = slice(p * width + t * TILE, p * width + (t + 1) * TILE)
            block = dot(r.normed[:, :half], r.act[:, cols], NN)
            block = (block + dot(r.normed[:, half:], r.grad_pre[:, cols], NN)).astype(BF)
            for e in range(TILE // own):
                r.qkv_send[p, t * (TILE // own) + e] = block[:, e * own : (e + 1) * own]
        r.qkv_heads[p, me] = r.qkv_send[p, me]
    for copy in g_halves[1]:
        copy.start()

    g_line = Line(r.g_own, r.g_all, r.gz_ss, r.gz_rs, grp, c, 2)
    x_line = Line(r.x_own, r.x_all, r.xz_ss, r.xz_rs, grp, c, 1)
    for copy in g_halves[0]:
        copy.wait()
    g_line.start(0)
    for p in range(3):
        for k in order:
            to_heads(p, k).start()
    for copy in g_halves[1]:
        copy.wait()
    g_line.start(1)

    load_out.wait()
    for p in range(3):
        for k in order:
            to_heads(p, k).wait_recv()

    def normed_halves(e):
        return [
            r.normed_all.at[e, pl.ds(0, rows // 2), :],
            r.normed_all.at[e, pl.ds(rows // 2, rows // 2), :],
        ]

    normed_gather = Gather(
        r.normed, lambda e: r.normed_all.at[e], normed_halves, r.n_ss, r.n_rs, me, n
    )
    mine = pltpu.make_async_copy(r.normed, r.normed_all.at[me], r.load_sem.at[5])
    mine.start()
    normed_gather.start()

    for i in range(n):
        r.values_t[i] = r.qkv_heads[2, i].astype(F32).T.astype(BF)

    def home(t):
        target = lax.rem(me + t, n)
        return send(
            r.att_heads.at[target],
            r.att_recv.at[me],
            r.o_ss.at[t],
            r.o_rs.at[t],
            {"ep": target},
        )

    def block_step(t, _):
        at = lax.rem(me + t, n)
        if n > UNROLLED:
            attend_block_loop(r, at)
        else:
            lax.switch(at, [functools.partial(attend_block, r, i) for i in range(n)])

        @pl.when(t > 0)
        def _():
            home(t).start()

        pl.when(t == 2)(lambda: g_line.hand_on(1))
        return 0

    lax.fori_loop(0, n, block_step, 0)
    r.att_recv[me] = r.att_heads[me]

    for t in range(1, n):
        home(t).wait_recv()
    for e in range(n):
        r.attended[:, e * own : (e + 1) * own] = r.att_recv[e]

    load_o.wait()
    for t in range(width // TILE):
        cols = slice(t * TILE, (t + 1) * TILE)
        r.hidden[:, cols] = r.tokens[:, cols].astype(F32) + dot(
            r.attended[...], r.w_o_v[:, cols], NN
        )
    norm_apply(r.hidden, r.gain_ffn, r.shift_ffn, r.block_out)
    for t in range(width // TILE):
        cols = slice(t * TILE, (t + 1) * TILE)
        r.x_send[:, :, cols] = (
            dot(r.place[...], r.block_out[:, cols], NN).astype(BF).reshape(n, cap, TILE)
        )
    x_copies = {k: to_expert(r.x_send, r.x_own, (r.x_ss, r.x_rs), k) for k in listed[1:]}
    for copy in x_copies.values():
        copy.start()
    r.x_own[0] = r.x_send[me]

    def act_grad(cols):
        r.grad_pre[:, cols] = dot(flat(r.g_own[...]), r.w_out_v[cols, :], NT).astype(BF)

    tiles(hidden, act_grad)
    load_in.wait()
    normed_gather.middle()
    g_line.hand_on(2)

    some = n // 2
    r_copies = {k: from_expert(r.g_send, r.r_recv, (r.r_ss, r.r_rs), k) for k in listed[1:]}

    def expert_half(at):
        mine_rows = slice(at * slots // 2, (at + 1) * slots // 2)
        blocks = slice(at * some, (at + 1) * some)
        for k in listed[blocks]:
            if k:
                x_copies[k].wait()
        if at:
            x_line.start(0)

        def expert_step(cols):
            pre = dot(flat(r.x_own[blocks]), r.w_in_v[cols, :], NT)
            for q in range(slots // 2 // CHUNK):
                part_at = slice(q * CHUNK, (q + 1) * CHUNK)
                rows_at = slice(mine_rows.start + q * CHUNK, mine_rows.start + (q + 1) * CHUNK)
                act, slope = gelu_both(pre[part_at])
                r.act[rows_at, cols] = act.astype(BF)
                r.grad_pre[rows_at, cols] = (
                    r.grad_pre[rows_at, cols].astype(F32) * slope
                ).astype(BF)

        tiles(hidden, expert_step)

        def routed_grad(cols):
            r.g_send[blocks, :, cols] = (
                dot(r.grad_pre[mine_rows, :], r.w_in_v[:, cols], NN)
                .astype(BF)
                .reshape(some, cap, TILE)
            )

        tiles(width, routed_grad)
        for k in listed[blocks]:
            if k:
                r_copies[k].start()

    expert_half(0)
    r.r_recv[me] = r.g_send[0]

    expert_half(1)

    def produce(cols):
        r.x_send[:, :, cols] = (
            dot(r.act[...], r.w_out_v[:, cols], NN).astype(BF).reshape(n, cap, TILE)
        )

    tiles(width, produce)
    mine_at = pl.multiple_of(grp * part, part)

    def weight_terms(act_at, x_rows, g_rows, first):
        def one(out):
            from_act = pl.ds(pl.multiple_of(act_at + out.start, TILE), TILE)

            def two(cols):
                term_in = dot(r.grad_pre[:, from_act], x_rows(cols), TN)
                r.sum_in[out, cols] = term_in if first else r.sum_in[out, cols] + term_in
                term_out = dot(r.act[:, from_act], g_rows(cols), TN)
                r.sum_out[out, cols] = term_out if first else r.sum_out[out, cols] + term_out

            tiles(width, two)

        tiles(part, one)

    weight_terms(
        mine_at,
        lambda cols: flat(r.x_own[:, :, cols]),
        lambda cols: flat(r.g_own[:, :, cols]),
        True,
    )

    normed_gather.last()

    for copy in r_copies.values():
        copy.wait()

    g_line.hand_on(*range(3, c))

    for t in range(width // TILE):
        cols = slice(t * TILE, (t + 1) * TILE)
        r.grad_tokens[:, cols] = dot(r.place[...], flat(r.r_recv[:, :, cols]), TN)

    def store_hidden(at, grad_in):
        grad_hidden = r.cotangent[at, :].astype(F32) + grad_in
        r.grad_tokens[at, :] = grad_hidden
        r.block_out[at, :] = grad_hidden.astype(BF)

    sums = norm_back(r.hidden, r.grad_tokens, r.gain_ffn, store_hidden)
    r.small_own[2:3], r.small_own[3:4] = sums
    r.small_own[4:SMALL] = jnp.zeros((SMALL - 4, width), F32)
    for t in range(width // TILE):
        block = dot(r.block_out[...], r.w_o_v[t * TILE : (t + 1) * TILE, :], NT).astype(BF)
        for e in range(TILE // own):
            r.att_recv[t * (TILE // own) + e] = block[:, e * own : (e + 1) * own]
    a_copies = [blocks_out(r.att_recv, r.grad_att, (r.b_ss, r.b_rs), k) for k in order]
    for copy in a_copies:
        copy.start()
    r.grad_att[me] = r.att_recv[me]

    def wo_rows(buf, e):
        at = e * own
        return buf.at[
            pl.ds(pl.multiple_of(lax.rem(at, slots), own), own),
            pl.ds(pl.multiple_of(lax.div(at, slots) * width, width), width),
        ]

    for t in range(width // slots):
        out = slice(t * slots, (t + 1) * slots)
        r.act[:, t * width : (t + 1) * width] = dot(
            r.attended[:, out], r.block_out[...], TN
        ).astype(BF)

    def to_sibling(k):
        at = partners[k]
        return to_partner(
            wo_rows(r.act, at), wo_rows(r.grad_pre, at), r.w_ss.at[k], r.w_rs.at[k], 1
        )

    def to_owner(k):
        return to_partner(
            wo_rows(r.act, partners[k]),
            wo_rows(r.grad_pre, partners[1]),
            r.w_ss.at[k],
            r.w_rs.at[k],
            k,
        )

    for copy in a_copies:
        copy.wait()

    for k in range(1, n, 2):
        to_sibling(k).start()

    def wo_across():
        for k in range(1, n, 2):
            to_sibling(k).wait()
        for k in [0] + direct:
            mine_k = wo_rows(r.act, partners[k])
            mine_k[...] = (
                mine_k[...].astype(F32) + wo_rows(r.grad_pre, partners[k])[...].astype(F32)
            ).astype(BF)
        for k in direct:
            to_owner(k).start()

    for p in range(3):
        for k in order:
            to_heads(p, k).wait_send()
    for t in range(1, n):
        home(t).wait_send()
    for i in range(n):
        both = (r.grad_att[i].astype(F32) * r.att_heads[i].astype(F32)).T
        size = own // r.heads
        deltas = [
            jnp.sum(both[h * size : (h + 1) * size], axis=0, keepdims=True) for h in range(r.heads)
        ]
        r.delta[i] = jnp.concatenate(
            deltas + [jnp.zeros((SMALL - r.heads, rows), F32)], axis=0
        )
    r.grad_q_t[...] = jnp.zeros(r.grad_q_t.shape, F32)

    def back_home(p, t):
        target = lax.rem(me + t, n)
        return send(
            r.qkv_send.at[p, target],
            r.grad_tok.at[p, me],
            r.d_ss.at[p, t],
            r.d_rs.at[p, t],
            {"ep": target},
        )

    def back_step(t, _):
        attend_back(r, lax.rem(me + t, n), n)
        pl.when(t == 0)(lambda: x_line.hand_on(1))
        pl.when(t == 1)(wo_across)

        @pl.when(t > 0)
        def _():
            for p in (1, 2):
                back_home(p, t).start()

        return 0

    lax.fori_loop(0, n, back_step, 0)
    for i in range(n):
        r.qkv_send[0, i] = (r.grad_q_t[i].T * ((own // r.heads) ** -0.5)).astype(BF)
    for t in range(1, n):
        back_home(0, t).start()
    for p in range(3):
        r.grad_tok[p, me] = r.qkv_send[p, me]
    p_copies = [from_expert(r.x_send, r.r_recv, (r.p_ss, r.p_rs), k) for k in order]
    for copy in p_copies:
        copy.start()
    r.r_recv[me] = r.x_send[0]

    def o_place(e, d):
        at = pl.ds(pl.multiple_of(e * own, own), own)
        piece = width // len(owners_of(c))
        if d is None:
            return r.o_all.at[at, :]
        return r.o_all.at[at, pl.ds(pl.multiple_of(d * piece, piece), piece)]

    def o_halves(e):
        at = pl.ds(pl.multiple_of(e * own, own), own)
        return [r.o_all.at[at, pl.ds(0, half)], r.o_all.at[at, pl.ds(half, half)]]

    def q_place(first, e, d):
        piece = TILE // len(owners_of(c))
        if d is None:
            return r.q_all.at[:, e, pl.ds(first, TILE), :]
        return r.q_all.at[:, e, pl.ds(pl.multiple_of(first + d * piece, piece), piece), :]

    def q_halves(first, e):
        return [
            r.q_all.at[:, e, pl.ds(first, TILE // 2), :],
            r.q_all.at[:, e, pl.ds(first + TILE // 2, TILE // 2), :],
        ]

    o_spread = Spread(
        r, "wo", me, grp, n, c, o_place, o_halves, lambda half: r.wo_send.at[half]
    )

    def q_source(t, half):
        if r.lent:
            return (r.grad_att, r.att_heads)[t].at[pl.ds(3 * half, 3)]
        return getattr(r, "wq" + str(t) + "_send").at[half]

    q_spreads = [
        Spread(
            r,
            "wq" + str(t),
            me,
            grp,
            n,
            c,
            functools.partial(q_place, t * TILE),
            functools.partial(q_halves, t * TILE),
            functools.partial(q_source, t),
        )
        for t in range(width // TILE)
    ]

    normed_gather.finish()
    mine.wait()
    at_once = width // rows
    turns = n // at_once

    def normed_loads(t):
        out = []
        for b in range(turns):
            spot = (t if turns <= 2 else b // 2) * TILE
            for s in range(at_once):
                out.append(
                    pltpu.make_async_copy(
                        r.normed_all.at[b * at_once + s, :, pl.ds(t * TILE, TILE)],
                        r.space.at[
                            pl.ds((b % 2) * width + s * rows, rows), pl.ds(spot, TILE)
                        ],
                        r.slab_sem.at[t % 2, b * at_once + s],
                    )
                )
        return out

    for t in range(width // TILE if turns <= 2 else 1):
        for load in normed_loads(t):
            load.start()
    for t, spread in enumerate(q_spreads):
        if turns > 2 and t:
            for load in normed_loads(t):
                load.start()
        for load in normed_loads(t):
            load.wait()
        total = None
        for b in range(turns):
            spot = (t if turns <= 2 else b // 2) * TILE
            grads = jnp.concatenate(
                [flat(r.qkv_send[p, b * at_once : (b + 1) * at_once]) for p in range(3)], axis=1
            )
            term = dot(
                r.space[(b % 2) * width : (b % 2 + 1) * width, spot : spot + TILE], grads, TN
            )
            total = term if b == 0 else total + term
        low = total.astype(BF)
        piece = TILE // len(owners_of(c))
        for d in range(len(owners_of(c))):
            for p in range(3):
                spread.source(d)[p] = low[
                    d * piece : (d + 1) * piece, p * own : (p + 1) * own
                ]
        if t == 0:
            spread.scatter()

    for k in direct:
        to_owner(k).wait()
    total = wo_rows(r.act, me)[...].astype(F32)
    for k in direct:
        total = total + wo_rows(r.grad_pre, partners[k + 1])[...].astype(F32)
    pieces = len(owners_of(c))
    for d in range(pieces):
        cols = slice(d * width // pieces, (d + 1) * width // pieces)
        r.wo_send[d] = total[:, cols].astype(BF)
    o_spread.scatter()


    def slab_loads(q):
        at = partner(grp, q, c)
        base = (q % 2) * width
        out = []
        for which, src in enumerate((r.x_all, r.g_all)):
            for s in range(n):
                out.append(
                    pltpu.make_async_copy(
                        src.at[at, s],
                        r.space.at[pl.ds(base + which * slots + s * cap, cap), :],
                        r.slab_sem.at[q % 2, which * n + s],
                    )
                )
        return out

    def slab_start(q):
        g_line.wait(partner(grp, q, c))
        x_line.wait(partner(grp, q, c))
        for load in slab_loads(q):
            load.start()

    def slab(q, beside=lambda: None):
        base = (q % 2) * width
        for load in slab_loads(q):
            load.wait()
        x_rows, g_rows = r.space.at[pl.ds(base, slots), :], r.space.at[pl.ds(base + slots, slots), :]

        def activate(out):
            at = pl.ds(pl.multiple_of(mine_at + out.start, TILE), TILE)
            cols = pl.ds(pl.multiple_of(3 * width + out.start, TILE), TILE)
            r.grad_pre[:, cols] = dot(g_rows[...], r.w_out_v[at, :], NT).astype(BF)
            pre = dot(x_rows[...], r.w_in_v[at, :], NT)
            for q in range(slots // CHUNK):
                some = slice(q * CHUNK, (q + 1) * CHUNK)
                act, slope = gelu_both(pre[some])
                r.act[some, cols] = act.astype(BF)
                r.grad_pre[some, cols] = (r.grad_pre[some, cols].astype(F32) * slope).astype(BF)

        tiles(part, activate)
        beside()
        weight_terms(
            3 * width, lambda cols: x_rows[:, cols], lambda cols: g_rows[:, cols], False
        )

    slab_start(1)

    def first_total():
        q_spreads[0].total()
        for spread in q_spreads[1:]:
            spread.scatter()

    slab(1, first_total)

    o_spread.total()
    last_loads = load_qkv(0)
    for load in last_loads:
        load.start()

    for p in (1, 2, 0):
        for t in range(1, n):
            back_home(p, t).wait_recv()
    for load in last_loads:
        load.wait()

    for copy in p_copies:
        copy.wait()
    for t in range(width // TILE):
        cols = slice(t * TILE, (t + 1) * TILE)
        r.block_out[:, cols] = (
            r.hidden[:, cols] + dot(r.place[...], flat(r.r_recv[:, :, cols]), TN)
        ).astype(BF)

    for p in range(3):
        for e in range(n):
            r.attended[:, e * own : (e + 1) * own] = r.grad_tok[p, e]
        cols = slice(p * width, (p + 1) * width)
        for at, weight in enumerate((r.act, r.grad_pre)):
            out = slice(at * half, (at + 1) * half)
            term = dot(r.attended[...], weight[:, cols], NT)
            r.hidden[:, out] = term if p == 0 else r.hidden[:, out] + term

    def store_tokens(at, grad_in):
        r.grad_tokens[at, :] += grad_in

    sums = norm_back(r.tokens, r.hidden, r.gain_attn, store_tokens)
    r.small_own[0:1], r.small_own[1:2] = sums

    def small_ep(k):
        return to_partner(r.small_own, r.small_ep.at[me], r.s_ss.at[0, k], r.s_rs.at[0, k], k)

    def small_dp(t):
        return send(
            r.small_sum,
            r.small_dp.at[grp],
            r.s_ss.at[1, t],
            r.s_rs.at[1, t],
            {"dp": lax.rem(grp + t, c)},
        )

    for k in order:
        small_ep(k).start()
    r.small_ep[me] = r.small_own[...]

    q_spreads[0].over()

    for spread in q_spreads[1:]:
        spread.total()
    x_line.hand_on(*range(2, c))

    if c > 3:
        slab_start(2)
        slab(2, q_spreads[0].gather.middle)
    else:
        q_spreads[0].gather.middle()

    for spread in [o_spread] + q_spreads[1:]:
        spread.over()

    for q in range(3, c - 1):
        slab_start(q)
        slab(q)
    out_copies = []
    for at, (src, dst) in enumerate(((r.sum_in, r.grad_in), (r.sum_out, r.grad_out))):
        base = at * width
        for s in range(0, part, CHUNK * 4):
            r.space[base + s : base + s + CHUNK * 4, :] = src[s : s + CHUNK * 4, :].astype(BF)
        out_copies.append(
            pltpu.make_async_copy(
                r.space.at[pl.ds(base, part), :], dst, r.load_sem.at[at]
            )
        )
    for copy in out_copies:
        copy.start()

    for k in order:
        small_ep(k).wait()
    total = r.small_ep[0]
    for e in range(1, n):
        total = total + r.small_ep[e]
    r.small_sum[...] = total
    for t in range(1, c):
        small_dp(t).start()
    r.small_dp[grp] = total

    spreads = q_spreads + [o_spread]
    q_spreads[0].gather.last()

    for spread in spreads[1:]:
        spread.gather.middle()

    for spread in spreads[1:]:
        spread.gather.last()

    for t in range(1, c):
        small_dp(t).wait()
    total = r.small_dp[0]
    for d in range(1, c):
        total = total + r.small_dp[d]
    r.small[...] = total
    last = partner(grp, c - 1, c)
    g_line.wait(last)
    x_line.wait(last)
    g_line.finish()
    x_line.finish()
    for copy in out_copies:
        copy.wait()
    for spread in spreads:
        spread.finish()
    for p in range(3):
        for t in range(1, n):
            back_home(p, t).wait_send()


def block_call(n, c, heads, operands):
    rows, width = operands["tokens"].shape
    hidden = operands["w_in"].shape[1]
    own, cap, part = width // n, 2 * rows // n, hidden // c
    slots, pieces = n * cap, len(owners_of(c))
    vm, hb = pl.BlockSpec(memory_space=pltpu.VMEM), pl.BlockSpec(memory_space=pl.ANY)
    sm = pl.BlockSpec(memory_space=pltpu.SMEM)
    inputs = dict(
        lengths=sm, ids=vm, tokens=vm, cotangent=vm, gain_attn=vm, shift_attn=vm, gain_ffn=vm,
        shift_ffn=vm, w_qkv=hb, w_o=hb, w_in=hb, w_out=hb,
    )
    outputs = dict(
        block_out=((rows, width), BF, vm),
        grad_tokens=((rows, width), F32, vm),
        q_all=((3, n, width, own), BF, hb),
        o_all=((width, width), BF, hb),
        small=((SMALL, width), F32, vm),
        grad_in=((part, width), BF, hb),
        grad_out=((part, width), BF, hb),
        g_all=((c, n, cap, width), BF, hb),
        x_all=((c, n, cap, width), BF, hb),
        normed_all=((n, rows, width), BF, hb),
    )

    def v(*shape):
        return pltpu.VMEM(shape, BF)

    def f(*shape):
        return pltpu.VMEM(shape, F32)

    def d(*shape):
        return pltpu.SemaphoreType.DMA(shape)

    heads_shape = (n, rows, own)
    scratch = dict(
        sum_in=f(part, width), sum_out=f(part, width),
        w_o_v=v(width, width), w_in_v=v(hidden, width), w_out_v=v(hidden, width),
        act=v(slots, hidden), grad_pre=v(slots, hidden), space=v(2 * width, width),
        normed=v(rows, width), place=v(slots, rows), hidden=f(rows, width),
        attended=v(rows, width),
        qkv_send=v(3, *heads_shape), qkv_heads=v(3, *heads_shape), grad_tok=v(3, *heads_shape),
        values_t=v(n, own, rows), att_heads=v(*heads_shape), att_recv=v(*heads_shape),
        grad_att=v(*heads_shape), grad_q_t=f(n, own, rows),
        lse=f(n, SMALL, rows), delta=f(n, SMALL, rows),
        g_send=v(n, cap, width), x_send=v(n, cap, width), g_own=v(n, cap, width),
        x_own=v(n, cap, width), r_recv=v(n, cap, width),
        wo_send=v(pieces, own, width // pieces), wo_recv=v(c, own, width // pieces),
        wo_fin=v(own, width // pieces),
        small_own=f(SMALL, width), small_ep=f(n, SMALL, width), small_sum=f(SMALL, width),
        small_dp=f(c, SMALL, width),
        load_sem=d(8), slab_sem=d(2, 2 * n),
        a_ss=d(3, n), a_rs=d(3, n), g_ss=d(2, n), g_rs=d(2, n), n_ss=d(n + 2), n_rs=d(n + 2),
        o_ss=d(n), o_rs=d(n), x_ss=d(n), x_rs=d(n), r_ss=d(n), r_rs=d(n), p_ss=d(n), p_rs=d(n),
        b_ss=d(n), b_rs=d(n), w_ss=d(n), w_rs=d(n), d_ss=d(3, n), d_rs=d(3, n),
        gz_ss=d(2, c, 2), gz_rs=d(c, 2), xz_ss=d(2, c, 1), xz_rs=d(c, 1),
        wo_ss=d(2, c), wo_rs=d(2, c), wo_ys=d(n + 2), wo_yr=d(n + 2), wo_ls=d(1),
        s_ss=d(2, max(n, c)), s_rs=d(2, max(n, c)),
    )
    for t in range(width // TILE):
        name = "wq" + str(t)
        piece = TILE // pieces
        lent = pieces == 2 and n >= 6 and piece == rows and width == 2 * TILE
        if not lent:
            scratch[name + "_send"] = v(pieces, 3, piece, own)
        scratch[name + "_recv"] = v(c, 3, piece, own)
        scratch[name + "_fin"] = v(3, piece, own)
        scratch[name + "_ss"] = scratch[name + "_rs"] = d(2, c)
        scratch[name + "_ys"] = scratch[name + "_yr"] = d(n + 2)
        scratch[name + "_ls"] = d(1)
    names = list(inputs) + list(outputs) + list(scratch)

    def kernel(*refs):
        r = types.SimpleNamespace(**dict(zip(names, refs)))
        r.heads, r.lent = heads, lent
        block_kernel(r, n, c)

    result = pl.pallas_call(
        kernel,
        out_shape=[jax.ShapeDtypeStruct(shape, kind) for shape, kind, _ in outputs.values()],
        in_specs=list(inputs.values()),
        out_specs=[spec for _, _, spec in outputs.values()],
        scratch_shapes=list(scratch.values()),
        compiler_params=pltpu.CompilerParams(
            collective_id=0, has_side_effects=True, vmem_limit_bytes=VMEM_LIMIT
        ),
    )(*[operands[name] for name in inputs])
    return dict(zip(outputs, result))


VMEM_LIMIT = 64 << 20
STEPS = 2


def widen_kernel(where, q_all, o_all, sum_in, sum_out, block, tokens, small, *rest):
    x_rows, g_rows, w_in, w_out, q_out, o_out, grad_in, grad_out, block_out, tokens_out = rest[:10]
    n, own = q_all.shape[1], q_all.shape[3]
    x_rows, g_rows = flat(x_rows[0]), flat(g_rows[0])
    pre = dot(x_rows, w_in[0], NT)
    grad_act = dot(g_rows, w_out[0], NT)
    acts, grads = [], []
    for q in range(x_rows.shape[0] // CHUNK):
        at = slice(q * CHUNK, (q + 1) * CHUNK)
        act, slope = gelu_both(pre[at])
        acts.append(act.astype(BF))
        grads.append((grad_act[at] * slope).astype(BF))
    grad_in[0] = sum_in[...].astype(F32) + dot(jnp.concatenate(grads, axis=0), x_rows, TN)
    grad_out[0] = sum_out[...].astype(F32) + dot(jnp.concatenate(acts, axis=0), g_rows, TN)
    for p in range(3):
        for e in range(n):
            at = (p * n + e) * own
            q_out[:, at : at + own] = q_all[p, e].astype(F32)
    o_out[...] = o_all[...].astype(F32)
    block_out[...] = block[...]
    tokens_out[...] = tokens[...]
    for at, one in enumerate(rest[10:]):
        one[...] = small[at : at + 1, :]


def widen(out, w_in, w_out):
    q_all, o_all, sum_in, block = out["q_all"], out["o_all"], out["grad_in"], out["block_out"]
    x_all = out["x_all"]
    c = x_all.shape[0]
    _, n, width, own = q_all.shape
    part, rows = sum_in.shape[0], block.shape[0]
    S = jax.ShapeDtypeStruct
    grp = lax.axis_index("dp")
    where = jnp.stack([partner(grp, c - 1, c), grp * STEPS]).astype(jnp.int32)

    def rowwise(count):
        return pl.BlockSpec((count // STEPS, width), lambda i, w: (i, 0))

    expert = pl.BlockSpec((1, part // STEPS, width), lambda i, w: (0, i, 0))
    weight = pl.BlockSpec((1, part // STEPS, width), lambda i, w: (0, w[1] + i, 0))
    group = pl.BlockSpec((1, *x_all.shape[1:]), lambda i, w: (w[0], 0, 0, 0))
    fixed = pl.BlockSpec((1, width), lambda i, w: (0, 0))
    return pl.pallas_call(
        widen_kernel,
        grid_spec=pltpu.PrefetchScalarGridSpec(
            num_scalar_prefetch=1,
            grid=(STEPS,),
            in_specs=[
                pl.BlockSpec((3, n, width // STEPS, own), lambda i, w: (0, 0, i, 0)),
                rowwise(width), rowwise(part), rowwise(part), rowwise(rows), rowwise(rows),
                pl.BlockSpec((SMALL, width), lambda i, w: (0, 0)), group, group, weight, weight,
            ],
            out_specs=[
                pl.BlockSpec((width // STEPS, 3 * width), lambda i, w: (i, 0)),
                rowwise(width), expert, expert, rowwise(rows), rowwise(rows),
            ] + [fixed] * 4,
        ),
        out_shape=[
            S((width, 3 * width), F32), S((width, width), F32), S((1, part, width), F32),
            S((1, part, width), F32), S((rows, width), BF), S((rows, width), F32),
        ] + [S((1, width), F32)] * 4,
        compiler_params=pltpu.CompilerParams(vmem_limit_bytes=VMEM_LIMIT),
    )(
        where, q_all, o_all, sum_in, out["grad_out"], block, out["grad_tokens"], out["small"],
        x_all, out["g_all"], w_in, w_out,
    )


def on_device(
    tokens,
    gain_attn,
    shift_attn,
    w_qkv,
    w_o,
    gain_ffn,
    shift_ffn,
    w_in,
    w_out,
    seq_lengths,
    expert_ids,
    cotangent,
):
    rows, width = tokens.shape
    n, c = lax.axis_size("ep"), lax.axis_size("dp")
    operands = dict(
        lengths=seq_lengths,
        ids=expert_ids.reshape(1, rows),
        tokens=tokens,
        cotangent=cotangent,
        gain_attn=gain_attn[None],
        shift_attn=shift_attn[None],
        gain_ffn=gain_ffn[None],
        shift_ffn=shift_ffn[None],
        w_qkv=w_qkv,
        w_o=w_o,
        w_in=w_in,
        w_out=w_out,
    )
    out = block_call(n, c, HEADS // n, operands)
    q_out, o_out, in_out, out_out, block, tokens_out, *small = widen(out, w_in, w_out)
    small = [one.reshape(width) for one in small]
    return (block, tokens_out, q_out, o_out, *small, in_out, out_out)


def solution(mesh):
    return jax.shard_map(
        on_device,
        mesh=mesh,
        in_specs=(
            P(("dp", "ep"), None),
            P(),
            P(),
            P(),
            P(),
            P(),
            P(),
            P("ep", None, None),
            P("ep", None, None),
            P("dp", None),
            P(("dp", "ep"), None),
            P(("dp", "ep"), None),
        ),
        out_specs=(
            P(("dp", "ep"), None),
            P(("dp", "ep"), None),
            P(),
            P(),
            P(),
            P(),
            P(),
            P(),
            P("ep", "dp", None),
            P("ep", "dp", None),
        ),
        check_vma=False,
    )
```
